32 devices in a mesh: grp: 2 (over y), ctx: 4 (over x, core), exp: 4 (over z).
Axes of the slice: x: 2, y: 2, z: 4, core: 2. Of those that a mesh axis runs over, the one named last changes fastest.
Arguments:
- queries: bfloat16 [8, 512, 4096], P(('grp', 'exp'), 'ctx'), parts along dimension 0, may hold values from -150 to 150
- keys: bfloat16 [8, 512, 256], P(('grp', 'exp'), 'ctx'), parts along dimension 0, may hold values from -5 to 5
- values: bfloat16 [8, 512, 256], P(('grp', 'exp'), 'ctx'), parts along dimension 0, may hold values from -6 to 6
- tree_parents: int32 [8, 4], P(('grp', 'exp')), parts along dimension 0, may hold values from 0 to 3, as said below
- routes: int32 [8, 512, 1], P(('grp', 'exp'), 'ctx'), parts along dimension 0, may hold values from 0 to 3; in each aligned block of 128 rows (0 to 127, 128 to 255, ..., all dimensions but the last counted through in order) at most 40 rows name the same one
- route_weight: float32 [8, 512, 1], P(('grp', 'exp'), 'ctx'), parts along dimension 0, may hold values from 0.3 to 1.5
- norm_gain: float32 [4096], replicated, may hold values from 0.5 to 1.5
- expert_in: bfloat16 [4, 4096, 2, 768], P('exp', 'ctx'), may hold values from -0.09375 to 0.09375
- expert_out: bfloat16 [4, 768, 4096], P('exp', None, 'ctx'), may hold values from -0.21875 to 0.21875
Outputs:
- layer_out: bfloat16 [8, 512, 4096], P(('grp', 'exp'), 'ctx'), parts along dimension 0
The draws below stay inside these ranges and needn't reach their ends.
There are 2 independent parts, one for each index of `grp`. The reference program is written for one: setup_inputs(seed, part) draws one part's arguments, and reference() takes and returns one part's arrays. A program takes and returns all parts, laid end to end along the dimension named above; an argument that names none is the same for every part. Nothing has to cross between parts.
Inputs may be any that keep to these rules, and one draw needn't show every extreme that they name: `routes`: in each aligned block of 128 rows (the rows of one device), no expert is named by more than 40 rows, a bound that some block reaches. `tree_parents`: the parent of block b is a block of the same sequence at or before b; a block that is its own parent begins a new tree. The last block of the first sequence begins a tree.
All inputs are finite; a program needn't handle non-finite values.
Results may differ from the reference program's by a relative error of at most 0.022.
Values may be sent and summed in bfloat16 or wider, within the bound.
No kernel may reach another device: no remote copies, remote signals or barrier semaphores. Data moves between devices by JAX's collectives and lax.ppermute only.
A program may use at most 64 MiB of HBM per device.

```python
import math
import jax
import jax.numpy as jnp
import numpy as np
from jax import lax

D = 4096
HEADS = 32
KV_HEADS = 2
HEAD_DIM = 128
FF = 768
TOP = 1
TREE_BLOCK = 128
TOK_DEV = 128
E_WIN = 4
CAP = 40
SEQS = 4
SEQ = 512
NB = 4
N_CTX = 4
N_EXP = 4


def shared_keys(key):
    return jnp.clip(jax.random.normal(key, (SEQS, SEQ, KV_HEADS * HEAD_DIM), jnp.float32), -5.0, 5.0)


def draw_keys(key, part):
    base_keys = shared_keys(key)
    return base_keys.astype(jnp.bfloat16)


def draw_queries(key, part):
    key = jax.random.fold_in(key, 7)
    first_key = jax.random.fold_in(key, 0)
    drawn = jnp.clip(jax.random.normal(first_key, (SEQS, SEQ, D), jnp.float32), -5.0, 5.0)
    return drawn.astype(jnp.bfloat16)


def draw_tree_parents(key, part):
    key = jax.random.fold_in(key, 11)
    raw_ids = jax.random.randint(key, (SEQS, NB), 0, 1 << 20)
    block_ids = jnp.arange(NB, dtype=jnp.int32)[None, :]
    parent_ids = raw_ids % (block_ids + 1)
    last_root = (block_ids == NB - 1) & (jnp.arange(SEQS, dtype=jnp.int32)[:, None] == 0)
    return jnp.where(last_root, NB - 1, parent_ids).astype(jnp.int32)


def levels(own_key, dims, pieces, least, largest):
    def one(dim, parts):
        steps = jax.random.uniform(jax.random.fold_in(jax.random.fold_in(own_key, 6), dim), (parts,), jnp.float32, least / len(pieces), largest / len(pieces))
        return jnp.repeat(jnp.exp(steps), dims[dim] // parts).reshape((-1,) + (1,) * (len(dims) - dim - 1))

    level = one(*pieces[0])
    for cut in pieces[1:]:
        level = level * one(*cut)
    return level


def assign_block(rng, own, number, rows, count, top, reach, lean):
    order = jax.random.permutation(rng, count)
    crowded, common = portions_of(count, rows * top, reach, lean, True), portions_of(count, rows * top, reach, lean, False)
    places = jnp.arange(count)

    def named(lengths, offset_by):
        used = int((lengths > 0).sum())
        fixed = max(1, used // 4)
        shifted = fixed + (places - fixed + offset_by * (used - fixed)) % max(1, count - fixed)
        return jnp.zeros((count,), jnp.int32).at[order[jnp.where(places < fixed, places, shifted)]].set(jnp.asarray(lengths, jnp.int32))

    lengths = jnp.where(number % 4 == 0, named(crowded, number // 4), named(common, number - number // 4 - 1))
    mixed = jax.random.permutation(jax.random.fold_in(own, 3), count)
    donor, receiver = mixed[0:count // 2 * 2:2], mixed[1:count // 2 * 2:2]
    slack = jnp.minimum(lengths[donor] - 1, reach - lengths[receiver]) // 2
    slack = jnp.where((donor == order[0]) | (receiver == order[0]) | (lengths[receiver] == 0), 0, jnp.maximum(slack, 0))
    shifted = jax.random.randint(jax.random.fold_in(own, 4), (count // 2,), 0, 1 << 20) % (slack + 1)
    lengths = lengths.at[donor].add(-shifted).at[receiver].add(shifted)
    labels = jnp.searchsorted(jnp.cumsum(lengths), jnp.arange(rows * top), side="right").astype(jnp.int32)
    listing = labels.reshape(top, rows).T
    listing = listing[jax.random.permutation(jax.random.fold_in(own, 1), rows)]
    offset_by = jax.random.randint(jax.random.fold_in(own, 2), (rows, 1), 0, top)
    return jnp.take_along_axis(listing, (jnp.arange(top)[None, :] + offset_by) % top, axis=1)


def portions_of(amount, total, most, skew, full):
    loads = [(1 << 20) // math.isqrt(standing ** skew) + 1 for standing in range(1, amount + 1)]
    largest = most if full else min(most, max(-(-total // amount), total * loads[0] // sum(loads)))
    least = 1 if total - largest >= amount - 1 else 0
    given, surplus = [largest] + [least] * (amount - 1), total - largest - least * (amount - 1)
    while surplus > 0:
        candidates = [i for i in range(1, amount) if given[i] < largest] or [i for i in range(1, amount) if given[i] < most]
        whole, remaining = sum([loads[i] for i in candidates]), surplus
        for i in candidates:
            addition = min(most - given[i], max(1, remaining * loads[i] // whole), surplus)
            given[i] = given[i] + addition
            surplus = surplus - addition
    return np.array(given)


def scatter_about(key, dims, spread, bound, pieces=(), held_as=jnp.bfloat16):
    gain = levels(key, dims, pieces, -0.22, 0.18) if pieces else 1.0
    entries = jax.random.normal(key, dims, jnp.float32) * spread * gain
    return jnp.minimum(jnp.maximum(entries, -bound), bound).astype(held_as)


def setup_inputs(seed: int = 0, part: int = 0) -> dict:
    key_list = jax.random.split(jax.random.key(seed), 10)
    part_keys = jax.random.split(jax.random.fold_in(key_list[9], part), 10)
    queries = draw_queries(jax.random.fold_in(jax.random.fold_in(key_list[9], part), 71), part)
    keys = draw_keys(jax.random.fold_in(jax.random.fold_in(key_list[9], part), 71), part)
    values = scatter_about(part_keys[2], (SEQS, SEQ, KV_HEADS * HEAD_DIM), 1.0, 6.0, ((0, 4), (1, 4)))
    tree_parents = draw_tree_parents(jax.random.fold_in(jax.random.fold_in(key_list[9], part), 71), part)
    routes_keys = jax.random.split(jax.random.fold_in(part_keys[4], 1), SEQS * SEQ // TOK_DEV)
    routes_turns = jax.random.permutation(jax.random.fold_in(part_keys[4], 3), SEQS * SEQ // TOK_DEV)
    routes = jax.vmap(lambda own, number: assign_block(jax.random.fold_in(part_keys[4], 2), own, number, TOK_DEV, E_WIN, TOP, CAP, 1))(routes_keys, routes_turns).reshape((SEQS, SEQ, TOP))
    route_weight = jnp.clip(jnp.exp(math.log(1.5) - 1.60943787 * jax.random.uniform(part_keys[5], (SEQS, SEQ, TOP), jnp.float32) ** levels(part_keys[5], (SEQS, SEQ, TOP), ((0, 4), (1, 4)), -0.2, 0.2)), 0.3, 1.5)
    norm_gain = jnp.clip(1.0 + 0.1 * jax.random.normal(key_list[6], (D,), jnp.float32), 0.5, 1.5)
    expert_in = scatter_about(key_list[7], (E_WIN, D, 2, FF), D ** -0.5, 0.09375, ((0, 4), (1, 4)))
    expert_out = scatter_about(key_list[8], (E_WIN, FF, D), FF ** -0.5, 0.21875, ((0, 4), (2, 4)))
    return dict(queries=queries, keys=keys, values=values, tree_parents=tree_parents, routes=routes, route_weight=route_weight, norm_gain=norm_gain, expert_in=expert_in, expert_out=expert_out)


def ancestor_table(parent_ids):
    blocks = parent_ids.shape[0]
    block_ids = jnp.arange(blocks, dtype=jnp.int32)

    def follow(turn_index, held_state):
        current, reach_table = held_state
        current_hot = current[:, None] == block_ids[None, :]
        following = lax.optimization_barrier(jnp.sum(jnp.where(current_hot, parent_ids[None, :], 0), axis=1)).astype(jnp.int32)
        reached = (following[:, None] == block_ids[None, :]).astype(jnp.float32)
        return (following, jnp.maximum(reach_table, reached))
    start_table = (block_ids[:, None] == block_ids[None, :]).astype(jnp.float32)
    return lax.fori_loop(0, blocks, follow, (block_ids, start_table))[1]

def attend_sequence(bundle):
    query_seq, key_seq, value_seq, parent_seq = bundle
    seq_length = query_seq.shape[0]
    blocks = parent_seq.shape[0]
    ancestry = ancestor_table(parent_seq)
    position = jnp.arange(seq_length, dtype=jnp.int32)
    block_of = position // TREE_BLOCK
    block_hot = (block_of[:, None] == jnp.arange(blocks, dtype=jnp.int32)[None, :]).astype(jnp.float32)
    related = jnp.dot(jnp.dot(block_hot, ancestry), block_hot.T) > 0.5
    causal = (block_of[:, None] != block_of[None, :]) | (position[None, :] <= position[:, None])
    allowed = related & causal
    per_group = HEADS // KV_HEADS
    query_heads = query_seq.astype(jnp.float32).reshape(seq_length, KV_HEADS, per_group, HEAD_DIM)
    key_heads = key_seq.astype(jnp.float32).reshape(seq_length, KV_HEADS, HEAD_DIM)
    value_heads = value_seq.astype(jnp.float32).reshape(seq_length, KV_HEADS, HEAD_DIM)
    score_scale = 1.0 / math.sqrt(HEAD_DIM)
    scores = jnp.einsum('tgjd,ngd->gjtn', query_heads, key_heads, precision=lax.Precision.HIGHEST) * score_scale
    masked = jnp.where(allowed[None, None], scores, -1e+30)
    row_peak = lax.optimization_barrier(jnp.max(masked, axis=-1, keepdims=True))
    exp_scores = jnp.where(allowed[None, None], jnp.exp(masked - row_peak), 0.0)
    numerator = jnp.einsum('gjtn,ngd->tgjd', exp_scores, value_heads, precision=lax.Precision.HIGHEST)
    denominator = jnp.transpose(lax.optimization_barrier(jnp.sum(exp_scores, axis=-1)), (2, 0, 1))[..., None]
    return (numerator / denominator).reshape(seq_length, D).astype(jnp.bfloat16)

def reference(queries, keys, values, tree_parents, routes, route_weight, norm_gain, expert_in, expert_out):
    attended = lax.map(attend_sequence, (queries, keys, values, tree_parents))
    flat_values = attended.reshape(-1, D).astype(jnp.float32)
    mean_square = lax.optimization_barrier(jnp.mean(flat_values * flat_values, axis=-1, keepdims=True))
    moe_in = (flat_values * lax.rsqrt(mean_square + 1e-06) * norm_gain).astype(jnp.bfloat16)
    picks = routes.reshape(-1).astype(jnp.int32)
    pick_rows = jnp.repeat(moe_in, TOP, axis=0)
    most_rows = N_EXP * N_CTX * CAP
    slice_width = D // N_CTX

    def one_expert(collected, expert):
        chosen_rows = jnp.nonzero(picks == expert, size=most_rows, fill_value=0)[0].astype(jnp.int32)
        live_rows = (jnp.arange(most_rows, dtype=jnp.int32) < jnp.sum((picks == expert).astype(jnp.int32))).astype(jnp.float32)
        row_block = pick_rows[chosen_rows].astype(jnp.float32).reshape(most_rows, N_CTX, slice_width)
        weights_in = lax.dynamic_index_in_dim(expert_in, expert, 0, keepdims=False).astype(jnp.float32).reshape(N_CTX, slice_width, 2 * FF)
        partial_value = jnp.einsum('rkc,kcf->krf', row_block, weights_in, precision=lax.Precision.HIGHEST)
        rounded = lax.optimization_barrier(partial_value.astype(jnp.bfloat16)).astype(jnp.float32)
        gate_up = lax.optimization_barrier(jnp.sum(rounded, axis=0))
        hidden = (jax.nn.silu(gate_up[:, :FF]) * gate_up[:, FF:]).astype(jnp.bfloat16)
        weights_out = lax.dynamic_index_in_dim(expert_out, expert, 0, keepdims=False)
        out_rows = jnp.dot(hidden, weights_out, preferred_element_type=jnp.float32).astype(jnp.bfloat16)
        out_rows = lax.optimization_barrier(out_rows).astype(jnp.float32)
        return (collected.at[chosen_rows].add(out_rows * live_rows[:, None]), None)
    start_rows = jnp.zeros((picks.shape[0], D), jnp.float32)
    gathered, unused = lax.scan(one_expert, start_rows, jnp.arange(E_WIN, dtype=jnp.int32))
    mixed = lax.optimization_barrier(jnp.sum(gathered.reshape(-1, TOP, D) * route_weight.reshape(-1, TOP, 1), axis=1))
    return (flat_values + mixed).astype(jnp.bfloat16).reshape(SEQS, SEQ, D)
```

```python
import functools
import math

import jax
import jax.numpy as jnp
from jax import lax
from jax.experimental import pallas as pl
from jax.experimental.pallas import tpu as pltpu
from jax.sharding import PartitionSpec as P

KV_HEADS = 2
HEAD_DIM = 128
TREE_BLOCK = 128
NEG = -1e30
VMEM_BYTES = 56 * 1024 * 1024


def params():
    return pltpu.CompilerParams(vmem_limit_bytes=VMEM_BYTES)


def placement_of(route_row, capacity, experts, first, relative):
    tokens = route_row.shape[1]
    if relative:
        route_row = lax.rem(route_row - first + experts, experts)
    rows = max(8, experts)
    expert_ids = lax.broadcasted_iota(jnp.int32, (rows, tokens), 0)
    hot = jnp.where(expert_ids == route_row, 1.0, 0.0)
    before = lax.broadcasted_iota(jnp.int32, (tokens, tokens), 0) < lax.broadcasted_iota(
        jnp.int32, (tokens, tokens), 1
    )
    earlier = jnp.dot(
        hot.astype(jnp.bfloat16),
        jnp.where(before, 1.0, 0.0).astype(jnp.bfloat16),
        preferred_element_type=jnp.float32,
    )
    rank = jnp.sum(earlier * hot, axis=0, keepdims=True).astype(jnp.int32)
    slot = route_row * capacity + rank
    slot_ids = lax.broadcasted_iota(jnp.int32, (experts * capacity, tokens), 0)
    return jnp.where(slot_ids == slot, 1.0, 0.0).astype(jnp.bfloat16)


def attention_kernel(
    n_ctx, experts, capacity, blocks_out, meta, parents, q_ref, route_ref, *refs
):
    kv = refs[: 2 * n_ctx]
    att_ref = refs[2 * n_ctx]
    out_refs = refs[2 * n_ctx + 1 : 2 * n_ctx + 1 + blocks_out]
    tokens = q_ref.shape[0]
    heads = q_ref.shape[1] // HEAD_DIM
    me = meta[1]
    reached = [jnp.int32(0)] * n_ctx
    current = me
    for _ in range(n_ctx):
        current = parents[current]
        for j in range(1, n_ctx):
            reached[j] = jnp.where(current == (me ^ j), jnp.int32(1), reached[j])
    causal = lax.broadcasted_iota(jnp.int32, (tokens, tokens), 1) <= lax.broadcasted_iota(
        jnp.int32, (tokens, tokens), 0
    )
    keys_t = jnp.concatenate([kv[2 * j][...] for j in range(n_ctx)], axis=0).T
    ones = jnp.ones((tokens, HEAD_DIM), jnp.bfloat16)
    values = jnp.concatenate(
        [jnp.concatenate([kv[2 * j + 1][...], ones], axis=1) for j in range(n_ctx)], axis=0
    )
    bias = jnp.concatenate(
        [jnp.where(causal, 0.0, NEG)]
        + [
            jnp.broadcast_to(jnp.where(reached[j] == 1, 0.0, NEG), (tokens, tokens))
            for j in range(1, n_ctx)
        ],
        axis=1,
    )
    scale = math.log2(math.e) / math.sqrt(HEAD_DIM)
    for h in range(heads):
        columns = slice(h * HEAD_DIM, (h + 1) * HEAD_DIM)
        scores = jnp.dot(q_ref[:, columns], keys_t, preferred_element_type=jnp.float32)
        scores = scores * scale + bias
        peak = jnp.max(scores, axis=1, keepdims=True)
        weights = jnp.exp2(scores - peak).astype(jnp.bfloat16)
        total = jnp.dot(weights, values, preferred_element_type=jnp.float32)
        att_ref[:, columns] = (total[:, :HEAD_DIM] / total[:, HEAD_DIM:]).astype(jnp.bfloat16)
    place = placement_of(route_ref[...], capacity, experts, meta[2], blocks_out > 1)
    packed = jnp.dot(place, att_ref[...], preferred_element_type=jnp.float32)
    rows = experts * capacity // blocks_out
    for k in range(blocks_out):
        out_refs[k][...] = packed[k * rows : (k + 1) * rows].astype(jnp.bfloat16)


def attention(meta, parents, queries, route_row, kvs, experts, capacity, blocks_out, half):
    n_ctx = len(kvs)
    tokens, width = queries.shape
    half_width = width // KV_HEADS
    rows = experts * capacity // blocks_out

    def pick(scalars):
        return scalars[0] if half == 0 else 1 - scalars[0]

    kv_specs, kv_args = [], []
    for kv in kvs:
        kv_specs.append(pl.BlockSpec((tokens, HEAD_DIM), lambda i, m, p: (0, pick(m))))
        kv_specs.append(pl.BlockSpec((tokens, HEAD_DIM), lambda i, m, p: (0, KV_HEADS + pick(m))))
        kv_args += [kv, kv]
    outs = pl.pallas_call(
        functools.partial(attention_kernel, n_ctx, experts, capacity, blocks_out),
        grid_spec=pltpu.PrefetchScalarGridSpec(
            num_scalar_prefetch=2,
            grid=(1,),
            in_specs=[
                pl.BlockSpec((tokens, half_width), lambda i, m, p: (0, pick(m))),
                pl.BlockSpec((1, tokens), lambda i, m, p: (0, 0)),
            ]
            + kv_specs,
            out_specs=[pl.BlockSpec((tokens, half_width), lambda i, m, p: (0, 0))]
            + [pl.BlockSpec((rows, half_width), lambda i, m, p: (0, 0))] * blocks_out,
        ),
        out_shape=[jax.ShapeDtypeStruct((tokens, half_width), jnp.bfloat16)]
        + [jax.ShapeDtypeStruct((rows, half_width), jnp.bfloat16)] * blocks_out,
        compiler_params=params(),
        name="attend_" + "ab"[half],
    )(meta, parents, queries, route_row, *kv_args)
    return outs[0], list(outs[1:])


def load_rows(row_refs, gain_ref, rows_scratch):
    rows = jnp.concatenate([r[...].astype(jnp.float32) for r in row_refs], axis=0)
    rows_scratch[...] = (rows * gain_ref[...]).astype(jnp.bfloat16)
    return jnp.sum(rows * rows, axis=1, keepdims=True)


def start_copies(sources, targets, sems):
    copies = [
        pltpu.make_async_copy(s, t, sems.at[i]) for i, (s, t) in enumerate(zip(sources, targets))
    ]
    for copy in copies:
        copy.start()
    return copies


def first_kernel(n_rows, n_in, offset_at, meta, gain_ref, *refs):
    row_refs, refs = refs[:n_rows], refs[n_rows:]
    w_refs, refs = refs[:n_in], refs[n_in:]
    sums_ref, squares_ref, rows_scratch, sems = refs[0], refs[1], refs[2], refs[3]
    w_scratch = refs[4:]
    copies = start_copies(w_refs, w_scratch, sems)
    squares = load_rows(row_refs, gain_ref, rows_scratch)
    squares_ref[...] = jnp.broadcast_to(squares, squares_ref.shape)
    for i in range(n_in):
        depth = w_refs[i].shape[0]
        offset = pl.multiple_of(meta[offset_at + i], 128)
        copies[i].wait()
        part = jnp.dot(
            rows_scratch[:, pl.ds(offset, depth)],
            w_scratch[i][...],
            preferred_element_type=jnp.float32,
        )
        sums_ref[...] = part if i == 0 else sums_ref[...] + part


def first_half(meta, gain, rows, weights, offset_at, slots):
    half_width = rows[0].shape[1]
    columns = weights[0].shape[1]
    return pl.pallas_call(
        functools.partial(first_kernel, len(rows), len(weights), offset_at),
        grid_spec=pltpu.PrefetchScalarGridSpec(
            num_scalar_prefetch=1,
            grid=(1,),
            in_specs=[pl.BlockSpec((1, half_width), lambda i, m: (0, m[0]))]
            + [pl.BlockSpec(r.shape, lambda i, m: (0, 0)) for r in rows]
            + [pl.BlockSpec(memory_space=pl.ANY)] * len(weights),
            out_specs=[
                pl.BlockSpec((slots, columns), lambda i, m: (0, 0)),
                pl.BlockSpec((slots, 128), lambda i, m: (0, 0)),
            ],
            scratch_shapes=[
                pltpu.VMEM((slots, half_width), jnp.bfloat16),
                pltpu.SemaphoreType.DMA((len(weights),)),
            ]
            + [pltpu.VMEM(w.shape, w.dtype) for w in weights],
        ),
        out_shape=[
            jax.ShapeDtypeStruct((slots, columns), jnp.float32),
            jax.ShapeDtypeStruct((slots, 128), jnp.float32),
        ],
        compiler_params=params(),
        name="gate_up_a",
    )(meta, gain, *rows, *weights)


def store_blocks(value, out_refs, offset, columns):
    rows = value.shape[0] // len(out_refs)
    for k, out in enumerate(out_refs):
        out[:, pl.ds(offset, columns)] = value[k * rows : (k + 1) * rows].astype(jnp.bfloat16)


def second_kernel(n_rows, n_in, n_out, blocks_out, in_at, out_at, meta, gain_ref, *refs):
    row_refs, refs = refs[:n_rows], refs[n_rows:]
    sums_ref, squares_ref, refs = refs[0], refs[1], refs[2:]
    w_refs, refs = refs[: n_in + n_out], refs[n_in + n_out :]
    hidden_ref, refs = refs[0], refs[1:]
    out_refs, refs = refs[:blocks_out], refs[blocks_out:]
    rows_scratch, sums_scratch, sems = refs[:3]
    w_scratch = refs[3:]
    copies = start_copies(w_refs, w_scratch, sems)
    squares = load_rows(row_refs, gain_ref, rows_scratch) + squares_ref[:, :1]
    sums_scratch[...] = sums_ref[...]
    for i in range(n_in):
        depth = w_refs[i].shape[0]
        offset = pl.multiple_of(meta[in_at + i], 128)
        copies[i].wait()
        sums_scratch[...] += jnp.dot(
            rows_scratch[:, pl.ds(offset, depth)],
            w_scratch[i][...],
            preferred_element_type=jnp.float32,
        )
    width = 2 * rows_scratch.shape[1]
    factor = lax.rsqrt(squares * (1.0 / width) + 1e-06)
    inner = hidden_ref.shape[1]
    gate = sums_scratch[:, :inner] * factor
    up = sums_scratch[:, inner:] * factor
    hidden = (gate / (1.0 + jnp.exp(-gate)) * up).astype(jnp.bfloat16)
    hidden_ref[...] = hidden
    for i in range(n_out):
        columns = w_refs[n_in + i].shape[1]
        offset = pl.multiple_of(meta[out_at + i], 128)
        copies[n_in + i].wait()
        value = jnp.dot(hidden, w_scratch[n_in + i][...], preferred_element_type=jnp.float32)
        store_blocks(value, out_refs, offset, columns)


def second_half(meta, gain, rows, sums, squares, w_in, w_out, in_at, out_at, blocks_out):
    half_width = rows[0].shape[1]
    slots, columns = sums.shape
    inner = columns // 2
    block_rows = slots // blocks_out
    weights = list(w_in) + list(w_out)
    outs = pl.pallas_call(
        functools.partial(
            second_kernel, len(rows), len(w_in), len(w_out), blocks_out, in_at, out_at
        ),
        grid_spec=pltpu.PrefetchScalarGridSpec(
            num_scalar_prefetch=1,
            grid=(1,),
            in_specs=[pl.BlockSpec((1, half_width), lambda i, m: (0, 1 - m[0]))]
            + [pl.BlockSpec(r.shape, lambda i, m: (0, 0)) for r in rows]
            + [pl.BlockSpec(sums.shape, lambda i, m: (0, 0))]
            + [pl.BlockSpec(squares.shape, lambda i, m: (0, 0))]
            + [pl.BlockSpec(memory_space=pl.ANY)] * len(weights),
            out_specs=[pl.BlockSpec((slots, inner), lambda i, m: (0, 0))]
            + [pl.BlockSpec((block_rows, half_width), lambda i, m: (0, 0))] * blocks_out,
            scratch_shapes=[
                pltpu.VMEM((slots, half_width), jnp.bfloat16),
                pltpu.VMEM(sums.shape, jnp.float32),
                pltpu.SemaphoreType.DMA((len(weights),)),
            ]
            + [pltpu.VMEM(w.shape, w.dtype) for w in weights],
        ),
        out_shape=[jax.ShapeDtypeStruct((slots, inner), jnp.bfloat16)]
        + [jax.ShapeDtypeStruct((block_rows, half_width), jnp.bfloat16)] * blocks_out,
        compiler_params=params(),
        name="gate_up_b_down_a",
    )(meta, gain, *rows, sums, squares, *weights)
    return outs[0], list(outs[1:])


def third_kernel(n_out, blocks_out, out_at, meta, hidden_ref, *refs):
    w_refs, refs = refs[:n_out], refs[n_out:]
    out_refs, refs = refs[:blocks_out], refs[blocks_out:]
    sems, w_scratch = refs[0], refs[1:]
    copies = start_copies(w_refs, w_scratch, sems)
    for i in range(n_out):
        columns = w_refs[i].shape[1]
        offset = pl.multiple_of(meta[out_at + i], 128)
        copies[i].wait()
        value = jnp.dot(hidden_ref[...], w_scratch[i][...], preferred_element_type=jnp.float32)
        store_blocks(value, out_refs, offset, columns)


def down_half(meta, hidden, weights, out_at, blocks_out, half_width):
    block_rows = hidden.shape[0] // blocks_out
    return pl.pallas_call(
        functools.partial(third_kernel, len(weights), blocks_out, out_at),
        grid_spec=pltpu.PrefetchScalarGridSpec(
            num_scalar_prefetch=1,
            grid=(1,),
            in_specs=[pl.BlockSpec(hidden.shape, lambda i, m: (0, 0))]
            + [pl.BlockSpec(memory_space=pl.ANY)] * len(weights),
            out_specs=[pl.BlockSpec((block_rows, half_width), lambda i, m: (0, 0))] * blocks_out,
            scratch_shapes=[pltpu.SemaphoreType.DMA((len(weights),))]
            + [pltpu.VMEM(w.shape, w.dtype) for w in weights],
        ),
        out_shape=[jax.ShapeDtypeStruct((block_rows, half_width), jnp.bfloat16)] * blocks_out,
        compiler_params=params(),
        name="down_b",
    )(meta, hidden, *weights)


def combine_kernel(experts, capacity, n_rows, meta, att_ref, route_ref, weight_ref, *refs):
    row_refs, out_ref = refs[:n_rows], refs[-1]
    tokens = att_ref.shape[0]
    place = placement_of(route_ref[...], capacity, experts, meta[2], n_rows > 1)
    rows = jnp.concatenate([r[...].astype(jnp.float32) for r in row_refs], axis=0)
    mine = lax.dot_general(
        place,
        rows.astype(jnp.bfloat16),
        (((0,), (0,)), ((), ())),
        preferred_element_type=jnp.float32,
    )
    diagonal = lax.broadcasted_iota(jnp.int32, (tokens, tokens), 0) == lax.broadcasted_iota(
        jnp.int32, (tokens, tokens), 1
    )
    weight = jnp.sum(jnp.where(diagonal, weight_ref[...], 0.0), axis=1, keepdims=True)
    out_ref[...] = (att_ref[...].astype(jnp.float32) + mine * weight).astype(jnp.bfloat16)


def combine(meta, att, route_row, weight_row, rows, experts, capacity, half, before):
    tokens, half_width = att.shape

    def pick(scalars):
        return scalars[0] if half == 0 else 1 - scalars[0]

    n_before = 0 if before is None else 1
    return pl.pallas_call(
        functools.partial(combine_kernel, experts, capacity, len(rows)),
        grid_spec=pltpu.PrefetchScalarGridSpec(
            num_scalar_prefetch=1,
            grid=(1,),
            in_specs=[
                pl.BlockSpec(att.shape, lambda i, m: (0, 0)),
                pl.BlockSpec(route_row.shape, lambda i, m: (0, 0)),
                pl.BlockSpec(weight_row.shape, lambda i, m: (0, 0)),
            ]
            + [pl.BlockSpec(r.shape, lambda i, m: (0, 0)) for r in rows]
            + [pl.BlockSpec(memory_space=pl.ANY)] * n_before,
            out_specs=pl.BlockSpec((tokens, half_width), lambda i, m: (0, pick(m))),
        ),
        out_shape=jax.ShapeDtypeStruct((tokens, KV_HEADS * half_width), jnp.bfloat16),
        input_output_aliases={4 + len(rows): 0} if n_before else {},
        compiler_params=params(),
        name="combine_" + "ab"[half],
    )(meta, att, route_row, weight_row, *rows, *([before] if n_before else []))


def swap(array, axis, size, bit):
    return lax.ppermute(array, axis, [(i, i ^ bit) for i in range(size)])


def body(
    queries, keys, values, tree_parents, routes, route_weight, norm_gain, expert_in, expert_out
):
    n_grp, n_ctx, n_exp = (lax.axis_size(name) for name in ("grp", "ctx", "exp"))
    grp, ctx, exp = (lax.axis_index(name) for name in ("grp", "ctx", "exp"))
    tokens, width = queries.shape[1:]
    assert tokens == TREE_BLOCK and tree_parents.shape[1] == n_ctx and routes.shape[2] == 1
    assert n_ctx & (n_ctx - 1) == 0 and n_ctx > 1
    capacity = max(2, 5 * tokens // (4 * n_exp))
    slots = n_exp * capacity
    shifted = n_exp <= 8 and capacity % 8 == 0
    blocks_out = n_exp if shifted else 1
    half_width = width // KV_HEADS
    top = n_ctx // 2
    low_bits = [1 << b for b in range(top.bit_length() - 1)]
    half = ctx // top

    depth = expert_in.shape[1]
    inner = expert_out.shape[1]
    columns = expert_out.shape[2]
    w_in = expert_in[0].reshape(depth, 2 * inner)
    w_out = expert_out[0]
    route_row = routes.reshape(1, tokens)
    weight_row = route_weight.reshape(1, tokens)
    gain = norm_gain.reshape(1, width)

    kv = jnp.concatenate([keys[0], values[0]], axis=1)
    near = [kv]
    far = [swap(kv, "ctx", n_ctx, top)]
    for bit in low_bits:
        near = near + [swap(x, "ctx", n_ctx, bit) for x in near]
        far = far + [swap(x, "ctx", n_ctx, bit) for x in far]
    kvs = near + far

    def spread(pieces):
        for bit in low_bits:
            pieces = pieces + [(swap(a, "ctx", n_ctx, bit), s ^ bit, o) for a, s, o in pieces]
        return pieces

    place = lax.rem(ctx, top)
    w_in_a = spread([(w_in, place, 0)])
    w_out_a = spread([(w_out, place, 0)])
    w_in_b, w_out_b = [], []
    parts = n_grp if n_grp == 2 else 1
    chunks = 2 if depth % 1024 == 0 else 1
    step = depth // (parts * chunks)
    for i in range(chunks):
        start = i * step
        mine = grp * (parts - 1) * (depth // 2) + start
        other = (1 - grp) * (parts - 1) * (depth // 2) + start
        piece = lax.dynamic_slice_in_dim(w_in, mine, step, 0)
        piece = swap(piece, "ctx", n_ctx, top)
        got = [(piece, place, mine)]
        if parts == 2:
            got.append((swap(piece, "grp", 2, 1), place, other))
        w_in_b += spread(got)
    step = columns // parts
    piece = lax.dynamic_slice_in_dim(w_out, grp * (parts - 1) * step, step, 1)
    piece = swap(piece, "ctx", n_ctx, top)
    got = [(piece, place, grp * (parts - 1) * step)]
    if parts == 2:
        got.append((swap(piece, "grp", 2, 1), place, (1 - grp) * step))
    w_out_b = spread(got)

    groups = (w_in_a, w_in_b, w_out_a, w_out_b)
    sizes = (depth, depth, columns, columns)
    scalars, starts = [half, ctx, exp], []
    for group, size in zip(groups, sizes):
        starts.append(len(scalars))
        scalars += [s * size + o for _, s, o in group]
    meta = jnp.stack([jnp.asarray(s, jnp.int32) for s in scalars])
    w_in_a, w_in_b, w_out_a, w_out_b = ([a for a, _, _ in group] for group in groups)

    def send(blocks, back):
        if not shifted:
            whole = blocks[0].reshape(n_exp, capacity, half_width)
            whole = lax.all_to_all(whole, "exp", 0, 0, tiled=True)
            return [whole.reshape(slots, half_width)]
        moved = [blocks[0]]
        for k in range(1, n_exp):
            shift = n_exp - k if back else k
            moved.append(
                lax.ppermute(blocks[k], "exp", [(i, (i + shift) % n_exp) for i in range(n_exp)])
            )
        return moved

    parents = tree_parents[0]
    att_a, packed_a = attention(
        meta, parents, queries[0], route_row, kvs, n_exp, capacity, blocks_out, 0
    )
    rows_a = send(packed_a, False)
    att_b, packed_b = attention(
        meta, parents, queries[0], route_row, kvs, n_exp, capacity, blocks_out, 1
    )
    rows_b = send(packed_b, False)
    sums, squares = first_half(meta, gain, rows_a, w_in_a, starts[0], slots)
    hidden, out_a = second_half(
        meta, gain, rows_b, sums, squares, w_in_b, w_out_a, starts[1], starts[2], blocks_out
    )
    back_a = send(out_a, True)
    out_b = down_half(meta, hidden, w_out_b, starts[3], blocks_out, half_width)
    back_b = send(out_b, True)
    done = combine(meta, att_a, route_row, weight_row, back_a, n_exp, capacity, 0, None)
    done = combine(meta, att_b, route_row, weight_row, back_b, n_exp, capacity, 1, done)
    return done[None]


def solution(mesh):
    in_specs = (
        P(("grp", "exp"), "ctx", None),
        P(("grp", "exp"), "ctx", None),
        P(("grp", "exp"), "ctx", None),
        P(("grp", "exp"), None),
        P(("grp", "exp"), "ctx", None),
        P(("grp", "exp"), "ctx", None),
        P(),
        P("exp", "ctx", None, None),
        P("exp", None, "ctx"),
    )
    out_specs = P(("grp", "exp"), "ctx", None)
    return jax.shard_map(body, mesh=mesh, in_specs=in_specs, out_specs=out_specs, check_vma=False)
```

```python
import functools
import math

import jax
import jax.numpy as jnp
from jax import lax
from jax.experimental import pallas as pl
from jax.experimental.pallas import tpu as pltpu
from jax.sharding import PartitionSpec as P

KV_HEADS = 2
HEAD_DIM = 128
TREE_BLOCK = 128
NEG = -1e30
MIB = 1024 * 1024
VMEM = pl.BlockSpec(memory_space=pltpu.VMEM)
SMEM = pl.BlockSpec(memory_space=pltpu.SMEM)


def call(kernel, name, args, specs, outs, scratch=(), mib=16, flops=1000):
    return pl.pallas_call(
        kernel,
        in_specs=specs,
        out_specs=[VMEM] * len(outs),
        out_shape=[jax.ShapeDtypeStruct(s, d) for s, d in outs],
        scratch_shapes=list(scratch),
        compiler_params=pltpu.CompilerParams(vmem_limit_bytes=mib * MIB),
        cost_estimate=pl.CostEstimate(flops=flops, bytes_accessed=1000, transcendentals=0),
        name=name,
    )(*args)


def placement_of(route_row, capacity, experts, first, relative):
    tokens = route_row.shape[1]
    if relative:
        route_row = lax.rem(route_row - first + experts, experts)
    rows = max(8, experts)
    expert_ids = lax.broadcasted_iota(jnp.int32, (rows, tokens), 0)
    hot = jnp.where(expert_ids == route_row, 1.0, 0.0)
    before = lax.broadcasted_iota(jnp.int32, (tokens, tokens), 0) < lax.broadcasted_iota(
        jnp.int32, (tokens, tokens), 1
    )
    earlier = jnp.dot(
        hot.astype(jnp.bfloat16),
        jnp.where(before, 1.0, 0.0).astype(jnp.bfloat16),
        preferred_element_type=jnp.float32,
    )
    rank = jnp.sum(earlier * hot, axis=0, keepdims=True).astype(jnp.int32)
    slot = route_row * capacity + rank
    slot_ids = lax.broadcasted_iota(jnp.int32, (experts * capacity, tokens), 0)
    return jnp.where(slot_ids == slot, 1.0, 0.0).astype(jnp.bfloat16)


def attention_kernel(n_ctx, experts, capacity, blocks_out, half, meta, parents, q_ref, route_ref, *refs):
    kv = refs[:n_ctx]
    att_ref = refs[n_ctx]
    out_refs = refs[n_ctx + 1 :]
    tokens, half_width = att_ref.shape
    heads = half_width // HEAD_DIM
    side = meta[0] if half == 0 else 1 - meta[0]
    me = meta[1]
    reached = [jnp.int32(0)] * n_ctx
    current = me
    for _ in range(n_ctx):
        current = parents[0, current]
        for j in range(1, n_ctx):
            reached[j] = jnp.where(current == (me ^ j), jnp.int32(1), reached[j])
    causal = lax.broadcasted_iota(jnp.int32, (tokens, tokens), 1) <= lax.broadcasted_iota(
        jnp.int32, (tokens, tokens), 0
    )
    key_at = pl.ds(pl.multiple_of(side * HEAD_DIM, HEAD_DIM), HEAD_DIM)
    value_at = pl.ds(pl.multiple_of((KV_HEADS + side) * HEAD_DIM, HEAD_DIM), HEAD_DIM)
    keys_t = jnp.concatenate([r[:, key_at] for r in kv], axis=0).T
    ones = jnp.ones((tokens, HEAD_DIM), jnp.bfloat16)
    values = jnp.concatenate(
        [jnp.concatenate([r[:, value_at], ones], axis=1) for r in kv], axis=0
    )
    bias = jnp.concatenate(
        [jnp.where(causal, 0.0, NEG)]
        + [
            jnp.broadcast_to(jnp.where(reached[j] == 1, 0.0, NEG), (tokens, tokens))
            for j in range(1, n_ctx)
        ],
        axis=1,
    )
    scale = math.log2(math.e) / math.sqrt(HEAD_DIM)
    for h in range(heads):
        columns = slice(h * HEAD_DIM, (h + 1) * HEAD_DIM)
        q_at = pl.ds(pl.multiple_of(side * half_width + h * HEAD_DIM, HEAD_DIM), HEAD_DIM)
        scores = jnp.dot(q_ref[:, q_at], keys_t, preferred_element_type=jnp.float32)
        scores = scores * scale + bias
        peak = jnp.max(scores, axis=1, keepdims=True)
        weights = jnp.exp2(scores - peak).astype(jnp.bfloat16)
        total = jnp.dot(weights, values, preferred_element_type=jnp.float32)
        att_ref[:, columns] = (total[:, :HEAD_DIM] / total[:, HEAD_DIM:]).astype(jnp.bfloat16)
    place = placement_of(route_ref[...], capacity, experts, meta[2], blocks_out > 1)
    packed = jnp.dot(place, att_ref[...], preferred_element_type=jnp.float32)
    rows = experts * capacity // blocks_out
    for k in range(blocks_out):
        out_refs[k][...] = packed[k * rows : (k + 1) * rows].astype(jnp.bfloat16)


def attention(meta, parents, queries, route_row, kvs, experts, capacity, blocks_out, half):
    tokens, width = queries.shape
    half_width = width // KV_HEADS
    rows = experts * capacity // blocks_out
    bf16 = jnp.bfloat16
    outs = call(
        functools.partial(attention_kernel, len(kvs), experts, capacity, blocks_out, half),
        "attend_" + "ab"[half],
        [meta, parents, queries, route_row, *kvs],
        [SMEM, SMEM] + [VMEM] * (2 + len(kvs)),
        [((tokens, half_width), bf16)] + [((rows, half_width), bf16)] * blocks_out,
        flops=2 * 10**9,
    )
    return outs[0], list(outs[1:])


def prepare_kernel(n_rows, half, meta, gain_ref, *refs):
    row_refs, (scaled_ref, squares_ref) = refs[:n_rows], refs[n_rows:]
    width = scaled_ref.shape[1]
    side = meta[0] if half == 0 else 1 - meta[0]
    gain = gain_ref[:, pl.ds(pl.multiple_of(side * width, width), width)]
    rows = jnp.concatenate([r[...].astype(jnp.float32) for r in row_refs], axis=0)
    scaled_ref[...] = (rows * gain).astype(jnp.bfloat16)
    squares = jnp.sum(rows * rows, axis=1, keepdims=True)
    squares_ref[...] = jnp.broadcast_to(squares, squares_ref.shape)


def prepare(meta, gain, rows, slots, half):
    return call(
        functools.partial(prepare_kernel, len(rows), half),
        "rows_" + "ab"[half],
        [meta, gain, *rows],
        [SMEM] + [VMEM] * (1 + len(rows)),
        [((slots, rows[0].shape[1]), jnp.bfloat16), ((slots, 128), jnp.float32)],
        flops=20 * 10**9,
    )


def add_products(meta, pieces, w_refs, rows_scratch, sums_ref, fresh):
    done = set()
    for (row_at, col_at), w_ref in zip(pieces, w_refs):
        depth, columns = w_ref.shape
        rows = rows_scratch[:, pl.ds(pl.multiple_of(meta[row_at], 128), depth)]
        part = jnp.dot(rows, w_ref[...], preferred_element_type=jnp.float32)
        where = pl.ds(pl.multiple_of(meta[col_at], 128), columns)
        if fresh and col_at not in done:
            sums_ref[:, where] = part
        else:
            sums_ref[:, where] += part
        done.add(col_at)


def first_kernel(pieces, meta, rows_ref, *refs):
    add_products(meta, pieces, refs[:-1], rows_ref, refs[-1], True)


def first_half(meta, rows, weights, pieces, inner):
    return call(
        functools.partial(first_kernel, pieces),
        "gate_up_a",
        [meta, rows, *weights],
        [SMEM] + [VMEM] * (1 + len(weights)),
        [((rows.shape[0], 2 * inner), jnp.float32)],
    )[0]


def store_down(meta, pieces, w_refs, hidden, out_refs):
    value, blocks = None, len(out_refs)
    for i, ((row_at, col_at), w_ref) in enumerate(zip(pieces, w_refs)):
        depth, columns = w_ref.shape
        rows = hidden[:, pl.ds(pl.multiple_of(meta[row_at], 128), depth)]
        part = jnp.dot(rows, w_ref[...], preferred_element_type=jnp.float32)
        value = part if value is None else value + part
        if i + 1 == len(pieces) or pieces[i + 1][1] != col_at:
            where = pl.ds(pl.multiple_of(meta[col_at], 128), columns)
            height = value.shape[0] // blocks
            for k, out in enumerate(out_refs):
                out[:, where] = value[k * height : (k + 1) * height].astype(jnp.bfloat16)
            value = None


def second_kernel(in_pieces, out_pieces, meta, rows_ref, start_ref, near_ref, far_ref, *refs):
    n_in, n_out = len(in_pieces), len(out_pieces)
    w_refs, refs = refs[: n_in + n_out], refs[n_in + n_out :]
    hidden_ref, out_refs, sums_ref = refs[0], refs[1:-1], refs[-1]
    sums_ref[...] = start_ref[...]
    add_products(meta, in_pieces, w_refs[:n_in], rows_ref, sums_ref, False)
    width = 2 * rows_ref.shape[1]
    squares = near_ref[:, :1] + far_ref[:, :1]
    factor = lax.rsqrt(squares * (1.0 / width) + 1e-06)
    inner = hidden_ref.shape[1]
    gate = sums_ref[:, :inner] * factor
    up = sums_ref[:, inner:] * factor
    hidden_ref[...] = (gate / (1.0 + jnp.exp(-gate)) * up).astype(jnp.bfloat16)
    store_down(meta, out_pieces, w_refs[n_in:], hidden_ref, out_refs)


def second_half(meta, rows, sums, near, far, w_in, in_pieces, w_out, out_pieces, blocks_out):
    slots, columns = sums.shape
    weights = list(w_in) + list(w_out)
    bf16 = jnp.bfloat16
    outs = call(
        functools.partial(second_kernel, in_pieces, out_pieces),
        "gate_up_b_down_a",
        [meta, rows, sums, near, far, *weights],
        [SMEM] + [VMEM] * (4 + len(weights)),
        [((slots, columns // 2), bf16)]
        + [((slots // blocks_out, rows.shape[1]), bf16)] * blocks_out,
        [pltpu.VMEM((slots, columns), jnp.float32)],
        flops=20 * 10**9,
    )
    return outs[0], list(outs[1:])


def third_kernel(pieces, meta, hidden_ref, *refs):
    store_down(meta, pieces, refs[: len(pieces)], hidden_ref, refs[len(pieces) :])


def down_half(meta, hidden, weights, pieces, blocks_out, half_width):
    outs = [((hidden.shape[0] // blocks_out, half_width), jnp.bfloat16)] * blocks_out
    return list(
        call(
            functools.partial(third_kernel, pieces),
            "down_b",
            [meta, hidden, *weights],
            [SMEM] + [VMEM] * (1 + len(weights)),
            outs,
        )
    )


def combine_kernel(experts, capacity, n_rows, last, meta, att_ref, route_ref, weight_ref, *refs):
    row_refs, out_ref = refs[:n_rows], refs[-1]
    tokens, half_width = att_ref.shape
    place = placement_of(route_ref[...], capacity, experts, meta[2], n_rows > 1)
    rows = jnp.concatenate([r[...].astype(jnp.float32) for r in row_refs], axis=0)
    mine = lax.dot_general(
        place,
        rows.astype(jnp.bfloat16),
        (((0,), (0,)), ((), ())),
        preferred_element_type=jnp.float32,
    )
    diagonal = lax.broadcasted_iota(jnp.int32, (tokens, tokens), 0) == lax.broadcasted_iota(
        jnp.int32, (tokens, tokens), 1
    )
    weight = jnp.sum(jnp.where(diagonal, weight_ref[...], 0.0), axis=1, keepdims=True)
    value = (att_ref[...].astype(jnp.float32) + mine * weight).astype(jnp.bfloat16)
    if last:
        before_ref = refs[n_rows]
        before_at = pl.multiple_of(meta[0] * half_width, half_width)
        mine_at = pl.multiple_of((1 - meta[0]) * half_width, half_width)
        out_ref[:, pl.ds(before_at, half_width)] = before_ref[...]
        out_ref[:, pl.ds(mine_at, half_width)] = value
    else:
        out_ref[...] = value


def combine(meta, att, route_row, weight_row, rows, experts, capacity, before):
    tokens, half_width = att.shape
    last = before is not None
    extra = [before] if last else []
    return call(
        functools.partial(combine_kernel, experts, capacity, len(rows), last),
        "combine_" + "ab"[last],
        [meta, att, route_row, weight_row, *rows, *extra],
        [SMEM] + [VMEM] * (3 + len(rows) + len(extra)),
        [((tokens, half_width * (1 + last)), jnp.bfloat16)],
        flops=20 * 10**9,
    )[0]


def swap(array, axis, size, bit):
    return lax.ppermute(array, axis, [(i, i ^ bit) for i in range(size)])


def after(array, *others):
    return lax.optimization_barrier((array, *others))[0]


def body(
    queries, keys, values, tree_parents, routes, route_weight, norm_gain, expert_in, expert_out
):
    n_grp, n_ctx, n_exp = (lax.axis_size(name) for name in ("grp", "ctx", "exp"))
    grp, ctx, exp = (lax.axis_index(name) for name in ("grp", "ctx", "exp"))
    tokens, width = queries.shape[1:]
    assert tokens == TREE_BLOCK and tree_parents.shape[1] == n_ctx and routes.shape[2] == 1
    assert n_ctx & (n_ctx - 1) == 0 and n_ctx > 1 and n_grp == 2
    capacity = max(2, 5 * tokens // (4 * n_exp))
    slots = n_exp * capacity
    shifted = n_exp <= 8 and capacity % 8 == 0
    blocks_out = n_exp if shifted else 1
    half_width = width // KV_HEADS
    top = n_ctx // 2
    low_bits = [1 << b for b in range(top.bit_length() - 1)]
    half = ctx // top

    depth = expert_in.shape[1]
    inner = expert_out.shape[1]
    columns = expert_out.shape[2]
    w_out = expert_out[0]
    route_row = routes.reshape(1, tokens)
    weight_row = route_weight.reshape(1, tokens)
    gain = norm_gain.reshape(1, width)

    kv = jnp.concatenate([keys[0], values[0]], axis=1)
    kv_far = swap(kv, "ctx", n_ctx, top)
    near, far = [kv], [kv_far]
    for bit in low_bits:
        near = near + [swap(x, "ctx", n_ctx, bit) for x in near]
        far = far + [swap(x, "ctx", n_ctx, bit) for x in far]
    kvs = near + far

    scalars = [half, ctx, exp, jnp.int32(0)]

    def note(value):
        scalars.append(jnp.asarray(value, jnp.int32))
        return len(scalars) - 1

    zero = 3
    shard = lax.rem(ctx, top)
    in_row = [note((shard ^ j) * depth) for j in range(top)]
    out_col = [note((shard ^ j) * columns) for j in range(top)]
    in_third, out_third = 2 * inner // 3, inner // 3
    in_cols = [note(grp * in_third), note((1 - grp) * in_third), note(2 * in_third)]
    out_rows = [note(grp * out_third), note((1 - grp) * out_third), note(2 * out_third)]
    meta = jnp.stack(scalars)

    def spread(array):
        found = [array]
        for bit in low_bits:
            found = found + [swap(a, "ctx", n_ctx, bit) for a in found]
        return found

    def send(blocks, back):
        if not shifted:
            whole = blocks[0].reshape(n_exp, capacity, half_width)
            whole = lax.all_to_all(whole, "exp", 0, 0, tiled=True)
            return [whole.reshape(slots, half_width)]
        moved = [blocks[0]]
        for k in range(1, n_exp):
            shift = n_exp - k if back else k
            moved.append(
                lax.ppermute(blocks[k], "exp", [(i, (i + shift) % n_exp) for i in range(n_exp)])
            )
        return moved

    w_in = expert_in[0].reshape(depth, 2 * inner)
    w_first = lax.dynamic_slice_in_dim(w_in, grp * in_third, in_third, 1)
    w_first = swap(after(w_first, kv_far), "ctx", n_ctx, top)
    w_direct = swap(after(w_in[:, 2 * in_third :], kv_far), "ctx", n_ctx, top)
    w_in_a = spread(after(w_in, kvs[-1]))

    att_a, packed_a = attention(
        meta,
        tree_parents,
        after(queries[0], w_in_a[-1]),
        route_row,
        kvs,
        n_exp,
        capacity,
        blocks_out,
        0,
    )
    rows_a = send(packed_a, False)
    att_b, packed_b = attention(
        meta,
        tree_parents,
        after(queries[0], att_a),
        route_row,
        kvs,
        n_exp,
        capacity,
        blocks_out,
        1,
    )
    rows_b = send([after(x, *rows_a) for x in packed_b], False)

    w_second = swap(after(w_first, *rows_a), "grp", 2, 1)
    scaled_a, squares_a = prepare(meta, gain, rows_a, slots, 0)
    sums = first_half(meta, scaled_a, w_in_a, [(r, zero) for r in in_row], inner)
    w_in_b = [spread(after(w_first, *rows_b))]
    w_out_a = spread(after(w_out, *rows_b))
    v_first = lax.dynamic_slice_in_dim(w_out, grp * out_third, out_third, 0)
    v_first = swap(after(v_first, *rows_b), "ctx", n_ctx, top)
    w_in_b.append(spread(after(w_direct, *rows_b)))
    w_in_b.append(spread(after(w_second, *rows_b)))
    w_in_b = list(zip(w_in_b[0], w_in_b[2], w_in_b[1]))
    scaled_b, squares_b = prepare(meta, gain, rows_b, slots, 1)

    in_pieces = [(r, c) for r in in_row for c in in_cols]
    hidden, out_a = second_half(
        meta,
        scaled_b,
        sums,
        squares_a,
        squares_b,
        [w for shard_pieces in w_in_b for w in shard_pieces],
        in_pieces,
        w_out_a,
        [(zero, c) for c in out_col],
        blocks_out,
    )
    back_a = send(out_a, True)
    v_direct = swap(after(w_out[2 * out_third :], hidden), "ctx", n_ctx, top)
    v_second = swap(after(v_first, hidden), "grp", 2, 1)
    w_out_b = list(zip(*[spread(after(v, *back_a)) for v in (v_first, v_second, v_direct)]))
    out_b = down_half(
        meta,
        after(hidden, *out_a),
        [w for shard_pieces in w_out_b for w in shard_pieces],
        [(r, c) for c in out_col for r in out_rows],
        blocks_out,
        half_width,
    )
    back_b = send(out_b, True)
    done = combine(meta, att_a, route_row, weight_row, back_a, n_exp, capacity, None)
    done = combine(meta, att_b, route_row, weight_row, back_b, n_exp, capacity, done)
    return done[None]


def solution(mesh):
    in_specs = (
        P(("grp", "exp"), "ctx", None),
        P(("grp", "exp"), "ctx", None),
        P(("grp", "exp"), "ctx", None),
        P(("grp", "exp"), None),
        P(("grp", "exp"), "ctx", None),
        P(("grp", "exp"), "ctx", None),
        P(),
        P("exp", "ctx", None, None),
        P("exp", None, "ctx"),
    )
    out_specs = P(("grp", "exp"), "ctx", None)
    return jax.shard_map(body, mesh=mesh, in_specs=in_specs, out_specs=out_specs, check_vma=False)
```

```python
import functools
import math

import jax
import jax.numpy as jnp
from jax import lax
from jax.experimental import pallas as pl
from jax.experimental.pallas import tpu as pltpu
from jax.sharding import PartitionSpec as P

KV_HEADS = 2
HEAD_DIM = 128
TREE_BLOCK = 128
NEG = -1e30
MIB = 1024 * 1024
VMEM = pl.BlockSpec(memory_space=pltpu.VMEM)
SMEM = pl.BlockSpec(memory_space=pltpu.SMEM)


def call(kernel, name, args, specs, outs, scratch=(), mib=16, flops=1000):
    return pl.pallas_call(
        kernel,
        in_specs=specs,
        out_specs=[VMEM] * len(outs),
        out_shape=[jax.ShapeDtypeStruct(s, d) for s, d in outs],
        scratch_shapes=list(scratch),
        compiler_params=pltpu.CompilerParams(vmem_limit_bytes=mib * MIB),
        cost_estimate=pl.CostEstimate(flops=flops, bytes_accessed=1000, transcendentals=0),
        name=name,
    )(*args)


def placement_of(route_row, capacity, experts, first, relative):
    tokens = route_row.shape[1]
    if relative:
        route_row = lax.rem(route_row - first + experts, experts)
    rows = max(8, experts)
    expert_ids = lax.broadcasted_iota(jnp.int32, (rows, tokens), 0)
    hot = jnp.where(expert_ids == route_row, 1.0, 0.0)
    before = lax.broadcasted_iota(jnp.int32, (tokens, tokens), 0) < lax.broadcasted_iota(
        jnp.int32, (tokens, tokens), 1
    )
    earlier = jnp.dot(
        hot.astype(jnp.bfloat16),
        jnp.where(before, 1.0, 0.0).astype(jnp.bfloat16),
        preferred_element_type=jnp.float32,
    )
    rank = jnp.sum(earlier * hot, axis=0, keepdims=True).astype(jnp.int32)
    slot = route_row * capacity + rank
    slot_ids = lax.broadcasted_iota(jnp.int32, (experts * capacity, tokens), 0)
    return jnp.where(slot_ids == slot, 1.0, 0.0).astype(jnp.bfloat16)


def attention_kernel(n_ctx, experts, capacity, blocks_out, half, meta, parents, q_ref, route_ref, *refs):
    kv = refs[:n_ctx]
    att_ref = refs[n_ctx]
    out_refs = refs[n_ctx + 1 :]
    tokens, half_width = att_ref.shape
    heads = half_width // HEAD_DIM
    side = meta[0] if half == 0 else 1 - meta[0]
    me = meta[1]
    reached = [jnp.int32(0)] * n_ctx
    current = me
    for _ in range(n_ctx):
        current = parents[0, current]
        for j in range(1, n_ctx):
            reached[j] = jnp.where(current == (me ^ j), jnp.int32(1), reached[j])
    causal = lax.broadcasted_iota(jnp.int32, (tokens, tokens), 1) <= lax.broadcasted_iota(
        jnp.int32, (tokens, tokens), 0
    )
    key_at = pl.ds(pl.multiple_of(side * HEAD_DIM, HEAD_DIM), HEAD_DIM)
    value_at = pl.ds(pl.multiple_of((KV_HEADS + side) * HEAD_DIM, HEAD_DIM), HEAD_DIM)
    keys_t = jnp.concatenate([r[:, key_at] for r in kv], axis=0).T
    ones = jnp.ones((tokens, HEAD_DIM), jnp.bfloat16)
    values = jnp.concatenate(
        [jnp.concatenate([r[:, value_at], ones], axis=1) for r in kv], axis=0
    )
    bias = jnp.concatenate(
        [jnp.where(causal, 0.0, NEG)]
        + [
            jnp.broadcast_to(jnp.where(reached[j] == 1, 0.0, NEG), (tokens, tokens))
            for j in range(1, n_ctx)
        ],
        axis=1,
    )
    scale = math.log2(math.e) / math.sqrt(HEAD_DIM)
    for h in range(heads):
        columns = slice(h * HEAD_DIM, (h + 1) * HEAD_DIM)
        q_at = pl.ds(pl.multiple_of(side * half_width + h * HEAD_DIM, HEAD_DIM), HEAD_DIM)
        scores = jnp.dot(q_ref[:, q_at], keys_t, preferred_element_type=jnp.float32)
        scores = scores * scale + bias
        peak = jnp.max(scores, axis=1, keepdims=True)
        weights = jnp.exp2(scores - peak).astype(jnp.bfloat16)
        total = jnp.dot(weights, values, preferred_element_type=jnp.float32)
        att_ref[:, columns] = (total[:, :HEAD_DIM] / total[:, HEAD_DIM:]).astype(jnp.bfloat16)
    place = placement_of(route_ref[...], capacity, experts, meta[2], blocks_out > 1)
    packed = jnp.dot(place, att_ref[...], preferred_element_type=jnp.float32)
    rows = experts * capacity // blocks_out
    for k in range(blocks_out):
        out_refs[k][...] = packed[k * rows : (k + 1) * rows].astype(jnp.bfloat16)


def attention(meta, parents, queries, route_row, kvs, experts, capacity, blocks_out, half):
    tokens, width = queries.shape
    half_width = width // KV_HEADS
    rows = experts * capacity // blocks_out
    bf16 = jnp.bfloat16
    outs = call(
        functools.partial(attention_kernel, len(kvs), experts, capacity, blocks_out, half),
        "attend_" + "ab"[half],
        [meta, parents, queries, route_row, *kvs],
        [SMEM, SMEM] + [VMEM] * (2 + len(kvs)),
        [((tokens, half_width), bf16)] + [((rows, half_width), bf16)] * blocks_out,
        flops=2 * 10**9,
    )
    return outs[0], list(outs[1:])


def prepare_kernel(n_rows, half, meta, gain_ref, *refs):
    row_refs, (scaled_ref, squares_ref) = refs[:n_rows], refs[n_rows:]
    width = scaled_ref.shape[1]
    side = meta[0] if half == 0 else 1 - meta[0]
    gain = gain_ref[:, pl.ds(pl.multiple_of(side * width, width), width)]
    rows = jnp.concatenate([r[...].astype(jnp.float32) for r in row_refs], axis=0)
    scaled_ref[...] = (rows * gain).astype(jnp.bfloat16)
    squares = jnp.sum(rows * rows, axis=1, keepdims=True)
    squares_ref[...] = jnp.broadcast_to(squares, squares_ref.shape)


def prepare(meta, gain, rows, slots, half):
    return call(
        functools.partial(prepare_kernel, len(rows), half),
        "rows_" + "ab"[half],
        [meta, gain, *rows],
        [SMEM] + [VMEM] * (1 + len(rows)),
        [((slots, rows[0].shape[1]), jnp.bfloat16), ((slots, 128), jnp.float32)],
        flops=20 * 10**9,
    )


def add_products(meta, pieces, w_refs, rows_scratch, sums_ref, fresh):
    total = sums_ref.shape[1]
    for (row_at, col_at), w_ref in zip(pieces, w_refs):
        depth, columns = w_ref.shape
        rows = rows_scratch[:, pl.ds(pl.multiple_of(meta[row_at], 128), depth)]
        part = jnp.dot(rows, w_ref[...], preferred_element_type=jnp.float32)
        if columns == total:
            sums_ref[...] = part if fresh else sums_ref[...] + part
            fresh = False
        else:
            unit = columns // 2
            sums_ref[:, pl.ds(pl.multiple_of(meta[col_at], 128), unit)] += part[:, :unit]
            up_at = pl.multiple_of(meta[col_at] + total // 2, 128)
            sums_ref[:, pl.ds(up_at, unit)] += part[:, unit:]


def first_kernel(pieces, meta, rows_ref, *refs):
    add_products(meta, pieces, refs[:-1], rows_ref, refs[-1], True)


def first_half(meta, rows, weights, pieces, inner):
    return call(
        functools.partial(first_kernel, pieces),
        "gate_up_a",
        [meta, rows, *weights],
        [SMEM] + [VMEM] * (1 + len(weights)),
        [((rows.shape[0], 2 * inner), jnp.float32)],
    )[0]


def store_down(meta, pieces, w_refs, hidden, out_refs):
    value, blocks = None, len(out_refs)
    for i, ((row_at, col_at), w_ref) in enumerate(zip(pieces, w_refs)):
        depth, columns = w_ref.shape
        rows = hidden[:, pl.ds(pl.multiple_of(meta[row_at], 128), depth)]
        part = jnp.dot(rows, w_ref[...], preferred_element_type=jnp.float32)
        value = part if value is None else value + part
        if i + 1 == len(pieces) or pieces[i + 1][1] != col_at:
            where = pl.ds(pl.multiple_of(meta[col_at], 128), columns)
            height = value.shape[0] // blocks
            for k, out in enumerate(out_refs):
                out[:, where] = value[k * height : (k + 1) * height].astype(jnp.bfloat16)
            value = None


def second_kernel(in_pieces, out_pieces, meta, rows_ref, start_ref, near_ref, far_ref, *refs):
    n_in, n_out = len(in_pieces), len(out_pieces)
    w_refs, refs = refs[: n_in + n_out], refs[n_in + n_out :]
    hidden_ref, out_refs, sums_ref = refs[0], refs[1:-1], refs[-1]
    sums_ref[...] = start_ref[...]
    add_products(meta, in_pieces, w_refs[:n_in], rows_ref, sums_ref, False)
    width = 2 * rows_ref.shape[1]
    squares = near_ref[:, :1] + far_ref[:, :1]
    factor = lax.rsqrt(squares * (1.0 / width) + 1e-06)
    inner = hidden_ref.shape[1]
    gate = sums_ref[:, :inner] * factor
    up = sums_ref[:, inner:] * factor
    hidden_ref[...] = (gate / (1.0 + jnp.exp(-gate)) * up).astype(jnp.bfloat16)
    store_down(meta, out_pieces, w_refs[n_in:], hidden_ref, out_refs)


def second_half(meta, rows, sums, near, far, w_in, in_pieces, w_out, out_pieces, blocks_out):
    slots, columns = sums.shape
    weights = list(w_in) + list(w_out)
    bf16 = jnp.bfloat16
    outs = call(
        functools.partial(second_kernel, in_pieces, out_pieces),
        "gate_up_b_down_a",
        [meta, rows, sums, near, far, *weights],
        [SMEM] + [VMEM] * (4 + len(weights)),
        [((slots, columns // 2), bf16)]
        + [((slots // blocks_out, rows.shape[1]), bf16)] * blocks_out,
        [pltpu.VMEM((slots, columns), jnp.float32)],
        flops=20 * 10**9,
    )
    return outs[0], list(outs[1:])


def third_kernel(pieces, meta, hidden_ref, *refs):
    store_down(meta, pieces, refs[: len(pieces)], hidden_ref, refs[len(pieces) :])


def down_half(meta, hidden, weights, pieces, blocks_out, half_width):
    outs = [((hidden.shape[0] // blocks_out, half_width), jnp.bfloat16)] * blocks_out
    return list(
        call(
            functools.partial(third_kernel, pieces),
            "down_b",
            [meta, hidden, *weights],
            [SMEM] + [VMEM] * (1 + len(weights)),
            outs,
        )
    )


def combine_kernel(experts, capacity, n_rows, last, meta, att_ref, route_ref, weight_ref, *refs):
    row_refs, out_ref = refs[:n_rows], refs[-1]
    tokens, half_width = att_ref.shape
    place = placement_of(route_ref[...], capacity, experts, meta[2], n_rows > 1)
    rows = jnp.concatenate([r[...].astype(jnp.float32) for r in row_refs], axis=0)
    mine = lax.dot_general(
        place,
        rows.astype(jnp.bfloat16),
        (((0,), (0,)), ((), ())),
        preferred_element_type=jnp.float32,
    )
    diagonal = lax.broadcasted_iota(jnp.int32, (tokens, tokens), 0) == lax.broadcasted_iota(
        jnp.int32, (tokens, tokens), 1
    )
    weight = jnp.sum(jnp.where(diagonal, weight_ref[...], 0.0), axis=1, keepdims=True)
    value = (att_ref[...].astype(jnp.float32) + mine * weight).astype(jnp.bfloat16)
    if last:
        before_ref = refs[n_rows]
        before_at = pl.multiple_of(meta[0] * half_width, half_width)
        mine_at = pl.multiple_of((1 - meta[0]) * half_width, half_width)
        out_ref[:, pl.ds(before_at, half_width)] = before_ref[...]
        out_ref[:, pl.ds(mine_at, half_width)] = value
    else:
        out_ref[...] = value


def combine(meta, att, route_row, weight_row, rows, experts, capacity, before):
    tokens, half_width = att.shape
    last = before is not None
    extra = [before] if last else []
    return call(
        functools.partial(combine_kernel, experts, capacity, len(rows), last),
        "combine_" + "ab"[last],
        [meta, att, route_row, weight_row, *rows, *extra],
        [SMEM] + [VMEM] * (3 + len(rows) + len(extra)),
        [((tokens, half_width * (1 + last)), jnp.bfloat16)],
        flops=20 * 10**9,
    )[0]


def swap(array, axis, size, bit):
    return lax.ppermute(array, axis, [(i, i ^ bit) for i in range(size)])


def after(array, *others):
    return lax.optimization_barrier((array, *others))[0]


def body(
    queries, keys, values, tree_parents, routes, route_weight, norm_gain, expert_in, expert_out
):
    n_grp, n_ctx, n_exp = (lax.axis_size(name) for name in ("grp", "ctx", "exp"))
    grp, ctx, exp = (lax.axis_index(name) for name in ("grp", "ctx", "exp"))
    tokens, width = queries.shape[1:]
    assert tokens == TREE_BLOCK and tree_parents.shape[1] == n_ctx and routes.shape[2] == 1
    assert n_ctx & (n_ctx - 1) == 0 and n_ctx > 1 and n_grp == 2
    capacity = max(2, 5 * tokens // (4 * n_exp))
    slots = n_exp * capacity
    shifted = n_exp <= 8 and capacity % 8 == 0
    blocks_out = n_exp if shifted else 1
    half_width = width // KV_HEADS
    top = n_ctx // 2
    low_bits = [1 << b for b in range(top.bit_length() - 1)]
    half = ctx // top

    depth = expert_in.shape[1]
    inner = expert_out.shape[1]
    columns = expert_out.shape[2]
    w_out = expert_out[0]
    route_row = routes.reshape(1, tokens)
    weight_row = route_weight.reshape(1, tokens)
    gain = norm_gain.reshape(1, width)

    kv = jnp.concatenate([keys[0], values[0]], axis=1)
    kv_far = swap(kv, "ctx", n_ctx, top)
    unit = expert_out.shape[1] // 3

    def third_of(array, start):
        cut = lax.dynamic_slice_in_dim(array, start, unit, 2)
        return cut.reshape(cut.shape[0], 2 * unit)

    w_mine = third_of(expert_in[0], grp * unit)
    near, far = [kv], [after(kv_far, w_mine)]
    for bit in low_bits:
        near = near + [swap(x, "ctx", n_ctx, bit) for x in near]
        far = far + [swap(x, "ctx", n_ctx, bit) for x in far]
    kvs = near + far

    scalars = [half, ctx, exp, jnp.int32(0)]

    def note(value):
        scalars.append(jnp.asarray(value, jnp.int32))
        return len(scalars) - 1

    zero = 3
    shard = lax.rem(ctx, top)
    in_row = [note((shard ^ j) * depth) for j in range(top)]
    out_col = [note((shard ^ j) * columns) for j in range(top)]
    thirds = [note(grp * unit), note((1 - grp) * unit), note(2 * unit)]
    meta = jnp.stack(scalars)

    def spread(array):
        found = [array]
        for bit in low_bits:
            found = found + [swap(a, "ctx", n_ctx, bit) for a in found]
        return found

    def send(blocks, back):
        if not shifted:
            whole = blocks[0].reshape(n_exp, capacity, half_width)
            whole = lax.all_to_all(whole, "exp", 0, 0, tiled=True)
            return [whole.reshape(slots, half_width)]
        moved = [blocks[0]]
        for k in range(1, n_exp):
            shift = n_exp - k if back else k
            moved.append(
                lax.ppermute(blocks[k], "exp", [(i, (i + shift) % n_exp) for i in range(n_exp)])
            )
        return moved

    w_first = swap(w_mine, "ctx", n_ctx, top)
    w_in = after(expert_in[0], kvs[-1]).reshape(depth, 2 * inner)
    w_in_a = spread(after(w_in, *kvs[1:]))

    att_a, packed_a = attention(
        meta,
        tree_parents,
        after(queries[0], w_in_a[-1]),
        route_row,
        kvs,
        n_exp,
        capacity,
        blocks_out,
        0,
    )
    rows_a = send(packed_a, False)
    w_direct = third_of(after(expert_in[0], att_a), 2 * unit)
    att_b, packed_b = attention(
        meta,
        tree_parents,
        after(queries[0], att_a, w_direct),
        route_row,
        kvs,
        n_exp,
        capacity,
        blocks_out,
        1,
    )
    rows_b = send([after(x, *rows_a) for x in packed_b], False)

    w_direct = swap(w_direct, "ctx", n_ctx, top)
    w_second = swap(after(w_first, att_b), "grp", 2, 1)
    scaled_a, squares_a = prepare(meta, gain, rows_a, slots, 0)
    sums = first_half(meta, scaled_a, w_in_a, [(r, zero) for r in in_row], inner)
    w_in_b = [spread(after(w_first, *rows_b))]
    w_out_a = spread(after(w_out, *rows_b))
    v_first = lax.dynamic_slice_in_dim(after(w_out, *rows_a), grp * unit, unit, 0)
    v_first = swap(after(v_first, *rows_b), "ctx", n_ctx, top)
    w_in_b.append(spread(after(w_direct, *rows_b)))
    w_in_b.append(spread(after(w_second, *rows_b)))
    w_in_b = list(zip(w_in_b[0], w_in_b[2], w_in_b[1]))
    scaled_b, squares_b = prepare(meta, gain, rows_b, slots, 1)

    in_pieces = [(r, c) for r in in_row for c in thirds]
    hidden, out_a = second_half(
        meta,
        scaled_b,
        sums,
        squares_a,
        squares_b,
        [w for shard_pieces in w_in_b for w in shard_pieces],
        in_pieces,
        w_out_a,
        [(zero, c) for c in out_col],
        blocks_out,
    )
    back_a = send(out_a, True)
    v_direct = swap(after(w_out[2 * unit :], hidden), "ctx", n_ctx, top)
    v_second = swap(after(v_first, hidden), "grp", 2, 1)
    done = combine(meta, att_a, route_row, weight_row, back_a, n_exp, capacity, None)
    w_out_b = list(zip(*[spread(after(v, done)) for v in (v_first, v_second, v_direct)]))
    out_b = down_half(
        meta,
        after(hidden, *out_a),
        [w for shard_pieces in w_out_b for w in shard_pieces],
        [(r, c) for c in out_col for r in thirds],
        blocks_out,
        half_width,
    )
    back_b = send(out_b, True)
    done = combine(meta, att_b, route_row, weight_row, back_b, n_exp, capacity, done)
    return done[None]


def solution(mesh):
    in_specs = (
        P(("grp", "exp"), "ctx", None),
        P(("grp", "exp"), "ctx", None),
        P(("grp", "exp"), "ctx", None),
        P(("grp", "exp"), None),
        P(("grp", "exp"), "ctx", None),
        P(("grp", "exp"), "ctx", None),
        P(),
        P("exp", "ctx", None, None),
        P("exp", None, "ctx"),
    )
    out_specs = P(("grp", "exp"), "ctx", None)
    return jax.shard_map(body, mesh=mesh, in_specs=in_specs, out_specs=out_specs, check_vma=False)
```

```python
import functools
import math

import jax
import jax.numpy as jnp
from jax import lax
from jax.experimental import pallas as pl
from jax.experimental.pallas import tpu as pltpu
from jax.sharding import PartitionSpec as P

KV_HEADS = 2
HEAD_DIM = 128
TREE_BLOCK = 128
NEG = -1e30
MIB = 1024 * 1024
VMEM = pl.BlockSpec(memory_space=pltpu.VMEM)
SMEM = pl.BlockSpec(memory_space=pltpu.SMEM)


def call(kernel, name, args, specs, outs, scratch=(), mib=16, flops=1000):
    return pl.pallas_call(
        kernel,
        in_specs=specs,
        out_specs=[VMEM] * len(outs),
        out_shape=[jax.ShapeDtypeStruct(s, d) for s, d in outs],
        scratch_shapes=list(scratch),
        compiler_params=pltpu.CompilerParams(vmem_limit_bytes=mib * MIB),
        cost_estimate=pl.CostEstimate(flops=flops, bytes_accessed=1000, transcendentals=0),
        name=name,
    )(*args)


def placement_of(route_row, capacity, experts, first, relative):
    tokens = route_row.shape[1]
    if relative:
        route_row = lax.rem(route_row - first + experts, experts)
    rows = max(8, experts)
    expert_ids = lax.broadcasted_iota(jnp.int32, (rows, tokens), 0)
    hot = jnp.where(expert_ids == route_row, 1.0, 0.0)
    before = lax.broadcasted_iota(jnp.int32, (tokens, tokens), 0) < lax.broadcasted_iota(
        jnp.int32, (tokens, tokens), 1
    )
    earlier = jnp.dot(
        hot.astype(jnp.bfloat16),
        jnp.where(before, 1.0, 0.0).astype(jnp.bfloat16),
        preferred_element_type=jnp.float32,
    )
    rank = jnp.sum(earlier * hot, axis=0, keepdims=True).astype(jnp.int32)
    slot = route_row * capacity + rank
    slot_ids = lax.broadcasted_iota(jnp.int32, (experts * capacity, tokens), 0)
    return jnp.where(slot_ids == slot, 1.0, 0.0)


def attention_kernel(n_ctx, experts, capacity, blocks_out, half, meta, parents, q_ref, route_ref, *refs):
    kv = refs[:n_ctx]
    att_ref = refs[n_ctx]
    out_refs = refs[n_ctx + 1 :]
    tokens, half_width = att_ref.shape
    heads = half_width // HEAD_DIM
    side = meta[0] if half == 0 else 1 - meta[0]
    me = meta[1]
    reached = [jnp.int32(0)] * n_ctx
    current = me
    for _ in range(n_ctx):
        current = parents[0, current]
        for j in range(1, n_ctx):
            reached[j] = jnp.where(current == (me ^ j), jnp.int32(1), reached[j])
    causal = lax.broadcasted_iota(jnp.int32, (tokens, tokens), 1) <= lax.broadcasted_iota(
        jnp.int32, (tokens, tokens), 0
    )
    key_at = pl.ds(pl.multiple_of(side * HEAD_DIM, HEAD_DIM), HEAD_DIM)
    value_at = pl.ds(pl.multiple_of((KV_HEADS + side) * HEAD_DIM, HEAD_DIM), HEAD_DIM)
    keys_t = jnp.concatenate([r[:, key_at] for r in kv], axis=0).T
    ones = jnp.ones((tokens, HEAD_DIM), jnp.bfloat16)
    values = jnp.concatenate(
        [jnp.concatenate([r[:, value_at], ones], axis=1) for r in kv], axis=0
    )
    bias = jnp.concatenate(
        [jnp.where(causal, 0.0, NEG)]
        + [
            jnp.broadcast_to(jnp.where(reached[j] == 1, 0.0, NEG), (tokens, tokens))
            for j in range(1, n_ctx)
        ],
        axis=1,
    )
    scale = math.log2(math.e) / math.sqrt(HEAD_DIM)
    for h in range(heads):
        columns = slice(h * HEAD_DIM, (h + 1) * HEAD_DIM)
        q_at = pl.ds(pl.multiple_of(side * half_width + h * HEAD_DIM, HEAD_DIM), HEAD_DIM)
        scores = jnp.dot(q_ref[:, q_at], keys_t, preferred_element_type=jnp.float32)
        scores = scores * scale + bias
        peak = jnp.max(scores, axis=1, keepdims=True)
        weights = jnp.exp2(scores - peak).astype(jnp.bfloat16)
        total = jnp.dot(weights, values, preferred_element_type=jnp.float32)
        att_ref[:, columns] = (total[:, :HEAD_DIM] / total[:, HEAD_DIM:]).astype(jnp.bfloat16)
    place = placement_of(route_ref[...], capacity, experts, meta[2], blocks_out > 1)
    packed = jnp.dot(place.astype(jnp.bfloat16), att_ref[...], preferred_element_type=jnp.float32)
    rows = experts * capacity // blocks_out
    for k in range(blocks_out):
        out_refs[k][...] = packed[k * rows : (k + 1) * rows].astype(jnp.bfloat16)


def attention(meta, parents, queries, route_row, kvs, experts, capacity, blocks_out, half):
    tokens, width = queries.shape
    half_width = width // KV_HEADS
    rows = experts * capacity // blocks_out
    bf16 = jnp.bfloat16
    outs = call(
        functools.partial(attention_kernel, len(kvs), experts, capacity, blocks_out, half),
        "attend_" + "ab"[half],
        [meta, parents, queries, route_row, *kvs],
        [SMEM, SMEM] + [VMEM] * (2 + len(kvs)),
        [((tokens, half_width), bf16)] + [((rows, half_width), bf16)] * blocks_out,
        flops=2 * 10**9,
    )
    return outs[0], list(outs[1:])


def products_kernel(n_rows, n_weights, row_at, packed, meta, gain_ref, *refs):
    row_refs, w_refs, refs = refs[:n_rows], refs[n_rows : n_rows + n_weights], refs[n_rows + n_weights :]
    scaled = refs[-1]
    width = scaled.shape[1]
    gain = gain_ref[:, pl.ds(pl.multiple_of(meta[0] * width, width), width)]
    rows = jnp.concatenate([r[...].astype(jnp.float32) for r in row_refs], axis=0)
    scaled[...] = (rows * gain).astype(jnp.bfloat16)
    squares = jnp.sum(rows * rows, axis=1, keepdims=True)
    squares = jnp.broadcast_to(squares, (scaled.shape[0], 128))
    sums = None
    for i, w_ref in enumerate(w_refs):
        features = pl.ds(pl.multiple_of(meta[row_at + i], 128), w_ref.shape[0])
        part = jnp.dot(scaled[:, features], w_ref[...], preferred_element_type=jnp.float32)
        sums = part if sums is None else sums + part
    if packed:
        columns = sums.shape[1]
        refs[0][:, :columns] = sums.astype(jnp.bfloat16)
        high = squares.astype(jnp.bfloat16)
        low = (squares - high.astype(jnp.float32)).astype(jnp.bfloat16)
        lane = lax.broadcasted_iota(jnp.int32, squares.shape, 1)
        refs[0][:, columns:] = jnp.where(
            lane < 64, high.astype(jnp.float32), low.astype(jnp.float32)
        ).astype(jnp.bfloat16)
    else:
        refs[0][...] = sums
        refs[1][...] = squares


def products(meta, gain, rows, weights, row_at, slots, packed):
    half_width = rows[0].shape[1]
    columns = weights[0].shape[1]
    f32, bf16 = jnp.float32, jnp.bfloat16
    outs = [((slots, columns + 128), bf16)] if packed else [((slots, columns), f32), ((slots, 128), f32)]
    return call(
        functools.partial(products_kernel, len(rows), len(weights), row_at, packed),
        "products_" + "ab"[packed],
        [meta, gain, *rows, *weights],
        [SMEM] + [VMEM] * (1 + len(rows) + len(weights)),
        outs,
        [pltpu.VMEM((slots, half_width), bf16)],
        flops=20 * 10**9,
    )


def store_down(meta, col_at, w_refs, hidden, out_refs):
    for i, w_ref in enumerate(w_refs):
        value = jnp.dot(hidden, w_ref[...], preferred_element_type=jnp.float32)
        where = pl.ds(pl.multiple_of(meta[col_at + i], 128), w_ref.shape[1])
        height = value.shape[0] // len(out_refs)
        for k, out in enumerate(out_refs):
            out[:, where] = value[k * height : (k + 1) * height].astype(jnp.bfloat16)


def finish_kernel(n_weights, col_at, width, meta, sums_ref, squares_ref, far_ref, *refs):
    w_refs, hidden_ref, out_refs = refs[:n_weights], refs[n_weights], refs[n_weights + 1 :]
    inner = hidden_ref.shape[1]
    squares = squares_ref[:, :1]
    for at in (0, 64):
        squares = squares + far_ref[:, 2 * inner + at : 2 * inner + at + 1].astype(jnp.float32)
    factor = lax.rsqrt(squares * (1.0 / width) + 1e-06)
    gate = (sums_ref[:, :inner] + far_ref[:, :inner].astype(jnp.float32)) * factor
    up = (sums_ref[:, inner:] + far_ref[:, inner : 2 * inner].astype(jnp.float32)) * factor
    hidden = (gate / (1.0 + jnp.exp(-gate)) * up).astype(jnp.bfloat16)
    hidden_ref[...] = hidden
    store_down(meta, col_at, w_refs, hidden, out_refs)


def finish(meta, sums, squares, far, weights, col_at, width, blocks_out):
    slots, columns = sums.shape
    bf16 = jnp.bfloat16
    outs = call(
        functools.partial(finish_kernel, len(weights), col_at, width),
        "hidden_down_a",
        [meta, sums, squares, far, *weights],
        [SMEM] + [VMEM] * (3 + len(weights)),
        [((slots, columns // 2), bf16)]
        + [((slots // blocks_out, width // KV_HEADS), bf16)] * blocks_out,
    )
    return outs[0], list(outs[1:])


def down_kernel(n_weights, col_at, meta, hidden_ref, *refs):
    store_down(meta, col_at, refs[:n_weights], hidden_ref[...], refs[n_weights:])


def down(meta, hidden, weights, col_at, width, blocks_out):
    outs = [((hidden.shape[0] // blocks_out, width // KV_HEADS), jnp.bfloat16)] * blocks_out
    return list(
        call(
            functools.partial(down_kernel, len(weights), col_at),
            "down_b",
            [meta, hidden, *weights],
            [SMEM] + [VMEM] * (1 + len(weights)),
            outs,
        )
    )


def combine_kernel(experts, capacity, n_rows, last, meta, att_ref, route_ref, weight_ref, *refs):
    row_refs, out_ref = refs[:n_rows], refs[-1]
    tokens, half_width = att_ref.shape
    place = placement_of(route_ref[...], capacity, experts, meta[2], n_rows > 1)
    height = place.shape[0] // n_rows
    mine = None
    for k, row_ref in enumerate(row_refs):
        part = lax.dot_general(
            place[k * height : (k + 1) * height].astype(jnp.bfloat16),
            row_ref[...],
            (((0,), (0,)), ((), ())),
            preferred_element_type=jnp.float32,
        )
        mine = part if mine is None else mine + part
    diagonal = lax.broadcasted_iota(jnp.int32, (tokens, tokens), 0) == lax.broadcasted_iota(
        jnp.int32, (tokens, tokens), 1
    )
    weight = jnp.sum(jnp.where(diagonal, weight_ref[...], 0.0), axis=1, keepdims=True)
    value = (att_ref[...].astype(jnp.float32) + mine * weight).astype(jnp.bfloat16)
    if last:
        before_ref = refs[n_rows]
        before_at = pl.multiple_of(meta[0] * half_width, half_width)
        mine_at = pl.multiple_of((1 - meta[0]) * half_width, half_width)
        out_ref[:, pl.ds(before_at, half_width)] = before_ref[...]
        out_ref[:, pl.ds(mine_at, half_width)] = value
    else:
        out_ref[...] = value


def combine(meta, att, route_row, weight_row, rows, experts, capacity, before):
    tokens, half_width = att.shape
    last = before is not None
    extra = [before] if last else []
    return call(
        functools.partial(combine_kernel, experts, capacity, len(rows), last),
        "combine_" + "ab"[last],
        [meta, att, route_row, weight_row, *rows, *extra],
        [SMEM] + [VMEM] * (3 + len(rows) + len(extra)),
        [((tokens, half_width * (1 + last)), jnp.bfloat16)],
        flops=20 * 10**9,
    )[0]


def swap(array, axis, size, bit):
    return lax.ppermute(array, axis, [(i, i ^ bit) for i in range(size)])


def after(array, *others):
    return lax.optimization_barrier((array, *others))[0]


def body(
    queries, keys, values, tree_parents, routes, route_weight, norm_gain, expert_in, expert_out
):
    n_ctx, n_exp = lax.axis_size("ctx"), lax.axis_size("exp")
    ctx, exp = lax.axis_index("ctx"), lax.axis_index("exp")
    tokens, width = queries.shape[1:]
    assert tokens == TREE_BLOCK and tree_parents.shape[1] == n_ctx and routes.shape[2] == 1
    assert n_ctx & (n_ctx - 1) == 0 and n_ctx > 1
    capacity = max(2, 5 * tokens // (4 * n_exp))
    slots = n_exp * capacity
    shifted = n_exp <= 8 and capacity % 8 == 0
    blocks_out = n_exp if shifted else 1
    half_width = width // KV_HEADS
    top = n_ctx // 2
    low_bits = [1 << b for b in range(top.bit_length() - 1)]
    half = ctx // top

    depth = expert_in.shape[1]
    inner = expert_out.shape[1]
    columns = expert_out.shape[2]
    route_row = routes.reshape(1, tokens)
    weight_row = route_weight.reshape(1, tokens)
    gain = norm_gain.reshape(1, width)

    w_in = expert_in[0].reshape(depth, 2 * inner)

    kv = jnp.concatenate([after(keys[0], w_in), values[0]], axis=1)
    near, far = [kv], [swap(kv, "ctx", n_ctx, top)]
    for bit in low_bits:
        near = near + [swap(x, "ctx", n_ctx, bit) for x in near]
        far = far + [swap(x, "ctx", n_ctx, bit) for x in far]
    kvs = near + far

    shards = [lax.rem(ctx, top) ^ j for j in range(top)]
    row_at, col_at = 3, 3 + top
    meta = jnp.stack([half, ctx, exp] + [j * depth for j in shards] + [j * columns for j in shards])

    def spread(array):
        found = [array]
        for bit in low_bits:
            found = found + [swap(a, "ctx", n_ctx, bit) for a in found]
        return found

    def send(blocks, back, cross):
        if not shifted:
            whole = blocks[0].reshape(n_exp, capacity, half_width)
            whole = lax.all_to_all(whole, "exp", 0, 0, tiled=True).reshape(slots, half_width)
            return [swap(whole, "ctx", n_ctx, top) if cross else whole]
        moved = []
        for k in range(n_exp):
            shift = (n_exp - k) % n_exp if back else k
            bit = top if cross else 0
            pairs = [
                (c * n_exp + e, (c ^ bit) * n_exp + (e + shift) % n_exp)
                for c in range(n_ctx)
                for e in range(n_exp)
            ]
            still = k == 0 and not cross
            moved.append(blocks[k] if still else lax.ppermute(blocks[k], ("ctx", "exp"), pairs))
        return moved

    def attend(queries, part):
        return attention(
            meta, tree_parents, queries, route_row, kvs, n_exp, capacity, blocks_out, part
        )

    att_b, packed_b = attend(queries[0], 1)
    rows_b = send(packed_b, False, True)
    att_a, packed_a = attend(after(queries[0], att_b), 0)
    rows_a = send(packed_a, False, False)

    w_ins = spread(after(w_in, *kvs[1:]))
    w_outs = spread(after(expert_out[0], *rows_b))
    rows_b = [after(r, att_a) for r in rows_b]
    far_sums = products(meta, gain, rows_b, w_ins, row_at, slots, True)[0]
    far_sums = swap(far_sums, "ctx", n_ctx, top)
    sums, squares = products(meta, gain, rows_a, w_ins, row_at, slots, False)
    hidden, out_a = finish(meta, sums, squares, far_sums, w_outs, col_at, width, blocks_out)
    back_a = send(out_a, True, False)
    out_b = down(meta, swap(hidden, "ctx", n_ctx, top), w_outs, col_at, width, blocks_out)
    back_b = send(out_b, True, True)
    done = combine(meta, att_a, route_row, weight_row, back_a, n_exp, capacity, None)
    done = combine(meta, att_b, route_row, weight_row, back_b, n_exp, capacity, done)
    return done[None]


def solution(mesh):
    in_specs = (
        P(("grp", "exp"), "ctx", None),
        P(("grp", "exp"), "ctx", None),
        P(("grp", "exp"), "ctx", None),
        P(("grp", "exp"), None),
        P(("grp", "exp"), "ctx", None),
        P(("grp", "exp"), "ctx", None),
        P(),
        P("exp", "ctx", None, None),
        P("exp", None, "ctx"),
    )
    out_specs = P(("grp", "exp"), "ctx", None)
    return jax.shard_map(body, mesh=mesh, in_specs=in_specs, out_specs=out_specs, check_vma=False)
```

```python
import functools
import math

import jax
import jax.numpy as jnp
from jax import lax
from jax.experimental import pallas as pl
from jax.experimental.pallas import tpu as pltpu
from jax.sharding import PartitionSpec as P

KV_HEADS = 2
HEAD_DIM = 128
TREE_BLOCK = 128
NEG = -1e30
MIB = 1024 * 1024
VMEM = pl.BlockSpec(memory_space=pltpu.VMEM)
SMEM = pl.BlockSpec(memory_space=pltpu.SMEM)


def call(kernel, name, args, specs, outs, scratch=(), mib=16, flops=1000, out_space=pltpu.VMEM):
    return pl.pallas_call(
        kernel,
        in_specs=specs,
        out_specs=[pl.BlockSpec(memory_space=out_space)] * len(outs),
        out_shape=[jax.ShapeDtypeStruct(s, d) for s, d in outs],
        scratch_shapes=list(scratch),
        compiler_params=pltpu.CompilerParams(vmem_limit_bytes=mib * MIB),
        cost_estimate=pl.CostEstimate(flops=flops, bytes_accessed=1000, transcendentals=0),
        name=name,
    )(*args)


def shifts(experts):
    return [experts // 2] + [s for s in range(1, experts) if 2 * s != experts] + [0]


def placement_of(route_row, capacity, experts, first, relative):
    tokens = route_row.shape[1]
    if relative:
        shift = lax.rem(route_row - first + experts, experts)
        for i, s in enumerate(shifts(experts)):
            route_row = jnp.where(shift == s, i, route_row)
    rows = max(8, experts)
    expert_ids = lax.broadcasted_iota(jnp.int32, (rows, tokens), 0)
    hot = jnp.where(expert_ids == route_row, 1.0, 0.0)
    before = lax.broadcasted_iota(jnp.int32, (tokens, tokens), 0) < lax.broadcasted_iota(
        jnp.int32, (tokens, tokens), 1
    )
    earlier = jnp.dot(
        hot.astype(jnp.bfloat16),
        jnp.where(before, 1.0, 0.0).astype(jnp.bfloat16),
        preferred_element_type=jnp.float32,
    )
    rank = jnp.sum(earlier * hot, axis=0, keepdims=True).astype(jnp.int32)
    slot = route_row * capacity + rank
    slot_ids = lax.broadcasted_iota(jnp.int32, (experts * capacity, tokens), 0)
    return jnp.where(slot_ids == slot, 1.0, 0.0)


def plan_kernel(experts, capacity, relative, meta, route_ref, weight_ref, q_hbm, *refs):
    place_ref, back_ref, column_ref, q_ref, sem = refs
    copy = pltpu.make_async_copy(q_hbm, q_ref, sem)
    copy.start()
    tokens = route_ref.shape[1]
    place = placement_of(route_ref[...], capacity, experts, meta[2], relative)
    place_ref[...] = place.astype(jnp.bfloat16)
    back_ref[...] = place.T.astype(jnp.bfloat16)
    diagonal = lax.broadcasted_iota(jnp.int32, (tokens, tokens), 0) == lax.broadcasted_iota(
        jnp.int32, (tokens, tokens), 1
    )
    weight = jnp.sum(jnp.where(diagonal, weight_ref[...], 0.0), axis=1, keepdims=True)
    column_ref[...] = jnp.broadcast_to(weight, column_ref.shape)
    copy.wait()


def plan(meta, route_row, weight_row, queries, experts, capacity, relative):
    tokens = route_row.shape[1]
    slots = experts * capacity
    bf16 = jnp.bfloat16
    return call(
        functools.partial(plan_kernel, experts, capacity, relative),
        "plan",
        [meta, route_row, weight_row, queries],
        [SMEM, VMEM, VMEM, pl.BlockSpec(memory_space=pl.ANY)],
        [
            ((slots, tokens), bf16),
            ((tokens, slots), bf16),
            ((tokens, 128), jnp.float32),
            (queries.shape, bf16),
        ],
        [pltpu.SemaphoreType.DMA],
    )


def attention_kernel(n_ctx, half, meta, parents, q_ref, place_ref, *refs):
    kv = refs[:n_ctx]
    att_ref = refs[n_ctx]
    out_refs = refs[n_ctx + 1 :]
    tokens, half_width = att_ref.shape
    heads = half_width // HEAD_DIM
    side = meta[0] if half == 0 else 1 - meta[0]
    me = meta[1]
    reached = [jnp.int32(0)] * n_ctx
    current = me
    for _ in range(n_ctx):
        current = parents[0, current]
        for j in range(1, n_ctx):
            reached[j] = jnp.where(current == (me ^ j), jnp.int32(1), reached[j])
    causal = lax.broadcasted_iota(jnp.int32, (tokens, tokens), 1) <= lax.broadcasted_iota(
        jnp.int32, (tokens, tokens), 0
    )
    key_at = pl.ds(pl.multiple_of(side * HEAD_DIM, HEAD_DIM), HEAD_DIM)
    value_at = pl.ds(pl.multiple_of((KV_HEADS + side) * HEAD_DIM, HEAD_DIM), HEAD_DIM)
    keys_t = jnp.concatenate([r[:, key_at] for r in kv], axis=0).T
    ones = jnp.ones((tokens, HEAD_DIM), jnp.bfloat16)
    values = jnp.concatenate(
        [jnp.concatenate([r[:, value_at], ones], axis=1) for r in kv], axis=0
    )
    bias = jnp.concatenate(
        [jnp.where(causal, 0.0, NEG)]
        + [
            jnp.broadcast_to(jnp.where(reached[j] == 1, 0.0, NEG), (tokens, tokens))
            for j in range(1, n_ctx)
        ],
        axis=1,
    )
    scale = math.log2(math.e) / math.sqrt(HEAD_DIM)
    for h in range(heads):
        columns = slice(h * HEAD_DIM, (h + 1) * HEAD_DIM)
        q_at = pl.ds(pl.multiple_of(side * half_width + h * HEAD_DIM, HEAD_DIM), HEAD_DIM)
        scores = jnp.dot(q_ref[:, q_at], keys_t, preferred_element_type=jnp.float32)
        scores = scores * scale + bias
        peak = jnp.max(scores, axis=1, keepdims=True)
        weights = jnp.exp2(scores - peak).astype(jnp.bfloat16)
        total = jnp.dot(weights, values, preferred_element_type=jnp.float32)
        att_ref[:, columns] = (total[:, :HEAD_DIM] / total[:, HEAD_DIM:]).astype(jnp.bfloat16)
    packed = jnp.dot(place_ref[...], att_ref[...], preferred_element_type=jnp.float32)
    for k, out in enumerate(out_refs):
        rows = out.shape[0]
        out[...] = packed[k * rows : (k + 1) * rows].astype(jnp.bfloat16)


def attention(meta, parents, queries, place, kvs, blocks_out, half):
    tokens, width = queries.shape
    half_width = width // KV_HEADS
    rows = place.shape[0] // blocks_out
    bf16 = jnp.bfloat16
    outs = call(
        functools.partial(attention_kernel, len(kvs), half),
        "attend_" + "ab"[half],
        [meta, parents, queries, place, *kvs],
        [SMEM, SMEM] + [VMEM] * (2 + len(kvs)),
        [((tokens, half_width), bf16)] + [((rows, half_width), bf16)] * blocks_out,
        flops=2 * 10**9,
    )
    return outs[0], list(outs[1:])


def products_kernel(n_rows, n_weights, row_at, packed, meta, gain_ref, *refs):
    row_refs, w_refs, refs = refs[:n_rows], refs[n_rows : n_rows + n_weights], refs[n_rows + n_weights :]
    scaled = refs[-1]
    width = scaled.shape[1]
    gain = gain_ref[:, pl.ds(pl.multiple_of(meta[0] * width, width), width)]
    rows = jnp.concatenate([r[...].astype(jnp.float32) for r in row_refs], axis=0)
    scaled[...] = (rows * gain).astype(jnp.bfloat16)
    squares = jnp.sum(rows * rows, axis=1, keepdims=True)
    squares = jnp.broadcast_to(squares, (scaled.shape[0], 128))
    sums = None
    for i, w_ref in enumerate(w_refs):
        features = pl.ds(pl.multiple_of(meta[row_at + i], 128), w_ref.shape[0])
        part = jnp.dot(scaled[:, features], w_ref[...], preferred_element_type=jnp.float32)
        sums = part if sums is None else sums + part
    if packed:
        columns = sums.shape[1]
        refs[0][:, :columns] = sums.astype(jnp.bfloat16)
        high = squares.astype(jnp.bfloat16)
        low = (squares - high.astype(jnp.float32)).astype(jnp.bfloat16)
        lane = lax.broadcasted_iota(jnp.int32, squares.shape, 1)
        refs[0][:, columns:] = jnp.where(
            lane < 64, high.astype(jnp.float32), low.astype(jnp.float32)
        ).astype(jnp.bfloat16)
    else:
        refs[0][...] = sums
        refs[1][...] = squares


def products(meta, gain, rows, weights, row_at, slots, packed):
    half_width = rows[0].shape[1]
    columns = weights[0].shape[1]
    f32, bf16 = jnp.float32, jnp.bfloat16
    outs = [((slots, columns + 128), bf16)] if packed else [((slots, columns), f32), ((slots, 128), f32)]
    return call(
        functools.partial(products_kernel, len(rows), len(weights), row_at, packed),
        "products_" + "ab"[packed],
        [meta, gain, *rows, *weights],
        [SMEM] + [VMEM] * (1 + len(rows) + len(weights)),
        outs,
        [pltpu.VMEM((slots, half_width), bf16)],
        flops=20 * 10**9,
    )


def store_down(meta, col_at, w_refs, hidden, out_refs):
    for i, w_ref in enumerate(w_refs):
        value = jnp.dot(hidden, w_ref[...], preferred_element_type=jnp.float32)
        where = pl.ds(pl.multiple_of(meta[col_at + i], 128), w_ref.shape[1])
        height = value.shape[0] // len(out_refs)
        for k, out in enumerate(out_refs):
            out[:, where] = value[k * height : (k + 1) * height].astype(jnp.bfloat16)


def finish_kernel(n_weights, col_at, width, meta, sums_ref, squares_ref, far_ref, *refs):
    w_refs, hidden_ref, out_refs = refs[:n_weights], refs[n_weights], refs[n_weights + 1 :]
    inner = hidden_ref.shape[1]
    squares = squares_ref[:, :1]
    for at in (0, 64):
        squares = squares + far_ref[:, 2 * inner + at : 2 * inner + at + 1].astype(jnp.float32)
    factor = lax.rsqrt(squares * (1.0 / width) + 1e-06)
    gate = (sums_ref[:, :inner] + far_ref[:, :inner].astype(jnp.float32)) * factor
    up = (sums_ref[:, inner:] + far_ref[:, inner : 2 * inner].astype(jnp.float32)) * factor
    hidden = (gate / (1.0 + jnp.exp(-gate)) * up).astype(jnp.bfloat16)
    hidden_ref[...] = hidden
    store_down(meta, col_at, w_refs, hidden, out_refs)


def finish(meta, sums, squares, far, weights, col_at, width, blocks_out):
    slots, columns = sums.shape
    bf16 = jnp.bfloat16
    outs = call(
        functools.partial(finish_kernel, len(weights), col_at, width),
        "hidden_down_a",
        [meta, sums, squares, far, *weights],
        [SMEM] + [VMEM] * (3 + len(weights)),
        [((slots, columns // 2), bf16)]
        + [((slots // blocks_out, width // KV_HEADS), bf16)] * blocks_out,
    )
    return outs[0], list(outs[1:])


def down_kernel(n_weights, col_at, meta, hidden_ref, *refs):
    store_down(meta, col_at, refs[:n_weights], hidden_ref[...], refs[n_weights:])


def down(meta, hidden, weights, col_at, width, blocks_out):
    outs = [((hidden.shape[0] // blocks_out, width // KV_HEADS), jnp.bfloat16)] * blocks_out
    return list(
        call(
            functools.partial(down_kernel, len(weights), col_at),
            "down_b",
            [meta, hidden, *weights],
            [SMEM] + [VMEM] * (1 + len(weights)),
            outs,
        )
    )


def combine_kernel(last, meta, att_ref, back_ref, column_ref, *refs):
    row_refs, refs = refs[: -1 - 3 * last], refs[-1 - 3 * last :]
    half_width = att_ref.shape[1]
    if last:
        before_ref, out_ref, value_ref, sems = refs
        before_at = pl.multiple_of(meta[0] * half_width, half_width)
        mine_at = pl.multiple_of((1 - meta[0]) * half_width, half_width)
        copies = [
            pltpu.make_async_copy(before_ref, out_ref.at[:, pl.ds(before_at, half_width)], sems.at[0])
        ]
        copies[0].start()
    rows = jnp.concatenate([r[...].astype(jnp.float32) for r in row_refs], axis=0)
    rows = rows.astype(jnp.bfloat16)
    parts = 4 if last else 1
    step = half_width // parts
    for i in range(parts):
        columns = slice(i * step, (i + 1) * step)
        mine = jnp.dot(back_ref[...], rows[:, columns], preferred_element_type=jnp.float32)
        value = att_ref[:, columns].astype(jnp.float32) + mine * column_ref[:, :1]
        value = value.astype(jnp.bfloat16)
        if last:
            value_ref[:, columns] = value
            place = out_ref.at[:, pl.ds(pl.multiple_of(mine_at + i * step, 128), step)]
            copies.append(
                pltpu.make_async_copy(value_ref.at[:, pl.ds(i * step, step)], place, sems.at[i + 1])
            )
            copies[-1].start()
        else:
            refs[0][:, columns] = value
    if last:
        for copy in copies:
            copy.wait()


def combine(meta, att, back, column, rows, before):
    tokens, half_width = att.shape
    last = before is not None
    extra = [before] if last else []
    scratch = [pltpu.VMEM(att.shape, att.dtype), pltpu.SemaphoreType.DMA((5,))] if last else []
    return call(
        functools.partial(combine_kernel, last),
        "combine_" + "ab"[last],
        [meta, att, back, column, *rows, *extra],
        [SMEM] + [VMEM] * (3 + len(rows) + len(extra)),
        [((tokens, half_width * (1 + last)), jnp.bfloat16)],
        scratch,
        flops=20 * 10**9,
        out_space=pl.ANY if last else pltpu.VMEM,
    )[0]


def swap(array, axis, size, bit):
    return lax.ppermute(array, axis, [(i, i ^ bit) for i in range(size)])


def after(array, *others):
    return lax.optimization_barrier((array, *others))[0]


def body(
    queries, keys, values, tree_parents, routes, route_weight, norm_gain, expert_in, expert_out
):
    n_ctx, n_exp = lax.axis_size("ctx"), lax.axis_size("exp")
    ctx, exp = lax.axis_index("ctx"), lax.axis_index("exp")
    tokens, width = queries.shape[1:]
    assert tokens == TREE_BLOCK and tree_parents.shape[1] == n_ctx and routes.shape[2] == 1
    assert n_ctx & (n_ctx - 1) == 0 and n_ctx > 1
    capacity = max(2, 5 * tokens // (4 * n_exp))
    slots = n_exp * capacity
    shifted = n_exp <= 8 and capacity % 8 == 0
    blocks_out = n_exp if shifted else 1
    half_width = width // KV_HEADS
    top = n_ctx // 2
    low_bits = [1 << b for b in range(top.bit_length() - 1)]
    half = ctx // top

    depth = expert_in.shape[1]
    inner = expert_out.shape[1]
    columns = expert_out.shape[2]
    route_row = routes.reshape(1, tokens)
    weight_row = route_weight.reshape(1, tokens)
    gain = norm_gain.reshape(1, width)


    shards = [lax.rem(ctx, top) ^ j for j in range(top)]
    row_at, col_at = 3, 3 + top
    meta = jnp.stack([half, ctx, exp] + [j * depth for j in shards] + [j * columns for j in shards])
    place, back, column, staged = plan(
        meta, route_row, weight_row, queries[0], n_exp, capacity, shifted
    )

    kv = jnp.concatenate([keys[0], values[0]], axis=1)
    near, far = [kv], [after(swap(kv, "ctx", n_ctx, top), place)]
    for bit in low_bits:
        near = near + [swap(x, "ctx", n_ctx, bit) for x in near]
        far = far + [swap(x, "ctx", n_ctx, bit) for x in far]
    kvs = near + far

    def spread(array):
        found = [array]
        for bit in low_bits:
            found = found + [swap(a, "ctx", n_ctx, bit) for a in found]
        return found

    def send(blocks, back, cross):
        if not shifted:
            whole = blocks[0].reshape(n_exp, capacity, half_width)
            whole = lax.all_to_all(whole, "exp", 0, 0, tiled=True).reshape(slots, half_width)
            return [swap(whole, "ctx", n_ctx, top) if cross else whole]
        moved = []
        for block, distance in zip(blocks, shifts(n_exp)):
            shift = (n_exp - distance) % n_exp if back else distance
            bit = top if cross else 0
            pairs = [
                (c * n_exp + e, (c ^ bit) * n_exp + (e + shift) % n_exp)
                for c in range(n_ctx)
                for e in range(n_exp)
            ]
            still = distance == 0 and not cross
            moved.append(block if still else lax.ppermute(block, ("ctx", "exp"), pairs))
        return moved

    def attend(queries, part):
        return attention(meta, tree_parents, queries, place, kvs, blocks_out, part)

    w_ins = [w.reshape(depth, 2 * inner) for w in spread(after(expert_in[0], *kvs[1:]))]
    att_b, packed_b = attend(staged, 1)
    rows_b = send(packed_b, False, True)
    att_a, packed_a = attend(after(staged, att_b, w_ins[-1]), 0)
    rows_b = [after(r, att_a) for r in rows_b]
    far_sums = products(meta, gain, rows_b, w_ins, row_at, slots, True)[0]
    rows_a = send(packed_a, False, False)
    far_sums = swap(far_sums, "ctx", n_ctx, top)
    w_outs = spread(after(expert_out[0], *rows_a))
    sums, squares = products(meta, gain, rows_a, w_ins, row_at, slots, False)
    hidden, out_a = finish(meta, sums, squares, far_sums, w_outs, col_at, width, blocks_out)
    back_a = send(out_a, True, False)
    out_b = down(meta, swap(hidden, "ctx", n_ctx, top), w_outs, col_at, width, blocks_out)
    back_b = send(out_b, True, True)
    done = combine(meta, att_a, back, column, back_a, None)
    done = combine(meta, att_b, back, column, back_b, done)
    return done[None]


def solution(mesh):
    in_specs = (
        P(("grp", "exp"), "ctx", None),
        P(("grp", "exp"), "ctx", None),
        P(("grp", "exp"), "ctx", None),
        P(("grp", "exp"), None),
        P(("grp", "exp"), "ctx", None),
        P(("grp", "exp"), "ctx", None),
        P(),
        P("exp", "ctx", None, None),
        P("exp", None, "ctx"),
    )
    out_specs = P(("grp", "exp"), "ctx", None)
    return jax.shard_map(body, mesh=mesh, in_specs=in_specs, out_specs=out_specs, check_vma=False)
```

```python
import functools
import math

import jax
import jax.numpy as jnp
from jax import lax
from jax.experimental import pallas as pl
from jax.experimental.pallas import tpu as pltpu
from jax.sharding import PartitionSpec as P

KV_HEADS = 2
HEAD_DIM = 128
TREE_BLOCK = 128
NEG = -1e30
MIB = 1024 * 1024
VMEM = pl.BlockSpec(memory_space=pltpu.VMEM)
SMEM = pl.BlockSpec(memory_space=pltpu.SMEM)


def call(kernel, name, args, specs, outs, scratch=(), mib=16, flops=1000, out_space=pltpu.VMEM):
    return pl.pallas_call(
        kernel,
        in_specs=specs,
        out_specs=[pl.BlockSpec(memory_space=out_space)] * len(outs),
        out_shape=[jax.ShapeDtypeStruct(s, d) for s, d in outs],
        scratch_shapes=list(scratch),
        compiler_params=pltpu.CompilerParams(vmem_limit_bytes=mib * MIB),
        cost_estimate=pl.CostEstimate(flops=flops, bytes_accessed=1000, transcendentals=0),
        name=name,
    )(*args)


def shifts(experts):
    return [experts // 2, 0] + [s for s in range(1, experts) if 2 * s != experts]


def placement_of(route_row, capacity, experts, first, relative):
    tokens = route_row.shape[1]
    if relative:
        shift = lax.rem(route_row - first + experts, experts)
        for i, s in enumerate(shifts(experts)):
            route_row = jnp.where(shift == s, i, route_row)
    rows = max(8, experts)
    expert_ids = lax.broadcasted_iota(jnp.int32, (rows, tokens), 0)
    hot = jnp.where(expert_ids == route_row, 1.0, 0.0)
    before = lax.broadcasted_iota(jnp.int32, (tokens, tokens), 0) < lax.broadcasted_iota(
        jnp.int32, (tokens, tokens), 1
    )
    earlier = jnp.dot(
        hot.astype(jnp.bfloat16),
        jnp.where(before, 1.0, 0.0).astype(jnp.bfloat16),
        preferred_element_type=jnp.float32,
    )
    rank = jnp.sum(earlier * hot, axis=0, keepdims=True).astype(jnp.int32)
    slot = route_row * capacity + rank
    slot_ids = lax.broadcasted_iota(jnp.int32, (experts * capacity, tokens), 0)
    return jnp.where(slot_ids == slot, 1.0, 0.0)


def start_copies(sources, targets, sems):
    copies = [
        pltpu.make_async_copy(s, t, sems.at[i]) for i, (s, t) in enumerate(zip(sources, targets))
    ]
    for copy in copies:
        copy.start()
    return copies


def plan_kernel(experts, capacity, relative, meta, route_hbm, weight_hbm, q_hbm, *refs):
    place_ref, back_ref, column_ref, q_ref, route_ref, weight_ref, sems = refs
    copies = start_copies((route_hbm, weight_hbm, q_hbm), (route_ref, weight_ref, q_ref), sems)
    tokens = route_ref.shape[1]
    copies[0].wait()
    place = placement_of(route_ref[...], capacity, experts, meta[2], relative)
    place_ref[...] = place.astype(jnp.bfloat16)
    back_ref[...] = place.T.astype(jnp.bfloat16)
    diagonal = lax.broadcasted_iota(jnp.int32, (tokens, tokens), 0) == lax.broadcasted_iota(
        jnp.int32, (tokens, tokens), 1
    )
    copies[1].wait()
    weight = jnp.sum(jnp.where(diagonal, weight_ref[...], 0.0), axis=1, keepdims=True)
    column_ref[...] = jnp.broadcast_to(weight, column_ref.shape)
    copies[2].wait()


def plan(meta, route_row, weight_row, queries, experts, capacity, relative):
    tokens = route_row.shape[1]
    slots = experts * capacity
    bf16 = jnp.bfloat16
    return call(
        functools.partial(plan_kernel, experts, capacity, relative),
        "plan",
        [meta, route_row, weight_row, queries],
        [SMEM] + [pl.BlockSpec(memory_space=pltpu.HBM)] * 3,
        [
            ((slots, tokens), bf16),
            ((tokens, slots), bf16),
            ((tokens, 128), jnp.float32),
            (queries.shape, bf16),
        ],
        [
            pltpu.VMEM(route_row.shape, route_row.dtype),
            pltpu.VMEM(weight_row.shape, weight_row.dtype),
            pltpu.SemaphoreType.DMA((3,)),
        ],
    )


def attention_kernel(n_ctx, half, parent_at, meta, q_ref, place_ref, *refs):
    kv = refs[:n_ctx]
    att_ref = refs[n_ctx]
    out_refs = refs[n_ctx + 1 :]
    tokens, half_width = att_ref.shape
    heads = half_width // HEAD_DIM
    side = meta[0] if half == 0 else 1 - meta[0]
    me = meta[1]
    reached = [jnp.int32(0)] * n_ctx
    current = me
    for _ in range(n_ctx):
        current = meta[parent_at + current]
        for j in range(1, n_ctx):
            reached[j] = jnp.where(current == (me ^ j), jnp.int32(1), reached[j])
    causal = lax.broadcasted_iota(jnp.int32, (tokens, tokens), 1) <= lax.broadcasted_iota(
        jnp.int32, (tokens, tokens), 0
    )
    key_at = pl.ds(pl.multiple_of(side * HEAD_DIM, HEAD_DIM), HEAD_DIM)
    value_at = pl.ds(pl.multiple_of((KV_HEADS + side) * HEAD_DIM, HEAD_DIM), HEAD_DIM)
    keys_t = jnp.concatenate([r[:, key_at] for r in kv], axis=0).T
    ones = jnp.ones((tokens, HEAD_DIM), jnp.bfloat16)
    values = jnp.concatenate(
        [jnp.concatenate([r[:, value_at], ones], axis=1) for r in kv], axis=0
    )
    bias = jnp.concatenate(
        [jnp.where(causal, 0.0, NEG)]
        + [
            jnp.broadcast_to(jnp.where(reached[j] == 1, 0.0, NEG), (tokens, tokens))
            for j in range(1, n_ctx)
        ],
        axis=1,
    )
    scale = math.log2(math.e) / math.sqrt(HEAD_DIM)
    for h in range(heads):
        columns = slice(h * HEAD_DIM, (h + 1) * HEAD_DIM)
        q_at = pl.ds(pl.multiple_of(side * half_width + h * HEAD_DIM, HEAD_DIM), HEAD_DIM)
        scores = jnp.dot(q_ref[:, q_at], keys_t, preferred_element_type=jnp.float32)
        scores = scores * scale + bias
        peak = jnp.max(scores, axis=1, keepdims=True)
        weights = jnp.exp2(scores - peak).astype(jnp.bfloat16)
        total = jnp.dot(weights, values, preferred_element_type=jnp.float32)
        att_ref[:, columns] = (total[:, :HEAD_DIM] / total[:, HEAD_DIM:]).astype(jnp.bfloat16)
    packed = jnp.dot(place_ref[...], att_ref[...], preferred_element_type=jnp.float32)
    for k, out in enumerate(out_refs):
        rows = out.shape[0]
        out[...] = packed[k * rows : (k + 1) * rows].astype(jnp.bfloat16)


def attention(meta, parent_at, queries, place, kvs, blocks_out, half):
    tokens, width = queries.shape
    half_width = width // KV_HEADS
    rows = place.shape[0] // blocks_out
    bf16 = jnp.bfloat16
    outs = call(
        functools.partial(attention_kernel, len(kvs), half, parent_at),
        "attend_" + "ab"[half],
        [meta, queries, place, *kvs],
        [SMEM] + [VMEM] * (2 + len(kvs)),
        [((tokens, half_width), bf16)] + [((rows, half_width), bf16)] * blocks_out,
        flops=2 * 10**9,
    )
    return outs[0], list(outs[1:])


def products_kernel(n_rows, n_weights, row_at, packed, meta, gain_ref, *refs):
    row_refs, w_refs, refs = refs[:n_rows], refs[n_rows : n_rows + n_weights], refs[n_rows + n_weights :]
    scaled = refs[-1]
    width = scaled.shape[1]
    gain = gain_ref[:, pl.ds(pl.multiple_of(meta[0] * width, width), width)]
    rows = jnp.concatenate([r[...].astype(jnp.float32) for r in row_refs], axis=0)
    scaled[...] = (rows * gain).astype(jnp.bfloat16)
    squares = jnp.sum(rows * rows, axis=1, keepdims=True)
    squares = jnp.broadcast_to(squares, (scaled.shape[0], 128))
    sums = None
    for i, w_ref in enumerate(w_refs):
        features = pl.ds(pl.multiple_of(meta[row_at + i], 128), w_ref.shape[0])
        part = jnp.dot(scaled[:, features], w_ref[...], preferred_element_type=jnp.float32)
        sums = part if sums is None else sums + part
    if packed:
        columns = sums.shape[1]
        refs[0][:, :columns] = sums.astype(jnp.bfloat16)
        high = squares.astype(jnp.bfloat16)
        low = (squares - high.astype(jnp.float32)).astype(jnp.bfloat16)
        lane = lax.broadcasted_iota(jnp.int32, squares.shape, 1)
        refs[0][:, columns:] = jnp.where(
            lane < 64, high.astype(jnp.float32), low.astype(jnp.float32)
        ).astype(jnp.bfloat16)
    else:
        refs[0][...] = sums
        refs[1][...] = squares


def products(meta, gain, rows, weights, row_at, packed):
    slots = sum(r.shape[0] for r in rows)
    half_width = rows[0].shape[1]
    columns = weights[0].shape[1]
    f32, bf16 = jnp.float32, jnp.bfloat16
    outs = [((slots, columns + 128), bf16)] if packed else [((slots, columns), f32), ((slots, 128), f32)]
    return call(
        functools.partial(products_kernel, len(rows), len(weights), row_at, packed),
        "products_" + "ab"[packed],
        [meta, gain, *rows, *weights],
        [SMEM] + [VMEM] * (1 + len(rows) + len(weights)),
        outs,
        [pltpu.VMEM((slots, half_width), bf16)],
        flops=20 * 10**9 if packed else 1000,
    )


def store_down(meta, col_at, w_refs, hidden, out_refs):
    for i, w_ref in enumerate(w_refs):
        value = jnp.dot(hidden, w_ref[...], preferred_element_type=jnp.float32)
        where = pl.ds(pl.multiple_of(meta[col_at + i], 128), w_ref.shape[1])
        height = value.shape[0] // len(out_refs)
        for k, out in enumerate(out_refs):
            out[:, where] = value[k * height : (k + 1) * height].astype(jnp.bfloat16)


def finish_kernel(n_far, n_weights, col_at, width, meta, sums_ref, squares_ref, *refs):
    far_refs, refs = refs[:n_far], refs[n_far:]
    w_refs, hidden_ref, out_refs = refs[:n_weights], refs[n_weights], refs[n_weights + 1 :]
    inner = hidden_ref.shape[1]
    start = 0
    for far_ref in far_refs:
        rows = slice(start, start + far_ref.shape[0])
        start = rows.stop
        squares = squares_ref[rows, :1]
        for at in (0, 64):
            squares = squares + far_ref[:, 2 * inner + at : 2 * inner + at + 1].astype(jnp.float32)
        factor = lax.rsqrt(squares * (1.0 / width) + 1e-06)
        gate = (sums_ref[rows, :inner] + far_ref[:, :inner].astype(jnp.float32)) * factor
        up = (sums_ref[rows, inner:] + far_ref[:, inner : 2 * inner].astype(jnp.float32)) * factor
        hidden_ref[rows] = (gate / (1.0 + jnp.exp(-gate)) * up).astype(jnp.bfloat16)
    store_down(meta, col_at, w_refs, hidden_ref[...], out_refs)


def finish(meta, sums, squares, far, weights, col_at, width, blocks_out):
    slots, columns = sums.shape
    bf16 = jnp.bfloat16
    outs = call(
        functools.partial(finish_kernel, len(far), len(weights), col_at, width),
        "hidden_down_a",
        [meta, sums, squares, *far, *weights],
        [SMEM] + [VMEM] * (2 + len(far) + len(weights)),
        [((slots, columns // 2), bf16)]
        + [((slots // blocks_out, width // KV_HEADS), bf16)] * blocks_out,
    )
    return outs[0], list(outs[1:])


def down_kernel(n_weights, col_at, meta, hidden_ref, *refs):
    store_down(meta, col_at, refs[:n_weights], hidden_ref[...], refs[n_weights:])


def down(meta, hidden, weights, col_at, width, blocks_out):
    outs = [((hidden.shape[0] // blocks_out, width // KV_HEADS), jnp.bfloat16)] * blocks_out
    return list(
        call(
            functools.partial(down_kernel, len(weights), col_at),
            "down_b",
            [meta, hidden, *weights],
            [SMEM] + [VMEM] * (1 + len(weights)),
            outs,
        )
    )


def combine_kernel(last, meta, att_ref, back_ref, column_ref, *refs):
    row_refs, refs = refs[: -1 - 3 * last], refs[-1 - 3 * last :]
    half_width = att_ref.shape[1]
    if last:
        before_ref, out_ref, value_ref, sems = refs
        before_at = pl.multiple_of(meta[0] * half_width, half_width)
        mine_at = pl.multiple_of((1 - meta[0]) * half_width, half_width)
        copies = [
            pltpu.make_async_copy(before_ref, out_ref.at[:, pl.ds(before_at, half_width)], sems.at[0])
        ]
        copies[0].start()
    rows = jnp.concatenate([r[...].astype(jnp.float32) for r in row_refs], axis=0)
    rows = rows.astype(jnp.bfloat16)
    parts = 4 if last else 1
    step = half_width // parts
    for i in range(parts):
        columns = slice(i * step, (i + 1) * step)
        mine = jnp.dot(back_ref[...], rows[:, columns], preferred_element_type=jnp.float32)
        value = att_ref[:, columns].astype(jnp.float32) + mine * column_ref[:, :1]
        value = value.astype(jnp.bfloat16)
        if last:
            value_ref[:, columns] = value
            place = out_ref.at[:, pl.ds(pl.multiple_of(mine_at + i * step, 128), step)]
            copies.append(
                pltpu.make_async_copy(value_ref.at[:, pl.ds(i * step, step)], place, sems.at[i + 1])
            )
            copies[-1].start()
        else:
            refs[0][:, columns] = value
    if last:
        for copy in copies:
            copy.wait()


def combine(meta, att, back, column, rows, before):
    tokens, half_width = att.shape
    last = before is not None
    extra = [before] if last else []
    scratch = [pltpu.VMEM(att.shape, att.dtype), pltpu.SemaphoreType.DMA((5,))] if last else []
    return call(
        functools.partial(combine_kernel, last),
        "combine_" + "ab"[last],
        [meta, att, back, column, *rows, *extra],
        [SMEM] + [VMEM] * (3 + len(rows) + len(extra)),
        [((tokens, half_width * (1 + last)), jnp.bfloat16)],
        scratch,
        flops=20 * 10**9,
        out_space=pl.ANY if last else pltpu.VMEM,
    )[0]


def swap(array, axis, size, bit):
    return lax.ppermute(array, axis, [(i, i ^ bit) for i in range(size)])


def after(array, *others):
    return lax.optimization_barrier((array, *others))[0]


def body(
    queries, keys, values, tree_parents, routes, route_weight, norm_gain, expert_in, expert_out
):
    n_ctx, n_exp = lax.axis_size("ctx"), lax.axis_size("exp")
    ctx, exp = lax.axis_index("ctx"), lax.axis_index("exp")
    tokens, width = queries.shape[1:]
    assert tokens == TREE_BLOCK and tree_parents.shape[1] == n_ctx and routes.shape[2] == 1
    assert n_ctx & (n_ctx - 1) == 0 and n_ctx > 1
    capacity = max(2, 5 * tokens // (4 * n_exp))
    slots = n_exp * capacity
    shifted = n_exp <= 8 and capacity % 8 == 0
    blocks_out = n_exp if shifted else 1
    half_width = width // KV_HEADS
    top = n_ctx // 2
    low_bits = [1 << b for b in range(top.bit_length() - 1)]
    half = ctx // top

    depth = expert_in.shape[1]
    inner = expert_out.shape[1]
    columns = expert_out.shape[2]
    route_row = routes.reshape(1, tokens)
    weight_row = route_weight.reshape(1, tokens)
    gain = norm_gain.reshape(1, width)


    shards = [lax.rem(ctx, top) ^ j for j in range(top)]
    row_at, col_at = 3, 3 + top
    parent_at = 3 + 2 * top
    meta = jnp.stack([half, ctx, exp] + [j * depth for j in shards] + [j * columns for j in shards])
    meta = jnp.concatenate([meta, tree_parents[0]])
    place, back, column, staged = plan(
        meta, route_row, weight_row, queries[0], n_exp, capacity, shifted
    )

    kv = jnp.concatenate([keys[0], values[0]], axis=1)
    near, far = [kv], [after(swap(kv, "ctx", n_ctx, top), place)]
    for bit in low_bits:
        near = near + [swap(x, "ctx", n_ctx, bit) for x in near]
        far = far + [swap(x, "ctx", n_ctx, bit) for x in far]
    kvs = near + far

    def spread(array):
        found = [array]
        for bit in low_bits:
            found = found + [swap(a, "ctx", n_ctx, bit) for a in found]
        return found

    def send(blocks, back, cross, gates={}):
        if not shifted:
            whole = blocks[0].reshape(n_exp, capacity, half_width)
            whole = lax.all_to_all(whole, "exp", 0, 0, tiled=True).reshape(slots, half_width)
            return [swap(whole, "ctx", n_ctx, top) if cross else whole]
        moved = []
        for block, distance in zip(blocks, shifts(n_exp)):
            shift = (n_exp - distance) % n_exp if back else distance
            bit = top if cross else 0
            pairs = [
                (c * n_exp + e, (c ^ bit) * n_exp + (e + shift) % n_exp)
                for c in range(n_ctx)
                for e in range(n_exp)
            ]
            still = distance == 0 and not cross
            if len(moved) in gates:
                block = after(block, *gates[len(moved)](moved))
            moved.append(block if still else lax.ppermute(block, ("ctx", "exp"), pairs))
        return moved

    def attend(queries, part):
        return attention(meta, parent_at, queries, place, kvs, blocks_out, part)

    w_raw = spread(after(expert_in[0], *kvs[1:]))
    att_b, packed_b = attend(staged, 1)
    rows_b = send(packed_b, False, True)
    w_ins = [after(w, att_b).reshape(depth, 2 * inner) for w in w_raw]
    w_outs = spread(after(expert_out[0], rows_b[0]))
    att_a, packed_a = attend(after(staged, att_b, rows_b[0], *w_ins), 0)
    rows_b = [after(r, att_a) for r in rows_b]
    rows_b[-1] = after(rows_b[-1], w_outs[-1])
    pair = len(rows_b) // 2 if len(rows_b) % 4 == 0 else len(rows_b)
    groups = [rows_b[i : i + pair] for i in range(0, len(rows_b), pair)]
    far_sums = [products(meta, gain, g, w_ins, row_at, True)[0] for g in groups]
    gates = {2: lambda m: [far_sums[0]], 3: lambda m: [m[0]]} if shifted else {}
    rows_a = send(packed_a, False, False, gates)
    made = far_sums[-1]
    far_sums = [swap(f, "ctx", n_ctx, top) for f in far_sums]
    out_a, hiddens, moved = [], [], []
    for i, far in enumerate(far_sums):
        rows = [after(r, made, *hiddens) for r in rows_a[i * pair : (i + 1) * pair]]
        sums, squares = products(meta, gain, rows, w_ins, row_at, False)
        sums = after(sums, *moved)
        hidden, blocks = finish(meta, sums, squares, [far], w_outs, col_at, width, len(rows))
        out_a += blocks
        hiddens.append(hidden)
        moved.append(swap(hidden, "ctx", n_ctx, top))
    back_a = send(out_a, True, False)
    out_b = []
    for hidden in moved:
        out_b += down(meta, hidden, w_outs, col_at, width, pair)
    back_b = send(out_b, True, True)
    done = combine(meta, att_a, back, column, back_a, None)
    done = combine(meta, att_b, back, column, back_b, done)
    return done[None]


def solution(mesh):
    in_specs = (
        P(("grp", "exp"), "ctx", None),
        P(("grp", "exp"), "ctx", None),
        P(("grp", "exp"), "ctx", None),
        P(("grp", "exp"), None),
        P(("grp", "exp"), "ctx", None),
        P(("grp", "exp"), "ctx", None),
        P(),
        P("exp", "ctx", None, None),
        P("exp", None, "ctx"),
    )
    out_specs = P(("grp", "exp"), "ctx", None)
    return jax.shard_map(body, mesh=mesh, in_specs=in_specs, out_specs=out_specs, check_vma=False)
```

```python
import functools
import math

import jax
import jax.numpy as jnp
from jax import lax
from jax.experimental import pallas as pl
from jax.experimental.pallas import tpu as pltpu
from jax.sharding import PartitionSpec as P

KV_HEADS = 2
HEAD_DIM = 128
TREE_BLOCK = 128
NEG = -1e30
MIB = 1024 * 1024
VMEM = pl.BlockSpec(memory_space=pltpu.VMEM)
SMEM = pl.BlockSpec(memory_space=pltpu.SMEM)


def call(kernel, name, args, specs, outs, scratch=(), mib=16, flops=1000, out_space=pltpu.VMEM):
    return pl.pallas_call(
        kernel,
        in_specs=specs,
        out_specs=[pl.BlockSpec(memory_space=out_space)] * len(outs),
        out_shape=[jax.ShapeDtypeStruct(s, d) for s, d in outs],
        scratch_shapes=list(scratch),
        compiler_params=pltpu.CompilerParams(vmem_limit_bytes=mib * MIB),
        cost_estimate=pl.CostEstimate(flops=flops, bytes_accessed=1000, transcendentals=0),
        name=name,
    )(*args)


def shifts(experts):
    return [experts // 2, 0] + [s for s in range(1, experts) if 2 * s != experts]


def placement_of(route_row, capacity, experts, first, relative):
    tokens = route_row.shape[1]
    if relative:
        shift = lax.rem(route_row - first + experts, experts)
        for i, s in enumerate(shifts(experts)):
            route_row = jnp.where(shift == s, i, route_row)
    rows = max(8, experts)
    expert_ids = lax.broadcasted_iota(jnp.int32, (rows, tokens), 0)
    hot = jnp.where(expert_ids == route_row, 1.0, 0.0)
    before = lax.broadcasted_iota(jnp.int32, (tokens, tokens), 0) < lax.broadcasted_iota(
        jnp.int32, (tokens, tokens), 1
    )
    earlier = jnp.dot(
        hot.astype(jnp.bfloat16),
        jnp.where(before, 1.0, 0.0).astype(jnp.bfloat16),
        preferred_element_type=jnp.float32,
    )
    rank = jnp.sum(earlier * hot, axis=0, keepdims=True).astype(jnp.int32)
    slot = route_row * capacity + rank
    slot_ids = lax.broadcasted_iota(jnp.int32, (experts * capacity, tokens), 0)
    return jnp.where(slot_ids == slot, 1.0, 0.0)


def plan_kernel(experts, capacity, relative, meta, route_ref, *refs):
    place_ref, back_ref = refs
    place = placement_of(route_ref[...], capacity, experts, meta[2], relative)
    place_ref[...] = place.astype(jnp.bfloat16)
    back_ref[...] = place.T.astype(jnp.bfloat16)


def plan(meta, route_row, experts, capacity, relative):
    tokens = route_row.shape[1]
    slots = experts * capacity
    bf16 = jnp.bfloat16
    return call(
        functools.partial(plan_kernel, experts, capacity, relative),
        "plan",
        [meta, route_row],
        [SMEM, VMEM],
        [((slots, tokens), bf16), ((tokens, slots), bf16)],
        flops=3 * 10**9,
    )


def attention_kernel(n_ctx, half, parent_at, meta, q_ref, place_ref, *refs):
    kv = refs[:n_ctx]
    att_ref = refs[n_ctx]
    out_refs = refs[n_ctx + 1 :]
    tokens, half_width = att_ref.shape
    heads = half_width // HEAD_DIM
    side = meta[0] if half == 0 else 1 - meta[0]
    me = meta[1]
    reached = [jnp.int32(0)] * n_ctx
    current = me
    for _ in range(n_ctx):
        current = meta[parent_at + current]
        for j in range(1, n_ctx):
            reached[j] = jnp.where(current == (me ^ j), jnp.int32(1), reached[j])
    causal = lax.broadcasted_iota(jnp.int32, (tokens, tokens), 1) <= lax.broadcasted_iota(
        jnp.int32, (tokens, tokens), 0
    )
    key_at = pl.ds(pl.multiple_of(side * HEAD_DIM, HEAD_DIM), HEAD_DIM)
    value_at = pl.ds(pl.multiple_of((KV_HEADS + side) * HEAD_DIM, HEAD_DIM), HEAD_DIM)
    keys_t = jnp.concatenate([r[:, key_at] for r in kv], axis=0).T
    ones = jnp.ones((tokens, HEAD_DIM), jnp.bfloat16)
    values = jnp.concatenate(
        [jnp.concatenate([r[:, value_at], ones], axis=1) for r in kv], axis=0
    )
    bias = jnp.concatenate(
        [jnp.where(causal, 0.0, NEG)]
        + [
            jnp.broadcast_to(jnp.where(reached[j] == 1, 0.0, NEG), (tokens, tokens))
            for j in range(1, n_ctx)
        ],
        axis=1,
    )
    scale = math.log2(math.e) / math.sqrt(HEAD_DIM)
    for h in range(heads):
        columns = slice(h * HEAD_DIM, (h + 1) * HEAD_DIM)
        q_at = pl.ds(pl.multiple_of(side * half_width + h * HEAD_DIM, HEAD_DIM), HEAD_DIM)
        scores = jnp.dot(q_ref[:, q_at], keys_t, preferred_element_type=jnp.float32)
        scores = scores * scale + bias
        peak = jnp.max(scores, axis=1, keepdims=True)
        weights = jnp.exp2(scores - peak).astype(jnp.bfloat16)
        total = jnp.dot(weights, values, preferred_element_type=jnp.float32)
        att_ref[:, columns] = (total[:, :HEAD_DIM] / total[:, HEAD_DIM:]).astype(jnp.bfloat16)
    packed = jnp.dot(place_ref[...], att_ref[...], preferred_element_type=jnp.float32)
    for k, out in enumerate(out_refs):
        rows = out.shape[0]
        out[...] = packed[k * rows : (k + 1) * rows].astype(jnp.bfloat16)


def attention(meta, parent_at, queries, place, kvs, blocks_out, half):
    tokens, width = queries.shape
    half_width = width // KV_HEADS
    rows = place.shape[0] // blocks_out
    bf16 = jnp.bfloat16
    outs = call(
        functools.partial(attention_kernel, len(kvs), half, parent_at),
        "attend_" + "ab"[half],
        [meta, queries, place, *kvs],
        [SMEM] + [VMEM] * (2 + len(kvs)),
        [((tokens, half_width), bf16)] + [((rows, half_width), bf16)] * blocks_out,
        flops=2 * 10**9,
    )
    return outs[0], list(outs[1:])


def products_kernel(n_rows, n_weights, row_at, packed, meta, gain_ref, *refs):
    row_refs, w_refs, refs = refs[:n_rows], refs[n_rows : n_rows + n_weights], refs[n_rows + n_weights :]
    scaled = refs[-1]
    width = scaled.shape[1]
    gain = gain_ref[:, pl.ds(pl.multiple_of(meta[0] * width, width), width)]
    rows = jnp.concatenate([r[...].astype(jnp.float32) for r in row_refs], axis=0)
    scaled[...] = (rows * gain).astype(jnp.bfloat16)
    squares = jnp.sum(rows * rows, axis=1, keepdims=True)
    squares = jnp.broadcast_to(squares, (scaled.shape[0], 128))
    sums = None
    for i, w_ref in enumerate(w_refs):
        features = pl.ds(pl.multiple_of(meta[row_at + i], 128), w_ref.shape[0])
        part = jnp.dot(scaled[:, features], w_ref[...], preferred_element_type=jnp.float32)
        sums = part if sums is None else sums + part
    if packed:
        columns = sums.shape[1]
        refs[0][:, :columns] = sums.astype(jnp.bfloat16)
        high = squares.astype(jnp.bfloat16)
        low = (squares - high.astype(jnp.float32)).astype(jnp.bfloat16)
        lane = lax.broadcasted_iota(jnp.int32, squares.shape, 1)
        refs[0][:, columns:] = jnp.where(
            lane < 64, high.astype(jnp.float32), low.astype(jnp.float32)
        ).astype(jnp.bfloat16)
    else:
        refs[0][...] = sums
        refs[1][...] = squares


def products(meta, gain, rows, weights, row_at, packed):
    slots = sum(r.shape[0] for r in rows)
    half_width = rows[0].shape[1]
    columns = weights[0].shape[1]
    f32, bf16 = jnp.float32, jnp.bfloat16
    outs = [((slots, columns + 128), bf16)] if packed else [((slots, columns), f32), ((slots, 128), f32)]
    return call(
        functools.partial(products_kernel, len(rows), len(weights), row_at, packed),
        "products_" + "ab"[packed],
        [meta, gain, *rows, *weights],
        [SMEM] + [VMEM] * (1 + len(rows) + len(weights)),
        outs,
        [pltpu.VMEM((slots, half_width), bf16)],
        flops=20 * 10**9 if packed else 1000,
    )


def store_down(meta, col_at, w_refs, hidden, out_refs):
    for i, w_ref in enumerate(w_refs):
        value = jnp.dot(hidden, w_ref[...], preferred_element_type=jnp.float32)
        where = pl.ds(pl.multiple_of(meta[col_at + i], 128), w_ref.shape[1])
        height = value.shape[0] // len(out_refs)
        for k, out in enumerate(out_refs):
            out[:, where] = value[k * height : (k + 1) * height].astype(jnp.bfloat16)


def finish_kernel(n_far, n_weights, col_at, width, meta, sums_ref, squares_ref, *refs):
    far_refs, refs = refs[:n_far], refs[n_far:]
    w_refs, hidden_ref, out_refs = refs[:n_weights], refs[n_weights], refs[n_weights + 1 :]
    inner = hidden_ref.shape[1]
    start = 0
    for far_ref in far_refs:
        rows = slice(start, start + far_ref.shape[0])
        start = rows.stop
        squares = squares_ref[rows, :1]
        for at in (0, 64):
            squares = squares + far_ref[:, 2 * inner + at : 2 * inner + at + 1].astype(jnp.float32)
        factor = lax.rsqrt(squares * (1.0 / width) + 1e-06)
        gate = (sums_ref[rows, :inner] + far_ref[:, :inner].astype(jnp.float32)) * factor
        up = (sums_ref[rows, inner:] + far_ref[:, inner : 2 * inner].astype(jnp.float32)) * factor
        hidden_ref[rows] = (gate / (1.0 + jnp.exp(-gate)) * up).astype(jnp.bfloat16)
    store_down(meta, col_at, w_refs, hidden_ref[...], out_refs)


def finish(meta, sums, squares, far, weights, col_at, width, blocks_out):
    slots, columns = sums.shape
    bf16 = jnp.bfloat16
    outs = call(
        functools.partial(finish_kernel, len(far), len(weights), col_at, width),
        "hidden_down_a",
        [meta, sums, squares, *far, *weights],
        [SMEM] + [VMEM] * (2 + len(far) + len(weights)),
        [((slots, columns // 2), bf16)]
        + [((slots // blocks_out, width // KV_HEADS), bf16)] * blocks_out,
    )
    return outs[0], list(outs[1:])


def down_kernel(n_weights, col_at, meta, hidden_ref, *refs):
    store_down(meta, col_at, refs[:n_weights], hidden_ref[...], refs[n_weights:])


def down(meta, hidden, weights, col_at, width, blocks_out):
    outs = [((hidden.shape[0] // blocks_out, width // KV_HEADS), jnp.bfloat16)] * blocks_out
    return list(
        call(
            functools.partial(down_kernel, len(weights), col_at),
            "down_b",
            [meta, hidden, *weights],
            [SMEM] + [VMEM] * (1 + len(weights)),
            outs,
        )
    )


def combine_kernel(last, meta, att_ref, back_ref, weight_ref, *refs):
    row_refs, refs = refs[: -2 - 2 * last], refs[-2 - 2 * last :]
    tokens, half_width = att_ref.shape
    if last:
        before_ref, out_ref, value_ref, sems = refs
        before_at = pl.multiple_of(meta[0] * half_width, half_width)
        mine_at = pl.multiple_of((1 - meta[0]) * half_width, half_width)
        copies = [
            pltpu.make_async_copy(before_ref, out_ref.at[:, pl.ds(before_at, half_width)], sems.at[0])
        ]
        copies[0].start()
        weight = weight_ref[:, :1]
    else:
        diagonal = lax.broadcasted_iota(jnp.int32, (tokens, tokens), 0) == lax.broadcasted_iota(
            jnp.int32, (tokens, tokens), 1
        )
        weight = jnp.sum(jnp.where(diagonal, weight_ref[...], 0.0), axis=1, keepdims=True)
        refs[1][...] = jnp.broadcast_to(weight, refs[1].shape)
    rows = jnp.concatenate([r[...].astype(jnp.float32) for r in row_refs], axis=0)
    rows = rows.astype(jnp.bfloat16)
    parts = 4 if last else 1
    step = half_width // parts
    for i in range(parts):
        columns = slice(i * step, (i + 1) * step)
        mine = jnp.dot(back_ref[...], rows[:, columns], preferred_element_type=jnp.float32)
        value = att_ref[:, columns].astype(jnp.float32) + mine * weight
        value = value.astype(jnp.bfloat16)
        if last:
            value_ref[:, columns] = value
            place = out_ref.at[:, pl.ds(pl.multiple_of(mine_at + i * step, 128), step)]
            copies.append(
                pltpu.make_async_copy(value_ref.at[:, pl.ds(i * step, step)], place, sems.at[i + 1])
            )
            copies[-1].start()
        else:
            refs[0][:, columns] = value
    if last:
        for copy in copies:
            copy.wait()


def combine(meta, att, back, weight, rows, before):
    tokens, half_width = att.shape
    last = before is not None
    extra = [before] if last else []
    if last:
        outs = [((tokens, KV_HEADS * half_width), jnp.bfloat16)]
    else:
        outs = [((tokens, half_width), jnp.bfloat16), ((tokens, 128), jnp.float32)]
    scratch = [pltpu.VMEM(att.shape, att.dtype), pltpu.SemaphoreType.DMA((5,))] if last else []
    return call(
        functools.partial(combine_kernel, last),
        "combine_" + "ab"[last],
        [meta, att, back, weight, *rows, *extra],
        [SMEM] + [VMEM] * (3 + len(rows) + len(extra)),
        outs,
        scratch,
        flops=20 * 10**9,
        out_space=pl.ANY if last else pltpu.VMEM,
    )


def swap(array, axis, size, bit):
    return lax.ppermute(array, axis, [(i, i ^ bit) for i in range(size)])


def after(array, *others):
    return lax.optimization_barrier((array, *others))[0]


def body(
    queries, keys, values, tree_parents, routes, route_weight, norm_gain, expert_in, expert_out
):
    n_ctx, n_exp = lax.axis_size("ctx"), lax.axis_size("exp")
    ctx, exp = lax.axis_index("ctx"), lax.axis_index("exp")
    tokens, width = queries.shape[1:]
    assert tokens == TREE_BLOCK and tree_parents.shape[1] == n_ctx and routes.shape[2] == 1
    assert n_ctx & (n_ctx - 1) == 0 and n_ctx > 1
    capacity = max(2, 5 * tokens // (4 * n_exp))
    slots = n_exp * capacity
    shifted = n_exp <= 8 and capacity % 8 == 0
    blocks_out = n_exp if shifted else 1
    half_width = width // KV_HEADS
    top = n_ctx // 2
    low_bits = [1 << b for b in range(top.bit_length() - 1)]
    half = ctx // top

    depth = expert_in.shape[1]
    inner = expert_out.shape[1]
    columns = expert_out.shape[2]
    route_row = routes.reshape(1, tokens)
    weight_row = route_weight.reshape(1, tokens)
    gain = norm_gain.reshape(1, width)


    shards = [lax.rem(ctx, top) ^ j for j in range(top)]
    row_at, col_at = 3, 3 + top
    parent_at = 3 + 2 * top
    meta = jnp.stack([half, ctx, exp] + [j * depth for j in shards] + [j * columns for j in shards])
    meta = jnp.concatenate([meta, tree_parents[0]])
    place, back = plan(meta, route_row, n_exp, capacity, shifted)
    staged = queries[0]

    kv = jnp.concatenate([keys[0], values[0]], axis=1)
    near, far = [kv], [after(swap(kv, "ctx", n_ctx, top), place)]
    for bit in low_bits:
        near = near + [swap(x, "ctx", n_ctx, bit) for x in near]
        far = far + [swap(x, "ctx", n_ctx, bit) for x in far]
    kvs = near + far

    def spread(array):
        found = [array]
        for bit in low_bits:
            found = found + [swap(a, "ctx", n_ctx, bit) for a in found]
        return found

    def send(blocks, back, cross, gates={}):
        if not shifted:
            whole = blocks[0].reshape(n_exp, capacity, half_width)
            whole = lax.all_to_all(whole, "exp", 0, 0, tiled=True).reshape(slots, half_width)
            return [swap(whole, "ctx", n_ctx, top) if cross else whole]
        moved = []
        for block, distance in zip(blocks, shifts(n_exp)):
            shift = (n_exp - distance) % n_exp if back else distance
            bit = top if cross else 0
            pairs = [
                (c * n_exp + e, (c ^ bit) * n_exp + (e + shift) % n_exp)
                for c in range(n_ctx)
                for e in range(n_exp)
            ]
            still = distance == 0 and not cross
            if len(moved) in gates:
                block = after(block, *gates[len(moved)](moved))
            moved.append(block if still else lax.ppermute(block, ("ctx", "exp"), pairs))
        return moved

    def attend(queries, part):
        return attention(meta, parent_at, queries, place, kvs, blocks_out, part)

    w_raw = spread(after(expert_in[0], *kvs[1:]))
    att_b, packed_b = attend(staged, 1)
    rows_b = send(packed_b, False, True)
    w_ins = [after(w, att_b).reshape(depth, 2 * inner) for w in w_raw]
    w_outs = spread(after(expert_out[0], rows_b[0]))
    att_a, packed_a = attend(after(staged, att_b, rows_b[0], *w_ins), 0)
    rows_b = [after(r, att_a) for r in rows_b]
    rows_b[-1] = after(rows_b[-1], w_outs[-1])
    pair = len(rows_b) // 2 if len(rows_b) % 4 == 0 else len(rows_b)
    groups = [rows_b[i : i + pair] for i in range(0, len(rows_b), pair)]
    far_sums = [products(meta, gain, g, w_ins, row_at, True)[0] for g in groups]
    gates = {2: lambda m: [far_sums[0]], 3: lambda m: [m[0]]} if shifted else {}
    rows_a = send(packed_a, False, False, gates)
    made = far_sums[-1]
    far_sums = [swap(f, "ctx", n_ctx, top) for f in far_sums]
    out_a, hiddens, moved = [], [], []
    for i, far in enumerate(far_sums):
        rows = [after(r, made, *hiddens) for r in rows_a[i * pair : (i + 1) * pair]]
        sums, squares = products(meta, gain, rows, w_ins, row_at, False)
        sums = after(sums, *moved)
        hidden, blocks = finish(meta, sums, squares, [far], w_outs, col_at, width, len(rows))
        out_a += blocks
        hiddens.append(hidden)
        moved.append(swap(hidden, "ctx", n_ctx, top))
    back_a = send(out_a, True, False)
    out_b = []
    for hidden in moved:
        out_b += down(meta, hidden, w_outs, col_at, width, pair)
    back_b = send(out_b, True, True)
    done, column = combine(meta, att_a, back, weight_row, back_a, None)
    done = combine(meta, att_b, back, column, back_b, done)[0]
    return done[None]


def solution(mesh):
    in_specs = (
        P(("grp", "exp"), "ctx", None),
        P(("grp", "exp"), "ctx", None),
        P(("grp", "exp"), "ctx", None),
        P(("grp", "exp"), None),
        P(("grp", "exp"), "ctx", None),
        P(("grp", "exp"), "ctx", None),
        P(),
        P("exp", "ctx", None, None),
        P("exp", None, "ctx"),
    )
    out_specs = P(("grp", "exp"), "ctx", None)
    return jax.shard_map(body, mesh=mesh, in_specs=in_specs, out_specs=out_specs, check_vma=False)
```

```python
import functools
import math

import jax
import jax.numpy as jnp
from jax import lax
from jax.experimental import pallas as pl
from jax.experimental.pallas import tpu as pltpu
from jax.sharding import PartitionSpec as P

KV_HEADS = 2
HEAD_DIM = 128
TREE_BLOCK = 128
NEG = -1e30
MIB = 1024 * 1024
VMEM = pl.BlockSpec(memory_space=pltpu.VMEM)
SMEM = pl.BlockSpec(memory_space=pltpu.SMEM)


def call(kernel, name, args, specs, outs, scratch=(), mib=16, flops=1000, out_space=pltpu.VMEM):
    return pl.pallas_call(
        kernel,
        in_specs=specs,
        out_specs=[pl.BlockSpec(memory_space=out_space)] * len(outs),
        out_shape=[jax.ShapeDtypeStruct(s, d) for s, d in outs],
        scratch_shapes=list(scratch),
        compiler_params=pltpu.CompilerParams(vmem_limit_bytes=mib * MIB),
        cost_estimate=pl.CostEstimate(flops=flops, bytes_accessed=1000, transcendentals=0),
        name=name,
    )(*args)


def shifts(experts):
    return [experts // 2, 0] + [s for s in range(1, experts) if 2 * s != experts]


def placement_of(route_row, capacity, experts, first, relative):
    tokens = route_row.shape[1]
    if relative:
        shift = lax.rem(route_row - first + experts, experts)
        for i, s in enumerate(shifts(experts)):
            route_row = jnp.where(shift == s, i, route_row)
    rows = max(8, experts)
    expert_ids = lax.broadcasted_iota(jnp.int32, (rows, tokens), 0)
    hot = jnp.where(expert_ids == route_row, 1.0, 0.0)
    before = lax.broadcasted_iota(jnp.int32, (tokens, tokens), 0) < lax.broadcasted_iota(
        jnp.int32, (tokens, tokens), 1
    )
    earlier = jnp.dot(
        hot.astype(jnp.bfloat16),
        jnp.where(before, 1.0, 0.0).astype(jnp.bfloat16),
        preferred_element_type=jnp.float32,
    )
    rank = jnp.sum(earlier * hot, axis=0, keepdims=True).astype(jnp.int32)
    slot = route_row * capacity + rank
    slot_ids = lax.broadcasted_iota(jnp.int32, (experts * capacity, tokens), 0)
    return jnp.where(slot_ids == slot, 1.0, 0.0)


def plan_kernel(experts, capacity, relative, meta, route_ref, *refs):
    place_ref, back_ref = refs
    place = placement_of(route_ref[...], capacity, experts, meta[2], relative)
    place_ref[...] = place.astype(jnp.bfloat16)
    back_ref[...] = place.T.astype(jnp.bfloat16)


def plan(meta, route_row, experts, capacity, relative):
    tokens = route_row.shape[1]
    slots = experts * capacity
    bf16 = jnp.bfloat16
    return call(
        functools.partial(plan_kernel, experts, capacity, relative),
        "plan",
        [meta, route_row],
        [SMEM, VMEM],
        [((slots, tokens), bf16), ((tokens, slots), bf16)],
        flops=3 * 10**9,
    )


def attention_kernel(n_ctx, half, parent_at, meta, q_ref, place_ref, *refs):
    kv = refs[:n_ctx]
    att_ref = refs[n_ctx]
    out_refs = refs[n_ctx + 1 :]
    tokens, half_width = att_ref.shape
    heads = half_width // HEAD_DIM
    side = meta[0] if half == 0 else 1 - meta[0]
    me = meta[1]
    reached = [jnp.int32(0)] * n_ctx
    current = me
    for _ in range(n_ctx):
        current = meta[parent_at + current]
        for j in range(1, n_ctx):
            reached[j] = jnp.where(current == (me ^ j), jnp.int32(1), reached[j])
    causal = lax.broadcasted_iota(jnp.int32, (tokens, tokens), 1) <= lax.broadcasted_iota(
        jnp.int32, (tokens, tokens), 0
    )
    key_at = pl.ds(pl.multiple_of(side * HEAD_DIM, HEAD_DIM), HEAD_DIM)
    value_at = pl.ds(pl.multiple_of((KV_HEADS + side) * HEAD_DIM, HEAD_DIM), HEAD_DIM)
    keys_t = jnp.concatenate([r[:, key_at] for r in kv], axis=0).T
    ones = jnp.ones((tokens, HEAD_DIM), jnp.bfloat16)
    values = jnp.concatenate(
        [jnp.concatenate([r[:, value_at], ones], axis=1) for r in kv], axis=0
    )
    bias = jnp.concatenate(
        [jnp.where(causal, 0.0, NEG)]
        + [
            jnp.broadcast_to(jnp.where(reached[j] == 1, 0.0, NEG), (tokens, tokens))
            for j in range(1, n_ctx)
        ],
        axis=1,
    )
    scale = math.log2(math.e) / math.sqrt(HEAD_DIM)
    for h in range(heads):
        columns = slice(h * HEAD_DIM, (h + 1) * HEAD_DIM)
        q_at = pl.ds(pl.multiple_of(side * half_width + h * HEAD_DIM, HEAD_DIM), HEAD_DIM)
        scores = jnp.dot(q_ref[:, q_at], keys_t, preferred_element_type=jnp.float32)
        scores = scores * scale + bias
        peak = jnp.max(scores, axis=1, keepdims=True)
        weights = jnp.exp2(scores - peak).astype(jnp.bfloat16)
        total = jnp.dot(weights, values, preferred_element_type=jnp.float32)
        att_ref[:, columns] = (total[:, :HEAD_DIM] / total[:, HEAD_DIM:]).astype(jnp.bfloat16)
    packed = jnp.dot(place_ref[...], att_ref[...], preferred_element_type=jnp.float32)
    for k, out in enumerate(out_refs):
        rows = out.shape[0]
        out[...] = packed[k * rows : (k + 1) * rows].astype(jnp.bfloat16)


def attention(meta, parent_at, queries, place, kvs, blocks_out, half):
    tokens, width = queries.shape
    half_width = width // KV_HEADS
    rows = place.shape[0] // blocks_out
    bf16 = jnp.bfloat16
    outs = call(
        functools.partial(attention_kernel, len(kvs), half, parent_at),
        "attend_" + "ab"[half],
        [meta, queries, place, *kvs],
        [SMEM] + [VMEM] * (2 + len(kvs)),
        [((tokens, half_width), bf16)] + [((rows, half_width), bf16)] * blocks_out,
        flops=2 * 10**9,
    )
    return outs[0], list(outs[1:])


def products_kernel(n_rows, n_weights, row_at, packed, meta, gain_ref, *refs):
    row_refs, w_refs, refs = refs[:n_rows], refs[n_rows : n_rows + n_weights], refs[n_rows + n_weights :]
    scaled = refs[-1]
    width = scaled.shape[1]
    gain = gain_ref[:, pl.ds(pl.multiple_of(meta[0] * width, width), width)]
    rows = jnp.concatenate([r[...].astype(jnp.float32) for r in row_refs], axis=0)
    scaled[...] = (rows * gain).astype(jnp.bfloat16)
    squares = jnp.sum(rows * rows, axis=1, keepdims=True)
    squares = jnp.broadcast_to(squares, (scaled.shape[0], 128))
    sums = None
    for i, w_ref in enumerate(w_refs):
        features = pl.ds(pl.multiple_of(meta[row_at + i], 128), w_ref.shape[0])
        part = jnp.dot(scaled[:, features], w_ref[...], preferred_element_type=jnp.float32)
        sums = part if sums is None else sums + part
    if packed:
        columns = sums.shape[1]
        refs[0][:, :columns] = sums.astype(jnp.bfloat16)
        high = squares.astype(jnp.bfloat16)
        low = (squares - high.astype(jnp.float32)).astype(jnp.bfloat16)
        lane = lax.broadcasted_iota(jnp.int32, squares.shape, 1)
        refs[0][:, columns:] = jnp.where(
            lane < 64, high.astype(jnp.float32), low.astype(jnp.float32)
        ).astype(jnp.bfloat16)
    else:
        refs[0][...] = sums
        refs[1][...] = squares


def products(meta, gain, rows, weights, row_at, packed):
    slots = sum(r.shape[0] for r in rows)
    half_width = rows[0].shape[1]
    columns = weights[0].shape[1]
    f32, bf16 = jnp.float32, jnp.bfloat16
    outs = [((slots, columns + 128), bf16)] if packed else [((slots, columns), f32), ((slots, 128), f32)]
    return call(
        functools.partial(products_kernel, len(rows), len(weights), row_at, packed),
        "products_" + "ab"[packed],
        [meta, gain, *rows, *weights],
        [SMEM] + [VMEM] * (1 + len(rows) + len(weights)),
        outs,
        [pltpu.VMEM((slots, half_width), bf16)],
        flops=20 * 10**9 if packed else 1000,
    )


def store_down(meta, col_at, w_refs, hidden, out_refs):
    for i, w_ref in enumerate(w_refs):
        value = jnp.dot(hidden, w_ref[...], preferred_element_type=jnp.float32)
        where = pl.ds(pl.multiple_of(meta[col_at + i], 128), w_ref.shape[1])
        height = value.shape[0] // len(out_refs)
        for k, out in enumerate(out_refs):
            out[:, where] = value[k * height : (k + 1) * height].astype(jnp.bfloat16)


def finish_kernel(n_far, n_weights, col_at, width, meta, sums_ref, squares_ref, *refs):
    far_refs, refs = refs[:n_far], refs[n_far:]
    w_refs, hidden_ref, out_refs = refs[:n_weights], refs[n_weights], refs[n_weights + 1 :]
    inner = hidden_ref.shape[1]
    start = 0
    for far_ref in far_refs:
        rows = slice(start, start + far_ref.shape[0])
        start = rows.stop
        squares = squares_ref[rows, :1]
        for at in (0, 64):
            squares = squares + far_ref[:, 2 * inner + at : 2 * inner + at + 1].astype(jnp.float32)
        factor = lax.rsqrt(squares * (1.0 / width) + 1e-06)
        gate = (sums_ref[rows, :inner] + far_ref[:, :inner].astype(jnp.float32)) * factor
        up = (sums_ref[rows, inner:] + far_ref[:, inner : 2 * inner].astype(jnp.float32)) * factor
        hidden_ref[rows] = (gate / (1.0 + jnp.exp(-gate)) * up).astype(jnp.bfloat16)
    store_down(meta, col_at, w_refs, hidden_ref[...], out_refs)


def finish(meta, sums, squares, far, weights, col_at, width, blocks_out):
    slots, columns = sums.shape
    bf16 = jnp.bfloat16
    outs = call(
        functools.partial(finish_kernel, len(far), len(weights), col_at, width),
        "hidden_down_a",
        [meta, sums, squares, *far, *weights],
        [SMEM] + [VMEM] * (2 + len(far) + len(weights)),
        [((slots, columns // 2), bf16)]
        + [((slots // blocks_out, width // KV_HEADS), bf16)] * blocks_out,
    )
    return outs[0], list(outs[1:])


def down_kernel(n_weights, col_at, meta, hidden_ref, *refs):
    store_down(meta, col_at, refs[:n_weights], hidden_ref[...], refs[n_weights:])


def down(meta, hidden, weights, col_at, width, blocks_out):
    outs = [((hidden.shape[0] // blocks_out, width // KV_HEADS), jnp.bfloat16)] * blocks_out
    return list(
        call(
            functools.partial(down_kernel, len(weights), col_at),
            "down_b",
            [meta, hidden, *weights],
            [SMEM] + [VMEM] * (1 + len(weights)),
            outs,
        )
    )


def combine_kernel(last, meta, att_ref, back_ref, weight_ref, *refs):
    row_refs, refs = refs[: -2 - 2 * last], refs[-2 - 2 * last :]
    tokens, half_width = att_ref.shape
    if last:
        before_ref, out_ref, value_ref, sems = refs
        before_at = pl.multiple_of(meta[0] * half_width, half_width)
        mine_at = pl.multiple_of((1 - meta[0]) * half_width, half_width)
        copies = [
            pltpu.make_async_copy(before_ref, out_ref.at[:, pl.ds(before_at, half_width)], sems.at[0])
        ]
        copies[0].start()
        weight = weight_ref[:, :1]
    else:
        diagonal = lax.broadcasted_iota(jnp.int32, (tokens, tokens), 0) == lax.broadcasted_iota(
            jnp.int32, (tokens, tokens), 1
        )
        weight = jnp.sum(jnp.where(diagonal, weight_ref[...], 0.0), axis=1, keepdims=True)
        refs[1][...] = jnp.broadcast_to(weight, refs[1].shape)
    rows = jnp.concatenate([r[...].astype(jnp.float32) for r in row_refs], axis=0)
    rows = rows.astype(jnp.bfloat16)
    parts = 4 if last else 1
    step = half_width // parts
    for i in range(parts):
        columns = slice(i * step, (i + 1) * step)
        mine = jnp.dot(back_ref[...], rows[:, columns], preferred_element_type=jnp.float32)
        value = att_ref[:, columns].astype(jnp.float32) + mine * weight
        value = value.astype(jnp.bfloat16)
        if last:
            value_ref[:, columns] = value
            place = out_ref.at[:, pl.ds(pl.multiple_of(mine_at + i * step, 128), step)]
            copies.append(
                pltpu.make_async_copy(value_ref.at[:, pl.ds(i * step, step)], place, sems.at[i + 1])
            )
            copies[-1].start()
        else:
            refs[0][:, columns] = value
    if last:
        for copy in copies:
            copy.wait()


def combine(meta, att, back, weight, rows, before):
    tokens, half_width = att.shape
    last = before is not None
    extra = [before] if last else []
    if last:
        outs = [((tokens, KV_HEADS * half_width), jnp.bfloat16)]
    else:
        outs = [((tokens, half_width), jnp.bfloat16), ((tokens, 128), jnp.float32)]
    scratch = [pltpu.VMEM(att.shape, att.dtype), pltpu.SemaphoreType.DMA((5,))] if last else []
    return call(
        functools.partial(combine_kernel, last),
        "combine_" + "ab"[last],
        [meta, att, back, weight, *rows, *extra],
        [SMEM] + [VMEM] * (3 + len(rows) + len(extra)),
        outs,
        scratch,
        flops=20 * 10**9,
        out_space=pl.ANY if last else pltpu.VMEM,
    )


def swap(array, axis, size, bit):
    return lax.ppermute(array, axis, [(i, i ^ bit) for i in range(size)])


def after(array, *others):
    return lax.optimization_barrier((array, *others))[0]


def body(
    queries, keys, values, tree_parents, routes, route_weight, norm_gain, expert_in, expert_out
):
    n_ctx, n_exp = lax.axis_size("ctx"), lax.axis_size("exp")
    ctx, exp = lax.axis_index("ctx"), lax.axis_index("exp")
    tokens, width = queries.shape[1:]
    assert tokens == TREE_BLOCK and tree_parents.shape[1] == n_ctx and routes.shape[2] == 1
    assert n_ctx & (n_ctx - 1) == 0 and n_ctx > 1
    capacity = max(2, 5 * tokens // (4 * n_exp))
    slots = n_exp * capacity
    shifted = n_exp <= 8 and capacity % 8 == 0
    blocks_out = n_exp if shifted else 1
    half_width = width // KV_HEADS
    top = n_ctx // 2
    low_bits = [1 << b for b in range(top.bit_length() - 1)]
    half = ctx // top

    depth = expert_in.shape[1]
    inner = expert_out.shape[1]
    columns = expert_out.shape[2]
    route_row = routes.reshape(1, tokens)
    weight_row = route_weight.reshape(1, tokens)
    gain = norm_gain.reshape(1, width)

    shards = [lax.rem(ctx, top) ^ j for j in range(top)]
    row_at, col_at = 3, 3 + top
    parent_at = 3 + 2 * top
    meta = jnp.stack([half, ctx, exp] + [j * depth for j in shards] + [j * columns for j in shards])
    meta = jnp.concatenate([meta, tree_parents[0]])
    place, back = plan(meta, route_row, n_exp, capacity, shifted)

    kv = jnp.concatenate([keys[0], values[0]], axis=1)
    near, far = [kv], [after(swap(kv, "ctx", n_ctx, top), place)]
    for bit in low_bits:
        near = near + [swap(x, "ctx", n_ctx, bit) for x in near]
        far = far + [swap(x, "ctx", n_ctx, bit) for x in far]
    kvs = near + far

    def spread(array):
        found = [array]
        for bit in low_bits:
            found = found + [swap(a, "ctx", n_ctx, bit) for a in found]
        return found

    def send(blocks, back, cross, gates={}):
        if not shifted:
            whole = blocks[0].reshape(n_exp, capacity, half_width)
            whole = lax.all_to_all(whole, "exp", 0, 0, tiled=True).reshape(slots, half_width)
            return [swap(whole, "ctx", n_ctx, top) if cross else whole]
        moved = []
        for block, distance in zip(blocks, shifts(n_exp)):
            shift = (n_exp - distance) % n_exp if back else distance
            bit = top if cross else 0
            pairs = [
                (c * n_exp + e, (c ^ bit) * n_exp + (e + shift) % n_exp)
                for c in range(n_ctx)
                for e in range(n_exp)
            ]
            still = distance == 0 and not cross
            if len(moved) in gates:
                block = after(block, *gates[len(moved)](moved))
            moved.append(block if still else lax.ppermute(block, ("ctx", "exp"), pairs))
        return moved

    def attend(queries, part):
        return attention(meta, parent_at, queries, place, kvs, blocks_out, part)

    w_raw = spread(after(expert_in[0], *kvs[1:]))
    att_b, packed_b = attend(queries[0], 1)
    rows_b = send(packed_b, False, True)
    w_ins = [after(w, att_b).reshape(depth, 2 * inner) for w in w_raw]
    w_outs = spread(after(expert_out[0], rows_b[0]))
    att_a, packed_a = attend(after(queries[0], att_b, rows_b[0], *w_ins), 0)
    rows_b = [after(r, att_a) for r in rows_b]
    rows_b[-1] = after(rows_b[-1], w_outs[-1])
    pair = len(rows_b) // 2 if len(rows_b) % 4 == 0 else len(rows_b)
    groups = [rows_b[i : i + pair] for i in range(0, len(rows_b), pair)]
    far_sums = [products(meta, gain, g, w_ins, row_at, True)[0] for g in groups]
    gates = {2: lambda m: [far_sums[0]], 3: lambda m: [m[0]]} if shifted else {}
    rows_a = send(packed_a, False, False, gates)
    made = far_sums[-1]
    far_sums = [swap(f, "ctx", n_ctx, top) for f in far_sums]
    out_a, hiddens, moved = [], [], []
    for i, far in enumerate(far_sums):
        rows = [after(r, made, *hiddens) for r in rows_a[i * pair : (i + 1) * pair]]
        sums, squares = products(meta, gain, rows, w_ins, row_at, False)
        sums = after(sums, *moved)
        hidden, blocks = finish(meta, sums, squares, [far], w_outs, col_at, width, len(rows))
        out_a += blocks
        hiddens.append(hidden)
        moved.append(swap(hidden, "ctx", n_ctx, top))
    back_a = send(out_a, True, False)
    out_b = []
    for hidden in moved:
        out_b += down(meta, hidden, w_outs, col_at, width, pair)
    back_b = send(out_b, True, True)
    done, column = combine(meta, att_a, back, weight_row, back_a, None)
    done = combine(meta, att_b, back, column, back_b, done)[0]
    return done[None]


def solution(mesh):
    in_specs = (
        P(("grp", "exp"), "ctx", None),
        P(("grp", "exp"), "ctx", None),
        P(("grp", "exp"), "ctx", None),
        P(("grp", "exp"), None),
        P(("grp", "exp"), "ctx", None),
        P(("grp", "exp"), "ctx", None),
        P(),
        P("exp", "ctx", None, None),
        P("exp", None, "ctx"),
    )
    out_specs = P(("grp", "exp"), "ctx", None)
    return jax.shard_map(body, mesh=mesh, in_specs=in_specs, out_specs=out_specs, check_vma=False)
```

```python
import functools
import math

import jax
import jax.numpy as jnp
from jax import lax
from jax.experimental import pallas as pl
from jax.experimental.pallas import tpu as pltpu
from jax.sharding import PartitionSpec as P

KV_HEADS = 2
HEAD_DIM = 128
TREE_BLOCK = 128
NEG = -1e30
MIB = 1024 * 1024
VMEM = pl.BlockSpec(memory_space=pltpu.VMEM)
SMEM = pl.BlockSpec(memory_space=pltpu.SMEM)


def call(kernel, name, args, specs, outs, scratch=(), mib=16, flops=1000, out_space=pltpu.VMEM):
    return pl.pallas_call(
        kernel,
        in_specs=specs,
        out_specs=[pl.BlockSpec(memory_space=out_space)] * len(outs),
        out_shape=[jax.ShapeDtypeStruct(s, d) for s, d in outs],
        scratch_shapes=list(scratch),
        compiler_params=pltpu.CompilerParams(vmem_limit_bytes=mib * MIB),
        cost_estimate=pl.CostEstimate(flops=flops, bytes_accessed=1000, transcendentals=0),
        name=name,
    )(*args)


def shifts(experts):
    return [experts // 2, 0] + [s for s in range(1, experts) if 2 * s != experts]


def placement_of(route_row, capacity, experts, first, relative):
    tokens = route_row.shape[1]
    if relative:
        shift = lax.rem(route_row - first + experts, experts)
        for i, s in enumerate(shifts(experts)):
            route_row = jnp.where(shift == s, i, route_row)
    rows = max(8, experts)
    expert_ids = lax.broadcasted_iota(jnp.int32, (rows, tokens), 0)
    hot = jnp.where(expert_ids == route_row, 1.0, 0.0)
    before = lax.broadcasted_iota(jnp.int32, (tokens, tokens), 0) < lax.broadcasted_iota(
        jnp.int32, (tokens, tokens), 1
    )
    earlier = jnp.dot(
        hot.astype(jnp.bfloat16),
        jnp.where(before, 1.0, 0.0).astype(jnp.bfloat16),
        preferred_element_type=jnp.float32,
    )
    rank = jnp.sum(earlier * hot, axis=0, keepdims=True).astype(jnp.int32)
    slot = route_row * capacity + rank
    slot_ids = lax.broadcasted_iota(jnp.int32, (experts * capacity, tokens), 0)
    return jnp.where(slot_ids == slot, 1.0, 0.0)


def plan_kernel(experts, capacity, relative, meta, route_ref, *refs):
    place_ref, back_ref = refs
    place = placement_of(route_ref[...], capacity, experts, meta[2], relative)
    place_ref[...] = place.astype(jnp.bfloat16)
    back_ref[...] = place.T.astype(jnp.bfloat16)


def plan(meta, route_row, experts, capacity, relative):
    tokens = route_row.shape[1]
    slots = experts * capacity
    bf16 = jnp.bfloat16
    return call(
        functools.partial(plan_kernel, experts, capacity, relative),
        "plan",
        [meta, route_row],
        [SMEM, VMEM],
        [((slots, tokens), bf16), ((tokens, slots), bf16)],
        flops=3 * 10**9,
    )


def attention_kernel(n_ctx, half, parent_at, meta, q_ref, place_ref, *refs):
    kv = refs[:n_ctx]
    att_ref = refs[n_ctx]
    out_refs = refs[n_ctx + 1 :]
    tokens, half_width = att_ref.shape
    heads = half_width // HEAD_DIM
    side = meta[0] if half == 0 else 1 - meta[0]
    me = meta[1]
    reached = [jnp.int32(0)] * n_ctx
    current = me
    for _ in range(n_ctx):
        current = meta[parent_at + current]
        for j in range(1, n_ctx):
            reached[j] = jnp.where(current == (me ^ j), jnp.int32(1), reached[j])
    causal = lax.broadcasted_iota(jnp.int32, (tokens, tokens), 1) <= lax.broadcasted_iota(
        jnp.int32, (tokens, tokens), 0
    )
    key_at = pl.ds(pl.multiple_of(side * HEAD_DIM, HEAD_DIM), HEAD_DIM)
    value_at = pl.ds(pl.multiple_of((KV_HEADS + side) * HEAD_DIM, HEAD_DIM), HEAD_DIM)
    keys_t = jnp.concatenate([r[:, key_at] for r in kv], axis=0).T
    ones = jnp.ones((tokens, HEAD_DIM), jnp.bfloat16)
    values = jnp.concatenate(
        [jnp.concatenate([r[:, value_at], ones], axis=1) for r in kv], axis=0
    )
    bias = jnp.concatenate(
        [jnp.where(causal, 0.0, NEG)]
        + [
            jnp.broadcast_to(jnp.where(reached[j] == 1, 0.0, NEG), (tokens, tokens))
            for j in range(1, n_ctx)
        ],
        axis=1,
    )
    scale = math.log2(math.e) / math.sqrt(HEAD_DIM)
    for h in range(heads):
        columns = slice(h * HEAD_DIM, (h + 1) * HEAD_DIM)
        q_at = pl.ds(pl.multiple_of(side * half_width + h * HEAD_DIM, HEAD_DIM), HEAD_DIM)
        scores = jnp.dot(q_ref[:, q_at], keys_t, preferred_element_type=jnp.float32)
        scores = scores * scale + bias
        peak = jnp.max(scores, axis=1, keepdims=True)
        weights = jnp.exp2(scores - peak).astype(jnp.bfloat16)
        total = jnp.dot(weights, values, preferred_element_type=jnp.float32)
        att_ref[:, columns] = (total[:, :HEAD_DIM] / total[:, HEAD_DIM:]).astype(jnp.bfloat16)
    packed = jnp.dot(place_ref[...], att_ref[...], preferred_element_type=jnp.float32)
    for k, out in enumerate(out_refs):
        rows = out.shape[0]
        out[...] = packed[k * rows : (k + 1) * rows].astype(jnp.bfloat16)


def attention(meta, parent_at, queries, place, kvs, blocks_out, half):
    tokens, width = queries.shape
    half_width = width // KV_HEADS
    rows = place.shape[0] // blocks_out
    bf16 = jnp.bfloat16
    outs = call(
        functools.partial(attention_kernel, len(kvs), half, parent_at),
        "attend_" + "ab"[half],
        [meta, queries, place, *kvs],
        [SMEM] + [VMEM] * (2 + len(kvs)),
        [((tokens, half_width), bf16)] + [((rows, half_width), bf16)] * blocks_out,
        flops=2 * 10**9,
    )
    return outs[0], list(outs[1:])


def products_kernel(n_rows, n_weights, row_at, packed, meta, gain_ref, *refs):
    row_refs, w_refs, refs = refs[:n_rows], refs[n_rows : n_rows + n_weights], refs[n_rows + n_weights :]
    scaled = refs[-1]
    width = scaled.shape[1]
    gain = gain_ref[:, pl.ds(pl.multiple_of(meta[0] * width, width), width)]
    rows = jnp.concatenate([r[...].astype(jnp.float32) for r in row_refs], axis=0)
    scaled[...] = (rows * gain).astype(jnp.bfloat16)
    squares = jnp.sum(rows * rows, axis=1, keepdims=True)
    squares = jnp.broadcast_to(squares, (scaled.shape[0], 128))
    sums = None
    for i, w_ref in enumerate(w_refs):
        features = pl.ds(pl.multiple_of(meta[row_at + i], 128), w_ref.shape[0])
        part = jnp.dot(scaled[:, features], w_ref[...], preferred_element_type=jnp.float32)
        sums = part if sums is None else sums + part
    if packed:
        columns = sums.shape[1]
        refs[0][:, :columns] = sums.astype(jnp.bfloat16)
        high = squares.astype(jnp.bfloat16)
        low = (squares - high.astype(jnp.float32)).astype(jnp.bfloat16)
        lane = lax.broadcasted_iota(jnp.int32, squares.shape, 1)
        refs[0][:, columns:] = jnp.where(
            lane < 64, high.astype(jnp.float32), low.astype(jnp.float32)
        ).astype(jnp.bfloat16)
    else:
        refs[0][...] = sums
        refs[1][...] = squares


def products(meta, gain, rows, weights, row_at, packed):
    slots = sum(r.shape[0] for r in rows)
    half_width = rows[0].shape[1]
    columns = weights[0].shape[1]
    f32, bf16 = jnp.float32, jnp.bfloat16
    outs = [((slots, columns + 128), bf16)] if packed else [((slots, columns), f32), ((slots, 128), f32)]
    return call(
        functools.partial(products_kernel, len(rows), len(weights), row_at, packed),
        "products_" + "ab"[packed],
        [meta, gain, *rows, *weights],
        [SMEM] + [VMEM] * (1 + len(rows) + len(weights)),
        outs,
        [pltpu.VMEM((slots, half_width), bf16)],
        flops=20 * 10**9 if packed else 1000,
    )


def store_down(meta, col_at, w_refs, hidden, out_refs):
    for i, w_ref in enumerate(w_refs):
        value = jnp.dot(hidden, w_ref[...], preferred_element_type=jnp.float32)
        where = pl.ds(pl.multiple_of(meta[col_at + i], 128), w_ref.shape[1])
        height = value.shape[0] // len(out_refs)
        for k, out in enumerate(out_refs):
            out[:, where] = value[k * height : (k + 1) * height].astype(jnp.bfloat16)


def finish_kernel(n_far, n_weights, col_at, width, meta, sums_ref, squares_ref, *refs):
    far_refs, refs = refs[:n_far], refs[n_far:]
    w_refs, hidden_ref, out_refs = refs[:n_weights], refs[n_weights], refs[n_weights + 1 :]
    inner = hidden_ref.shape[1]
    start = 0
    for far_ref in far_refs:
        rows = slice(start, start + far_ref.shape[0])
        start = rows.stop
        squares = squares_ref[rows, :1]
        for at in (0, 64):
            squares = squares + far_ref[:, 2 * inner + at : 2 * inner + at + 1].astype(jnp.float32)
        factor = lax.rsqrt(squares * (1.0 / width) + 1e-06)
        gate = (sums_ref[rows, :inner] + far_ref[:, :inner].astype(jnp.float32)) * factor
        up = (sums_ref[rows, inner:] + far_ref[:, inner : 2 * inner].astype(jnp.float32)) * factor
        hidden_ref[rows] = (gate / (1.0 + jnp.exp(-gate)) * up).astype(jnp.bfloat16)
    store_down(meta, col_at, w_refs, hidden_ref[...], out_refs)


def finish(meta, sums, squares, far, weights, col_at, width, blocks_out):
    slots, columns = sums.shape
    bf16 = jnp.bfloat16
    outs = call(
        functools.partial(finish_kernel, len(far), len(weights), col_at, width),
        "hidden_down_a",
        [meta, sums, squares, *far, *weights],
        [SMEM] + [VMEM] * (2 + len(far) + len(weights)),
        [((slots, columns // 2), bf16)]
        + [((slots // blocks_out, width // KV_HEADS), bf16)] * blocks_out,
    )
    return outs[0], list(outs[1:])


def down_kernel(n_weights, col_at, meta, hidden_ref, *refs):
    store_down(meta, col_at, refs[:n_weights], hidden_ref[...], refs[n_weights:])


def down(meta, hidden, weights, col_at, width, blocks_out):
    outs = [((hidden.shape[0] // blocks_out, width // KV_HEADS), jnp.bfloat16)] * blocks_out
    return list(
        call(
            functools.partial(down_kernel, len(weights), col_at),
            "down_b",
            [meta, hidden, *weights],
            [SMEM] + [VMEM] * (1 + len(weights)),
            outs,
        )
    )


def combine_kernel(last, meta, att_ref, back_ref, weight_ref, *refs):
    row_refs, refs = refs[: -2 - 2 * last], refs[-2 - 2 * last :]
    tokens, half_width = att_ref.shape
    if last:
        before_ref, out_ref, value_ref, sems = refs
        before_at = pl.multiple_of(meta[0] * half_width, half_width)
        mine_at = pl.multiple_of((1 - meta[0]) * half_width, half_width)
        copies = [
            pltpu.make_async_copy(before_ref, out_ref.at[:, pl.ds(before_at, half_width)], sems.at[0])
        ]
        copies[0].start()
        weight = weight_ref[:, :1]
    else:
        diagonal = lax.broadcasted_iota(jnp.int32, (tokens, tokens), 0) == lax.broadcasted_iota(
            jnp.int32, (tokens, tokens), 1
        )
        weight = jnp.sum(jnp.where(diagonal, weight_ref[...], 0.0), axis=1, keepdims=True)
        refs[1][...] = jnp.broadcast_to(weight, refs[1].shape)
    rows = jnp.concatenate([r[...].astype(jnp.float32) for r in row_refs], axis=0)
    rows = rows.astype(jnp.bfloat16)
    parts = 4 if last else 1
    step = half_width // parts
    for i in range(parts):
        columns = slice(i * step, (i + 1) * step)
        mine = jnp.dot(back_ref[...], rows[:, columns], preferred_element_type=jnp.float32)
        value = att_ref[:, columns].astype(jnp.float32) + mine * weight
        value = value.astype(jnp.bfloat16)
        if last:
            value_ref[:, columns] = value
            place = out_ref.at[:, pl.ds(pl.multiple_of(mine_at + i * step, 128), step)]
            copies.append(
                pltpu.make_async_copy(value_ref.at[:, pl.ds(i * step, step)], place, sems.at[i + 1])
            )
            copies[-1].start()
        else:
            refs[0][:, columns] = value
    if last:
        for copy in copies:
            copy.wait()


def combine(meta, att, back, weight, rows, before):
    tokens, half_width = att.shape
    last = before is not None
    extra = [before] if last else []
    if last:
        outs = [((tokens, KV_HEADS * half_width), jnp.bfloat16)]
    else:
        outs = [((tokens, half_width), jnp.bfloat16), ((tokens, 128), jnp.float32)]
    scratch = [pltpu.VMEM(att.shape, att.dtype), pltpu.SemaphoreType.DMA((5,))] if last else []
    return call(
        functools.partial(combine_kernel, last),
        "combine_" + "ab"[last],
        [meta, att, back, weight, *rows, *extra],
        [SMEM] + [VMEM] * (3 + len(rows) + len(extra)),
        outs,
        scratch,
        flops=20 * 10**9,
        out_space=pl.ANY if last else pltpu.VMEM,
    )


def swap(array, axis, size, bit):
    return lax.ppermute(array, axis, [(i, i ^ bit) for i in range(size)])


def after(array, *others):
    return lax.optimization_barrier((array, *others))[0]


def body(
    queries, keys, values, tree_parents, routes, route_weight, norm_gain, expert_in, expert_out
):
    n_ctx, n_exp = lax.axis_size("ctx"), lax.axis_size("exp")
    ctx, exp = lax.axis_index("ctx"), lax.axis_index("exp")
    tokens, width = queries.shape[1:]
    assert tokens == TREE_BLOCK and tree_parents.shape[1] == n_ctx and routes.shape[2] == 1
    assert n_ctx & (n_ctx - 1) == 0 and n_ctx > 1
    capacity = max(2, 5 * tokens // (4 * n_exp))
    slots = n_exp * capacity
    shifted = n_exp <= 8 and capacity % 8 == 0
    blocks_out = n_exp if shifted else 1
    half_width = width // KV_HEADS
    top = n_ctx // 2
    low_bits = [1 << b for b in range(top.bit_length() - 1)]
    half = ctx // top

    depth = expert_in.shape[1]
    inner = expert_out.shape[1]
    columns = expert_out.shape[2]
    route_row = routes.reshape(1, tokens)
    weight_row = route_weight.reshape(1, tokens)
    gain = norm_gain.reshape(1, width)

    shards = [lax.rem(ctx, top) ^ j for j in range(top)]
    row_at, col_at = 3, 3 + top
    parent_at = 3 + 2 * top
    meta = jnp.stack([half, ctx, exp] + [j * depth for j in shards] + [j * columns for j in shards])
    meta = jnp.concatenate([meta, tree_parents[0]])
    place, back = plan(meta, route_row, n_exp, capacity, shifted)

    kv = jnp.concatenate([keys[0], values[0]], axis=1)
    near, far = [kv], [after(swap(kv, "ctx", n_ctx, top), place)]
    for bit in low_bits:
        near = near + [swap(x, "ctx", n_ctx, bit) for x in near]
        far = far + [swap(x, "ctx", n_ctx, bit) for x in far]
    kvs = near + far

    def spread(array):
        found = [array]
        for bit in low_bits:
            found = found + [swap(a, "ctx", n_ctx, bit) for a in found]
        return found

    def send(blocks, back, cross, gates={}):
        if not shifted:
            whole = blocks[0].reshape(n_exp, capacity, half_width)
            whole = lax.all_to_all(whole, "exp", 0, 0, tiled=True).reshape(slots, half_width)
            return [swap(whole, "ctx", n_ctx, top) if cross else whole]
        moved = []
        for block, distance in zip(blocks, shifts(n_exp)):
            shift = (n_exp - distance) % n_exp if back else distance
            bit = top if cross else 0
            pairs = [
                (c * n_exp + e, (c ^ bit) * n_exp + (e + shift) % n_exp)
                for c in range(n_ctx)
                for e in range(n_exp)
            ]
            still = distance == 0 and not cross
            if len(moved) in gates:
                block = after(block, *gates[len(moved)](moved))
            moved.append(block if still else lax.ppermute(block, ("ctx", "exp"), pairs))
        return moved

    def attend(queries, part):
        return attention(meta, parent_at, queries, place, kvs, blocks_out, part)

    w_raw = spread(after(expert_in[0], *kvs[1:]))
    att_b, packed_b = attend(queries[0], 1)
    rows_b = send(packed_b, False, True)
    w_ins = [after(w, att_b).reshape(depth, 2 * inner) for w in w_raw]
    w_outs = spread(after(expert_out[0], rows_b[0]))
    att_a, packed_a = attend(after(queries[0], att_b, rows_b[0], *w_ins), 0)
    rows_b = [after(r, att_a) for r in rows_b]
    rows_b[-1] = after(rows_b[-1], w_outs[-1])
    pair = len(rows_b) // 2 if len(rows_b) % 4 == 0 else len(rows_b)
    groups = [rows_b[i : i + pair] for i in range(0, len(rows_b), pair)]
    far_sums = [products(meta, gain, g, w_ins, row_at, True)[0] for g in groups]
    gates = {2: lambda m: [far_sums[0]], 3: lambda m: [m[0]]} if shifted else {}
    rows_a = send(packed_a, False, False, gates)
    made = far_sums[-1]
    far_sums = [swap(f, "ctx", n_ctx, top) for f in far_sums]
    out_a, hiddens, moved = [], [], []
    for i, far in enumerate(far_sums):
        rows = [after(r, made, *hiddens) for r in rows_a[i * pair : (i + 1) * pair]]
        sums, squares = products(meta, gain, rows, w_ins, row_at, False)
        hold = moved
        hidden, blocks = finish(meta, sums, squares, [far], w_outs, col_at, width, len(rows))
        out_a += [after(b, *hold) for b in blocks] if hold else blocks
        hiddens.append(hidden)
        moved.append(swap(hidden, "ctx", n_ctx, top))
    back_a = send(out_a, True, False)
    out_b = []
    for hidden in moved:
        out_b += down(meta, hidden, w_outs, col_at, width, pair)
    back_b = send(out_b, True, True)
    done, column = combine(meta, att_a, back, weight_row, back_a, None)
    done = combine(meta, att_b, back, column, back_b, done)[0]
    return done[None]


def solution(mesh):
    in_specs = (
        P(("grp", "exp"), "ctx", None),
        P(("grp", "exp"), "ctx", None),
        P(("grp", "exp"), "ctx", None),
        P(("grp", "exp"), None),
        P(("grp", "exp"), "ctx", None),
        P(("grp", "exp"), "ctx", None),
        P(),
        P("exp", "ctx", None, None),
        P("exp", None, "ctx"),
    )
    out_specs = P(("grp", "exp"), "ctx", None)
    return jax.shard_map(body, mesh=mesh, in_specs=in_specs, out_specs=out_specs, check_vma=False)
```

```python
import functools
import math

import jax
import jax.numpy as jnp
from jax import lax
from jax.experimental import pallas as pl
from jax.experimental.pallas import tpu as pltpu
from jax.sharding import PartitionSpec as P

KV_HEADS = 2
HEAD_DIM = 128
TREE_BLOCK = 128
NEG = -1e30
MIB = 1024 * 1024
VMEM = pl.BlockSpec(memory_space=pltpu.VMEM)
SMEM = pl.BlockSpec(memory_space=pltpu.SMEM)


def call(kernel, name, args, specs, outs, scratch=(), mib=16, flops=1000, out_space=pltpu.VMEM):
    return pl.pallas_call(
        kernel,
        in_specs=specs,
        out_specs=[pl.BlockSpec(memory_space=out_space)] * len(outs),
        out_shape=[jax.ShapeDtypeStruct(s, d) for s, d in outs],
        scratch_shapes=list(scratch),
        compiler_params=pltpu.CompilerParams(vmem_limit_bytes=mib * MIB),
        cost_estimate=pl.CostEstimate(flops=flops, bytes_accessed=1000, transcendentals=0),
        name=name,
    )(*args)


def shifts(experts):
    return [experts // 2, 0] + [s for s in range(1, experts) if 2 * s != experts]


def placement_of(route_row, capacity, experts, first, relative):
    tokens = route_row.shape[1]
    if relative:
        shift = lax.rem(route_row - first + experts, experts)
        for i, s in enumerate(shifts(experts)):
            route_row = jnp.where(shift == s, i, route_row)
    rows = max(8, experts)
    expert_ids = lax.broadcasted_iota(jnp.int32, (rows, tokens), 0)
    hot = jnp.where(expert_ids == route_row, 1.0, 0.0)
    before = lax.broadcasted_iota(jnp.int32, (tokens, tokens), 0) < lax.broadcasted_iota(
        jnp.int32, (tokens, tokens), 1
    )
    earlier = jnp.dot(
        hot.astype(jnp.bfloat16),
        jnp.where(before, 1.0, 0.0).astype(jnp.bfloat16),
        preferred_element_type=jnp.float32,
    )
    rank = jnp.sum(earlier * hot, axis=0, keepdims=True).astype(jnp.int32)
    slot = route_row * capacity + rank
    slot_ids = lax.broadcasted_iota(jnp.int32, (experts * capacity, tokens), 0)
    return jnp.where(slot_ids == slot, 1.0, 0.0)


def plan_kernel(experts, capacity, relative, meta, route_ref, *refs):
    place_ref, back_ref = refs
    place = placement_of(route_ref[...], capacity, experts, meta[2], relative)
    place_ref[...] = place.astype(jnp.bfloat16)
    back_ref[...] = place.T.astype(jnp.bfloat16)


def plan(meta, route_row, experts, capacity, relative):
    tokens = route_row.shape[1]
    slots = experts * capacity
    bf16 = jnp.bfloat16
    return call(
        functools.partial(plan_kernel, experts, capacity, relative),
        "plan",
        [meta, route_row],
        [SMEM, VMEM],
        [((slots, tokens), bf16), ((tokens, slots), bf16)],
        flops=3 * 10**9,
    )


def attention_kernel(n_ctx, half, parent_at, meta, q_ref, place_ref, *refs):
    kv = refs[:n_ctx]
    att_ref = refs[n_ctx]
    out_refs = refs[n_ctx + 1 :]
    tokens, half_width = att_ref.shape
    heads = half_width // HEAD_DIM
    side = meta[0] if half == 0 else 1 - meta[0]
    me = meta[1]
    reached = [jnp.int32(0)] * n_ctx
    current = me
    for _ in range(n_ctx):
        current = meta[parent_at + current]
        for j in range(1, n_ctx):
            reached[j] = jnp.where(current == (me ^ j), jnp.int32(1), reached[j])
    causal = lax.broadcasted_iota(jnp.int32, (tokens, tokens), 1) <= lax.broadcasted_iota(
        jnp.int32, (tokens, tokens), 0
    )
    key_at = pl.ds(pl.multiple_of(side * HEAD_DIM, HEAD_DIM), HEAD_DIM)
    value_at = pl.ds(pl.multiple_of((KV_HEADS + side) * HEAD_DIM, HEAD_DIM), HEAD_DIM)
    keys_t = jnp.concatenate([r[:, key_at] for r in kv], axis=0).T
    ones = jnp.ones((tokens, HEAD_DIM), jnp.bfloat16)
    values = jnp.concatenate(
        [jnp.concatenate([r[:, value_at], ones], axis=1) for r in kv], axis=0
    )
    bias = jnp.concatenate(
        [jnp.where(causal, 0.0, NEG)]
        + [
            jnp.broadcast_to(jnp.where(reached[j] == 1, 0.0, NEG), (tokens, tokens))
            for j in range(1, n_ctx)
        ],
        axis=1,
    )
    scale = math.log2(math.e) / math.sqrt(HEAD_DIM)
    for h in range(heads):
        columns = slice(h * HEAD_DIM, (h + 1) * HEAD_DIM)
        q_at = pl.ds(pl.multiple_of(side * half_width + h * HEAD_DIM, HEAD_DIM), HEAD_DIM)
        scores = jnp.dot(q_ref[:, q_at], keys_t, preferred_element_type=jnp.float32)
        scores = scores * scale + bias
        peak = jnp.max(scores, axis=1, keepdims=True)
        weights = jnp.exp2(scores - peak).astype(jnp.bfloat16)
        total = jnp.dot(weights, values, preferred_element_type=jnp.float32)
        att_ref[:, columns] = (total[:, :HEAD_DIM] / total[:, HEAD_DIM:]).astype(jnp.bfloat16)
    packed = jnp.dot(place_ref[...], att_ref[...], preferred_element_type=jnp.float32)
    for k, out in enumerate(out_refs):
        rows = out.shape[0]
        out[...] = packed[k * rows : (k + 1) * rows].astype(jnp.bfloat16)


def attention(meta, parent_at, queries, place, kvs, blocks_out, half):
    tokens, width = queries.shape
    half_width = width // KV_HEADS
    rows = place.shape[0] // blocks_out
    bf16 = jnp.bfloat16
    outs = call(
        functools.partial(attention_kernel, len(kvs), half, parent_at),
        "attend_" + "ab"[half],
        [meta, queries, place, *kvs],
        [SMEM] + [VMEM] * (2 + len(kvs)),
        [((tokens, half_width), bf16)] + [((rows, half_width), bf16)] * blocks_out,
        flops=2 * 10**9,
    )
    return outs[0], list(outs[1:])


def products_kernel(n_rows, n_weights, row_at, packed, meta, gain_ref, *refs):
    row_refs, w_refs, refs = refs[:n_rows], refs[n_rows : n_rows + n_weights], refs[n_rows + n_weights :]
    scaled = refs[-1]
    width = scaled.shape[1]
    gain = gain_ref[:, pl.ds(pl.multiple_of(meta[0] * width, width), width)]
    rows = jnp.concatenate([r[...].astype(jnp.float32) for r in row_refs], axis=0)
    scaled[...] = (rows * gain).astype(jnp.bfloat16)
    squares = jnp.sum(rows * rows, axis=1, keepdims=True)
    squares = jnp.broadcast_to(squares, (scaled.shape[0], 128))
    sums = None
    for i, w_ref in enumerate(w_refs):
        features = pl.ds(pl.multiple_of(meta[row_at + i], 128), w_ref.shape[0])
        part = jnp.dot(scaled[:, features], w_ref[...], preferred_element_type=jnp.float32)
        sums = part if sums is None else sums + part
    if packed:
        columns = sums.shape[1]
        refs[0][:, :columns] = sums.astype(jnp.bfloat16)
        high = squares.astype(jnp.bfloat16)
        low = (squares - high.astype(jnp.float32)).astype(jnp.bfloat16)
        lane = lax.broadcasted_iota(jnp.int32, squares.shape, 1)
        refs[0][:, columns:] = jnp.where(
            lane < 64, high.astype(jnp.float32), low.astype(jnp.float32)
        ).astype(jnp.bfloat16)
    else:
        refs[0][...] = sums
        refs[1][...] = squares


def products(meta, gain, rows, weights, row_at, packed):
    slots = sum(r.shape[0] for r in rows)
    half_width = rows[0].shape[1]
    columns = weights[0].shape[1]
    f32, bf16 = jnp.float32, jnp.bfloat16
    outs = [((slots, columns + 128), bf16)] if packed else [((slots, columns), f32), ((slots, 128), f32)]
    return call(
        functools.partial(products_kernel, len(rows), len(weights), row_at, packed),
        "products_" + "ab"[packed],
        [meta, gain, *rows, *weights],
        [SMEM] + [VMEM] * (1 + len(rows) + len(weights)),
        outs,
        [pltpu.VMEM((slots, half_width), bf16)],
        flops=20 * 10**9 if packed else 1000,
    )


def store_down(meta, col_at, w_refs, hidden, out_refs):
    for i, w_ref in enumerate(w_refs):
        value = jnp.dot(hidden, w_ref[...], preferred_element_type=jnp.float32)
        where = pl.ds(pl.multiple_of(meta[col_at + i], 128), w_ref.shape[1])
        height = value.shape[0] // len(out_refs)
        for k, out in enumerate(out_refs):
            out[:, where] = value[k * height : (k + 1) * height].astype(jnp.bfloat16)


def finish_kernel(n_far, n_weights, col_at, width, meta, sums_ref, squares_ref, *refs):
    far_refs, refs = refs[:n_far], refs[n_far:]
    w_refs, hidden_ref, out_refs = refs[:n_weights], refs[n_weights], refs[n_weights + 1 :]
    inner = hidden_ref.shape[1]
    start = 0
    for far_ref in far_refs:
        rows = slice(start, start + far_ref.shape[0])
        start = rows.stop
        squares = squares_ref[rows, :1]
        for at in (0, 64):
            squares = squares + far_ref[:, 2 * inner + at : 2 * inner + at + 1].astype(jnp.float32)
        factor = lax.rsqrt(squares * (1.0 / width) + 1e-06)
        gate = (sums_ref[rows, :inner] + far_ref[:, :inner].astype(jnp.float32)) * factor
        up = (sums_ref[rows, inner:] + far_ref[:, inner : 2 * inner].astype(jnp.float32)) * factor
        hidden_ref[rows] = (gate / (1.0 + jnp.exp(-gate)) * up).astype(jnp.bfloat16)
    store_down(meta, col_at, w_refs, hidden_ref[...], out_refs)


def finish(meta, sums, squares, far, weights, col_at, width, blocks_out):
    slots, columns = sums.shape
    bf16 = jnp.bfloat16
    outs = call(
        functools.partial(finish_kernel, len(far), len(weights), col_at, width),
        "hidden_down_a",
        [meta, sums, squares, *far, *weights],
        [SMEM] + [VMEM] * (2 + len(far) + len(weights)),
        [((slots, columns // 2), bf16)]
        + [((slots // blocks_out, width // KV_HEADS), bf16)] * blocks_out,
    )
    return outs[0], list(outs[1:])


def down_kernel(n_weights, col_at, meta, hidden_ref, *refs):
    store_down(meta, col_at, refs[:n_weights], hidden_ref[...], refs[n_weights:])


def down(meta, hidden, weights, col_at, width, blocks_out):
    outs = [((hidden.shape[0] // blocks_out, width // KV_HEADS), jnp.bfloat16)] * blocks_out
    return list(
        call(
            functools.partial(down_kernel, len(weights), col_at),
            "down_b",
            [meta, hidden, *weights],
            [SMEM] + [VMEM] * (1 + len(weights)),
            outs,
        )
    )


def combine_kernel(last, meta, att_ref, back_ref, weight_ref, *refs):
    row_refs, refs = refs[: -2 - 2 * last], refs[-2 - 2 * last :]
    tokens, half_width = att_ref.shape
    if last:
        before_ref, out_ref, value_ref, sems = refs
        before_at = pl.multiple_of(meta[0] * half_width, half_width)
        mine_at = pl.multiple_of((1 - meta[0]) * half_width, half_width)
        copies = [
            pltpu.make_async_copy(before_ref, out_ref.at[:, pl.ds(before_at, half_width)], sems.at[0])
        ]
        copies[0].start()
        weight = weight_ref[:, :1]
    else:
        diagonal = lax.broadcasted_iota(jnp.int32, (tokens, tokens), 0) == lax.broadcasted_iota(
            jnp.int32, (tokens, tokens), 1
        )
        weight = jnp.sum(jnp.where(diagonal, weight_ref[...], 0.0), axis=1, keepdims=True)
        refs[1][...] = jnp.broadcast_to(weight, refs[1].shape)
    parts = 4 if last else 1
    step = half_width // parts
    for i in range(parts):
        columns = slice(i * step, (i + 1) * step)
        rows = jnp.concatenate([r[:, columns].astype(jnp.float32) for r in row_refs], axis=0)
        rows = rows.astype(jnp.bfloat16)
        mine = jnp.dot(back_ref[...], rows, preferred_element_type=jnp.float32)
        value = att_ref[:, columns].astype(jnp.float32) + mine * weight
        value = value.astype(jnp.bfloat16)
        if last:
            value_ref[:, columns] = value
            place = out_ref.at[:, pl.ds(pl.multiple_of(mine_at + i * step, 128), step)]
            copies.append(
                pltpu.make_async_copy(value_ref.at[:, pl.ds(i * step, step)], place, sems.at[i + 1])
            )
            copies[-1].start()
        else:
            refs[0][:, columns] = value
    if last:
        for copy in copies:
            copy.wait()


def combine(meta, att, back, weight, rows, before):
    tokens, half_width = att.shape
    last = before is not None
    extra = [before] if last else []
    if last:
        outs = [((tokens, KV_HEADS * half_width), jnp.bfloat16)]
    else:
        outs = [((tokens, half_width), jnp.bfloat16), ((tokens, 128), jnp.float32)]
    scratch = [pltpu.VMEM(att.shape, att.dtype), pltpu.SemaphoreType.DMA((5,))] if last else []
    return call(
        functools.partial(combine_kernel, last),
        "combine_" + "ab"[last],
        [meta, att, back, weight, *rows, *extra],
        [SMEM] + [VMEM] * (3 + len(rows) + len(extra)),
        outs,
        scratch,
        flops=20 * 10**9,
        out_space=pl.ANY if last else pltpu.VMEM,
    )


def swap(array, axis, size, bit):
    return lax.ppermute(array, axis, [(i, i ^ bit) for i in range(size)])


def after(array, *others):
    return lax.optimization_barrier((array, *others))[0]


def body(
    queries, keys, values, tree_parents, routes, route_weight, norm_gain, expert_in, expert_out
):
    n_ctx, n_exp = lax.axis_size("ctx"), lax.axis_size("exp")
    ctx, exp = lax.axis_index("ctx"), lax.axis_index("exp")
    tokens, width = queries.shape[1:]
    assert tokens == TREE_BLOCK and tree_parents.shape[1] == n_ctx and routes.shape[2] == 1
    assert n_ctx & (n_ctx - 1) == 0 and n_ctx > 1
    capacity = max(2, 5 * tokens // (4 * n_exp))
    slots = n_exp * capacity
    shifted = n_exp <= 8 and capacity % 8 == 0
    blocks_out = n_exp if shifted else 1
    half_width = width // KV_HEADS
    top = n_ctx // 2
    low_bits = [1 << b for b in range(top.bit_length() - 1)]
    half = ctx // top

    depth = expert_in.shape[1]
    inner = expert_out.shape[1]
    columns = expert_out.shape[2]
    route_row = routes.reshape(1, tokens)
    weight_row = route_weight.reshape(1, tokens)
    gain = norm_gain.reshape(1, width)

    shards = [lax.rem(ctx, top) ^ j for j in range(top)]
    row_at, col_at = 3, 3 + top
    parent_at = 3 + 2 * top
    meta = jnp.stack([half, ctx, exp] + [j * depth for j in shards] + [j * columns for j in shards])
    meta = jnp.concatenate([meta, tree_parents[0]])
    place, back = plan(meta, route_row, n_exp, capacity, shifted)

    kv = jnp.concatenate([keys[0], values[0]], axis=1)
    near, far = [kv], [after(swap(kv, "ctx", n_ctx, top), place)]
    for bit in low_bits:
        near = near + [swap(x, "ctx", n_ctx, bit) for x in near]
        far = far + [swap(x, "ctx", n_ctx, bit) for x in far]
    kvs = near + far

    def spread(array):
        found = [array]
        for bit in low_bits:
            found = found + [swap(a, "ctx", n_ctx, bit) for a in found]
        return found

    def send(blocks, back, cross, gates={}):
        if not shifted:
            whole = blocks[0].reshape(n_exp, capacity, half_width)
            whole = lax.all_to_all(whole, "exp", 0, 0, tiled=True).reshape(slots, half_width)
            return [swap(whole, "ctx", n_ctx, top) if cross else whole]
        moved = []
        for block, distance in zip(blocks, shifts(n_exp)):
            shift = (n_exp - distance) % n_exp if back else distance
            bit = top if cross else 0
            pairs = [
                (c * n_exp + e, (c ^ bit) * n_exp + (e + shift) % n_exp)
                for c in range(n_ctx)
                for e in range(n_exp)
            ]
            still = distance == 0 and not cross
            if len(moved) in gates:
                block = after(block, *gates[len(moved)](moved))
            moved.append(block if still else lax.ppermute(block, ("ctx", "exp"), pairs))
        return moved

    def attend(queries, part):
        return attention(meta, parent_at, queries, place, kvs, blocks_out, part)

    w_raw = spread(after(expert_in[0], *kvs[1:]))
    att_b, packed_b = attend(queries[0], 1)
    rows_b = send(packed_b, False, True)
    w_ins = [after(w, att_b).reshape(depth, 2 * inner) for w in w_raw]
    w_outs = spread(after(expert_out[0], rows_b[0]))
    att_a, packed_a = attend(after(queries[0], att_b, rows_b[0], *w_ins), 0)
    rows_b = [after(r, att_a) for r in rows_b]
    rows_b[-1] = after(rows_b[-1], w_outs[-1])
    pair = len(rows_b) // 2 if len(rows_b) % 4 == 0 else len(rows_b)
    groups = [rows_b[i : i + pair] for i in range(0, len(rows_b), pair)]
    far_sums = [products(meta, gain, g, w_ins, row_at, True)[0] for g in groups]
    gates = {2: lambda m: [far_sums[0]], 3: lambda m: [m[0]]} if shifted else {}
    rows_a = send(packed_a, False, False, gates)
    made = far_sums[-1]
    far_sums = [swap(f, "ctx", n_ctx, top) for f in far_sums]
    out_a, hiddens, moved = [], [], []
    for i, far in enumerate(far_sums):
        rows = [after(r, made, *hiddens) for r in rows_a[i * pair : (i + 1) * pair]]
        sums, squares = products(meta, gain, rows, w_ins, row_at, False)
        hold = moved
        hidden, blocks = finish(meta, sums, squares, [far], w_outs, col_at, width, len(rows))
        out_a += [after(b, *hold) for b in blocks] if hold else blocks
        hiddens.append(hidden)
        moved.append(swap(hidden, "ctx", n_ctx, top))
    back_a = send(out_a, True, False)
    out_b = []
    for hidden in moved:
        out_b += down(meta, hidden, w_outs, col_at, width, pair)
    back_b = send(out_b, True, True)
    done, column = combine(meta, att_a, back, weight_row, back_a, None)
    done = combine(meta, att_b, back, column, back_b, done)[0]
    return done[None]


def solution(mesh):
    in_specs = (
        P(("grp", "exp"), "ctx", None),
        P(("grp", "exp"), "ctx", None),
        P(("grp", "exp"), "ctx", None),
        P(("grp", "exp"), None),
        P(("grp", "exp"), "ctx", None),
        P(("grp", "exp"), "ctx", None),
        P(),
        P("exp", "ctx", None, None),
        P("exp", None, "ctx"),
    )
    out_specs = P(("grp", "exp"), "ctx", None)
    return jax.shard_map(body, mesh=mesh, in_specs=in_specs, out_specs=out_specs, check_vma=False)
```
